32 devices in a mesh: grp: 2 (over x), src: 8 (over z, y), tgt: 2 (over core).
Axes of the slice: x: 2, y: 2, z: 4, core: 2. Of those that a mesh axis runs over, the one named last changes fastest.
Arguments:
- source_mass: float32 [8192, 1024], P(('grp', 'src'), 'tgt'), parts along dimension 0, may hold values from 0.3 to 3
- target_mass: float32 [2, 1024, 1024], P('tgt', ('grp', 'src')), parts along dimension 1, may hold values from 0.3 to 3
- kernel_tiles: bfloat16 [32, 4, 256, 256], P(('grp', 'src'), 'tgt'), parts along dimension 0, may hold values from 0.00039863586 to 0.0039978027
- tile_cols: int32 [32, 4], P(('grp', 'src'), 'tgt'), parts along dimension 0, may hold values from 0 to 1, as said below
- tile_count: int32 [32, 2], P(('grp', 'src'), 'tgt'), parts along dimension 0, may hold values from 1 to 2, as said below
- source_cotangent: float32 [8192, 1024], P(('grp', 'src'), 'tgt'), parts along dimension 0, may hold values from -6 to 6
- target_cotangent: float32 [2, 1024, 1024], P('tgt', ('grp', 'src')), parts along dimension 1, may hold values from -6 to 6
Outputs:
- source_potential: float32 [8192, 1024], P(('grp', 'src'), 'tgt'), parts along dimension 0
- target_potential: float32 [2, 1024, 1024], P('tgt', ('grp', 'src')), parts along dimension 1
- source_grad: float32 [8192, 1024], P(('grp', 'src'), 'tgt'), parts along dimension 0
- target_grad: float32 [2, 1024, 1024], P('tgt', ('grp', 'src')), parts along dimension 1
The draws below stay inside these ranges and needn't reach their ends.
There are 2 independent parts, one for each index of `grp`. The reference program is written for one: setup_inputs(seed, part) draws one part's arguments, and reference() takes and returns one part's arrays. A program takes and returns all parts, laid end to end along the dimension named above; each array names one. Nothing has to cross between parts.
Inputs may be any that keep to these rules, and one draw needn't show every extreme that they name: `tile_cols`: the live slots of one row block in one set name distinct column blocks, and every column block of every set is named by a live slot of some row block. `tile_count`: every set has a row block with all 2 slots live.
All inputs are finite; a program needn't handle non-finite values.
Results may differ from the reference program's by a relative error of at most 0.0003.
Values may be sent and summed in bfloat16 or wider, within the bound.
No kernel may reach another device: no remote copies, remote signals or barrier semaphores. Data moves between devices by JAX's collectives and lax.ppermute only.
A program may use at most 64 MiB of HBM per device.

```python
import math
import jax
import jax.numpy as jnp
from jax import lax

H = 1024
TILE = 256
KEEP = 2
CB_DEV = 2
ROW_BLOCKS = 16
N = 4096
SETS = 2
SET_ROWS = 512
M = 1024


def draw_tile_cols(key, part):
    key = jax.random.fold_in(key, 23)
    first_key, second_key = jax.random.split(key)
    scores = jax.random.randint(first_key, (SETS, ROW_BLOCKS), 0, 1 << 20) * ROW_BLOCKS + jnp.arange(ROW_BLOCKS, dtype=jnp.int32)[None, :]
    order = jnp.argsort(scores, axis=1)
    ranks = jnp.argsort(order, axis=1).astype(jnp.int32)
    random_start = jax.random.randint(second_key, (SETS, ROW_BLOCKS), 0, CB_DEV)
    starts = jnp.where(ranks < CB_DEV, ranks, random_start)
    columns = (starts.T[:, :, None] + jnp.arange(KEEP, dtype=jnp.int32)[None, None, :]) % CB_DEV
    return columns.reshape(ROW_BLOCKS, SETS * KEEP).astype(jnp.int32)


def draw_tile_count(key, part):
    key = jax.random.fold_in(key, 11)
    first_key, second_key = jax.random.split(key)
    counts = jax.random.randint(first_key, (ROW_BLOCKS, SETS), 1, KEEP + 1)
    chosen = jax.random.randint(second_key, (1, SETS), 0, ROW_BLOCKS)
    positions = jnp.arange(ROW_BLOCKS, dtype=jnp.int32)[:, None]
    return jnp.where(positions == chosen, KEEP, counts).astype(jnp.int32)


def levels(stream_key, dims, cuts, smallest, top_value):
    def one(position, parts):
        steps = jax.random.uniform(jax.random.fold_in(jax.random.fold_in(stream_key, 6), position), (parts,), jnp.float32, smallest / len(cuts), top_value / len(cuts))
        return jnp.repeat(jnp.exp(steps), dims[position] // parts).reshape((-1,) + (1,) * (len(dims) - position - 1))

    gain = one(*cuts[0])
    for cut in cuts[1:]:
        gain = gain * one(*cut)
    return gain


def bell_draw(key, extent, width, limit, shards=(), kind=jnp.bfloat16):
    result = jax.random.normal(key, extent, jnp.float32) * width
    if len(shards) > 0:
        result = levels(key, extent, shards, -0.22, 0.18) * result
    return jnp.clip(result, min=-limit, max=limit).astype(kind)


def setup_inputs(seed: int = 0, part: int = 0) -> dict:
    key_list = jax.random.split(jax.random.key(seed), 8)
    part_splits = jax.random.split(jax.random.fold_in(key_list[7], part), 8)
    source_mass = jnp.clip(jnp.exp(math.log(3.0) - 2.3025851 * jax.random.uniform(part_splits[0], (N, H), jnp.float32) ** levels(part_splits[0], (N, H), ((0, 8), (1, 2)), -0.2, 0.2)), 0.3, 3.0)
    target_mass = jnp.clip(jnp.exp(math.log(3.0) - 2.3025851 * jax.random.uniform(part_splits[1], (SETS, SET_ROWS, H), jnp.float32) ** levels(part_splits[1], (SETS, SET_ROWS, H), ((0, 2), (1, 8)), -0.2, 0.2)), 0.3, 3.0)
    kernel_tiles = jnp.clip(jnp.exp(math.log(0.0039978027) - 2.3054518 * jax.random.uniform(part_splits[2], (ROW_BLOCKS, SETS * KEEP, TILE, TILE), jnp.float32) ** levels(part_splits[2], (ROW_BLOCKS, SETS * KEEP, TILE, TILE), ((0, 8), (1, 2)), -0.2, 0.2)), 0.00039863586, 0.0039978027).astype(jnp.bfloat16)
    tile_cols = draw_tile_cols(jax.random.fold_in(jax.random.fold_in(key_list[7], part), 71), part)
    tile_count = draw_tile_count(jax.random.fold_in(jax.random.fold_in(key_list[7], part), 71), part)
    source_cotangent = bell_draw(part_splits[5], (N, H), 1.0, 6.0, ((0, 8), (1, 2)), jnp.float32)
    target_cotangent = bell_draw(part_splits[6], (SETS, SET_ROWS, H), 1.0, 6.0, ((0, 2), (1, 8)), jnp.float32)
    return dict(source_mass=source_mass, target_mass=target_mass, kernel_tiles=kernel_tiles, tile_cols=tile_cols, tile_count=tile_count, source_cotangent=source_cotangent, target_cotangent=target_cotangent)


def dense_kernel(kernel_tiles, tile_cols, tile_count):
    block_count = kernel_tiles.shape[0]
    tiles = kernel_tiles.astype(jnp.float32).reshape(block_count, SETS, KEEP, TILE, TILE)
    columns = tile_cols.reshape(block_count, SETS, KEEP)
    live = jnp.arange(KEEP, dtype=jnp.int32)[None, None, :] < tile_count[:, :, None]
    hits = (columns[:, :, :, None] == jnp.arange(CB_DEV, dtype=jnp.int32)) & live[:, :, :, None]
    blocks = jnp.einsum("rskc,rskab->rascb", hits.astype(jnp.float32), tiles, precision=lax.Precision.HIGHEST)
    return blocks.reshape(block_count * TILE, SETS * CB_DEV * TILE)


def alternate(kernel_times, kernel_transposed, first, source_mass, target_mass, source_cotangent, target_cotangent):
    left_one = source_mass / first
    col_one = kernel_transposed(left_one.astype(jnp.bfloat16))
    right_one = target_mass / col_one
    row_two = kernel_times(right_one.astype(jnp.bfloat16))
    left_two = source_mass / row_two
    col_two = kernel_transposed(left_two.astype(jnp.bfloat16))
    right_two = target_mass / col_two
    row_three = kernel_times(right_two.astype(jnp.bfloat16))
    left_three = source_mass / row_three
    col_three = kernel_transposed(left_three.astype(jnp.bfloat16))
    right_three = target_mass / col_three
    colgrad_three = -target_cotangent / col_three
    leftgrad_three = source_cotangent / left_three + kernel_times(colgrad_three.astype(jnp.bfloat16))
    source_grad = leftgrad_three / row_three
    rowgrad_three = -leftgrad_three * left_three / row_three
    rightgrad_two = kernel_transposed(rowgrad_three.astype(jnp.bfloat16))
    target_grad = target_cotangent / target_mass + rightgrad_two / col_two
    colgrad_two = -rightgrad_two * right_two / col_two
    leftgrad_two = kernel_times(colgrad_two.astype(jnp.bfloat16))
    source_grad = source_grad + leftgrad_two / row_two
    rowgrad_two = -leftgrad_two * left_two / row_two
    rightgrad_one = kernel_transposed(rowgrad_two.astype(jnp.bfloat16))
    target_grad = target_grad + rightgrad_one / col_one
    colgrad_one = -rightgrad_one * right_one / col_one
    leftgrad_one = kernel_times(colgrad_one.astype(jnp.bfloat16))
    source_grad = source_grad + leftgrad_one / first
    return jnp.log(left_three), jnp.log(right_three), source_grad, target_grad


def as_operand(values):
    return lax.optimization_barrier(values).astype(jnp.float32)


def reference(source_mass, target_mass, kernel_tiles, tile_cols, tile_count, source_cotangent, target_cotangent):
    matrix = dense_kernel(kernel_tiles, tile_cols, tile_count)

    def kernel_times(panel):
        return jnp.dot(matrix, as_operand(panel), precision=lax.Precision.HIGHEST)

    def kernel_transposed(panel):
        return jnp.dot(matrix.T, as_operand(panel), precision=lax.Precision.HIGHEST)

    first = jnp.broadcast_to(jnp.sum(matrix, axis=1)[:, None], source_mass.shape)
    target_rows = target_mass.reshape(M, H)
    cot_rows = target_cotangent.reshape(M, H)
    source_potential, target_potential, source_grad, target_grad = alternate(
        kernel_times, kernel_transposed, first, source_mass, target_rows, source_cotangent, cot_rows)
    return (source_potential, target_potential.reshape(SETS, SET_ROWS, H), source_grad,
            target_grad.reshape(SETS, SET_ROWS, H))
```

```python
import functools

import jax
import jax.numpy as jnp
import numpy as np
from jax import lax
from jax.experimental import pallas as pl
from jax.experimental.pallas import tpu as pltpu
from jax.sharding import PartitionSpec as P

CB_DEV = 2
HALF = jnp.float16
COT_SCALE = 256.0
VMEM = 56 * 1024 * 1024


def ring_order(count):
    if count == 8:
        return [0, 2, 4, 6, 7, 5, 3, 1]
    return list(range(count))


def dense_blocks(kernel_tiles, tile_cols, tile_count):
    keep = kernel_tiles.shape[1]
    live = jnp.arange(keep, dtype=jnp.int32)[None, :] < tile_count
    hits = (tile_cols[:, :, None] == jnp.arange(CB_DEV, dtype=jnp.int32)) & live[:, :, None]
    blocks = jnp.einsum(
        "rkc,rkab->racb",
        hits.astype(jnp.bfloat16),
        kernel_tiles,
        preferred_element_type=jnp.float32,
    )
    rows, cols = blocks.shape[0] * blocks.shape[1], blocks.shape[2] * blocks.shape[3]
    return blocks.astype(jnp.bfloat16).reshape(rows, cols)


def nt(x, y):
    return lax.dot_general(x, y, (((1,), (1,)), ((), ())), preferred_element_type=jnp.float32)


def nn(x, y):
    return jnp.dot(x, y, preferred_element_type=jnp.float32)


class Shape:
    def __init__(self, count, rows, cols, hists, share):
        self.count = count
        self.rows = rows
        self.cols = cols
        self.hists = hists
        self.share = share
        self.lanes = rows + 2 * share


def load_matrix(s, units, matrix, sems):
    copies = []
    for d in range(s.count):
        for t in range(2):
            copy = pltpu.make_async_copy(
                units[2 * d + t], matrix.at[d, :, pl.ds(t * s.cols, s.cols)], sems.at[d]
            )
            copy.start()
            copies.append(copy)
    return copies


def gather_targets(s, pieces, index):
    parts = []
    for t in range(2):
        lo = s.rows + t * s.share
        parts += [pieces[index(i), :, lo : lo + s.share] for i in range(s.count)]
    return jnp.concatenate(parts, axis=1)


def scatter_targets(s, out, index, values):
    for i in range(s.count):
        out[index(i), :, s.rows : s.lanes] = jnp.concatenate(
            [
                values[:, t * s.cols + i * s.share : t * s.cols + (i + 1) * s.share]
                for t in range(2)
            ],
            axis=1,
        )


def each(count, body, init):
    if count <= 8:
        for d in range(count):
            init = body(d, init)
        return init
    return lax.fori_loop(0, count, body, init)


def forward_kernel(s, table, mass, *refs):
    units, (row_two, thirds, col_one_out, col_two_out, row_one) = (
        refs[: 2 * s.count],
        refs[2 * s.count : 2 * s.count + 5],
    )
    matrix, sems = refs[2 * s.count + 5 :]
    copies = load_matrix(s, units, matrix, sems)
    zero = jnp.zeros((s.hists, 2 * s.cols), jnp.float32)
    inverse = lambda i: table[s.count + i]
    target = gather_targets(s, mass, inverse)
    for copy in copies:
        copy.wait()
    ones = jnp.ones((8, 2 * s.cols), jnp.bfloat16)

    def first(d, total):
        sums = nt(ones, matrix[d])
        row_one[d] = sums
        left = mass[d, :, : s.rows] / sums[0:1]
        return total + nn(left.astype(jnp.bfloat16), matrix[d])

    col_one = each(s.count, first, zero)
    col_one_out[...] = col_one
    panel = (target / col_one).astype(jnp.bfloat16)

    def second(d, total):
        row = nt(panel, matrix[d])
        row_two[d] = row
        left = mass[d, :, : s.rows] / row
        return total + nn(left.astype(jnp.bfloat16), matrix[d])

    col_two = each(s.count, second, zero)
    col_two_out[...] = col_two
    panel = (target / col_two).astype(jnp.bfloat16)

    def third(d, total):
        row = nt(panel, matrix[d])
        k = table[d]
        thirds[k, :, : s.rows] = row
        left = mass[d, :, : s.rows] / row
        return total + nn(left.astype(jnp.bfloat16), matrix[d])

    col_three = each(s.count, third, zero)
    scatter_targets(s, thirds, lambda i: i, col_three)


def backward_kernel(s, table, mass, cot, row_two, thirds, col_one, col_two, row_one, *refs):
    units, out, (matrix, sems) = refs[: 2 * s.count], refs[2 * s.count], refs[2 * s.count + 1 :]
    copies = load_matrix(s, units, matrix, sems)
    zero = jnp.zeros((s.hists, 2 * s.cols), jnp.float32)
    inverse = lambda i: table[s.count + i]
    target = gather_targets(s, mass, inverse)
    target_cot = gather_targets(s, cot, lambda i: i)
    col_three = gather_targets(s, thirds, lambda i: i)
    right_one = target / col_one[...]
    right_two = target / col_two[...]
    for copy in copies:
        copy.wait()
    panel = (-target_cot / col_three).astype(jnp.bfloat16)

    def third(d, total):
        k = table[d]
        grad = nt(panel, matrix[d])
        row = thirds[k, :, : s.rows]
        left = mass[d, :, : s.rows] / row
        term = grad / row
        out[d, :, : s.rows] = term
        rowgrad = -(cot[k, :, : s.rows] / row + term * left)
        return total + nn(rowgrad.astype(jnp.bfloat16), matrix[d])

    term_two = each(s.count, third, zero) / col_two[...]
    panel = (-term_two * right_two).astype(jnp.bfloat16)

    def second(d, total):
        row = row_two[d]
        term = nt(panel, matrix[d]) / row
        out[d, :, : s.rows] += term
        rowgrad = -term * (mass[d, :, : s.rows] / row)
        return total + nn(rowgrad.astype(jnp.bfloat16), matrix[d])

    term_one = each(s.count, second, zero) / col_one[...]
    panel = (-term_one * right_one).astype(jnp.bfloat16)

    def first(d, carry):
        out[d, :, : s.rows] += nt(panel, matrix[d]) / row_one[d, 0:1]
        return carry

    each(s.count, first, 0)
    scatter_targets(s, out, inverse, term_two + term_one)


def call(kernel, s, outs, table, arrays, units):
    return pl.pallas_call(
        functools.partial(kernel, s),
        out_shape=outs,
        in_specs=[pl.BlockSpec(memory_space=pltpu.SMEM)]
        + [pl.BlockSpec(memory_space=pltpu.VMEM)] * len(arrays)
        + [pl.BlockSpec(memory_space=pl.ANY)] * len(units),
        scratch_shapes=[
            pltpu.VMEM((s.count, s.rows, 2 * s.cols), jnp.bfloat16),
            pltpu.SemaphoreType.DMA((s.count,)),
        ],
        compiler_params=pltpu.CompilerParams(vmem_limit_bytes=VMEM),
    )(table, *arrays, *units)


def swap_cores(x):
    return lax.ppermute(x, "tgt", [(0, 1), (1, 0)])


def local(
    source_mass,
    target_mass,
    kernel_tiles,
    tile_cols,
    tile_count,
    source_cotangent,
    target_cotangent,
):
    count = lax.axis_size("src")
    rows, cols_here = source_mass.shape
    share = target_mass.shape[1]
    s = Shape(count, rows, CB_DEV * kernel_tiles.shape[2], cols_here // count, share)
    ring = np.array(ring_order(count), np.int32)
    place = np.argsort(ring).astype(np.int32)
    me = lax.axis_index("src")
    core = lax.axis_index("tgt")
    at = jnp.asarray(place)[me]
    order = jnp.asarray(ring)[(at + jnp.arange(count, dtype=jnp.int32)) % count]
    inverse = (jnp.asarray(place) - at) % count
    table = jnp.concatenate([order, inverse]).astype(jnp.int32)

    def shift(x, distance):
        pairs = [(int(ring[p]), int(ring[(p + distance) % count])) for p in range(count)]
        return lax.ppermute(x, "src", pairs)

    unit = dense_blocks(kernel_tiles, tile_cols, tile_count)
    held = {0: unit}
    for step in range(1, count // 2 + 1):
        if step < count - step:
            held[step] = shift(held[step - 1], -1)
            held[count - step] = shift(held[(count - step + 1) % count], 1)
        else:
            middle = rows // 2
            ahead = shift(held[step - 1][:middle], -1)
            behind = shift(held[step + 1][middle:], 1)
            held[step] = jnp.concatenate([ahead, behind])
    units = []
    for d in range(count):
        units += [held[d], swap_cores(held[d])]

    def by_histogram(source, target):
        target = target.astype(HALF).reshape(share, 2, cols_here)
        mine = lax.dynamic_index_in_dim(target, core, 1, keepdims=False)
        other = lax.dynamic_index_in_dim(target, 1 - core, 1, keepdims=False)
        both = jnp.concatenate([mine, swap_cores(other)]).T
        return jnp.concatenate(
            [
                source.astype(HALF).T.reshape(count, s.hists, rows),
                both.reshape(count, s.hists, 2 * share),
            ],
            axis=2,
        )

    message = by_histogram(source_mass, target_mass[0])
    parts = []
    for d in range(count):
        chunk = lax.dynamic_index_in_dim(message, order[(count - d) % count], 0, keepdims=False)
        parts.append(shift(chunk, -d) if d else chunk)
    mass = jnp.stack(parts).astype(jnp.float32)
    cot = lax.all_to_all(
        by_histogram(source_cotangent * COT_SCALE, target_cotangent[0] * COT_SCALE),
        "src",
        0,
        0,
        tiled=True,
    ).astype(jnp.float32)

    panel = jax.ShapeDtypeStruct((count, s.hists, rows), jnp.float32)
    wide = jax.ShapeDtypeStruct((count, s.hists, s.lanes), jnp.float32)
    column = jax.ShapeDtypeStruct((s.hists, 2 * s.cols), jnp.float32)
    sums = jax.ShapeDtypeStruct((count, 8, rows), jnp.float32)
    row_two, thirds, col_one, col_two, row_one = call(
        forward_kernel, s, (panel, wide, column, column, sums), table, (mass,), units
    )
    grads = call(
        backward_kernel,
        s,
        wide,
        table,
        (mass, cot, row_two, thirds, col_one, col_two, row_one),
        units,
    )

    def by_point(pieces):
        flat = pieces.reshape(cols_here, s.lanes).astype(jnp.float32)
        target = flat[:, rows:].T.reshape(2, share, cols_here)
        other = swap_cores(target[1].astype(HALF)).astype(jnp.float32)
        own = target[0]
        halves = [jnp.where(core == t, own, other) for t in range(2)]
        return flat[:, :rows].T, jnp.concatenate(halves, axis=1)

    row_three, col_three = by_point(lax.all_to_all(thirds.astype(HALF), "src", 0, 0, tiled=True))
    parts = []
    narrow = grads.astype(HALF)
    for d in range(count):
        parts.append(shift(narrow[d], d) if d else narrow[d])
    back = jnp.stack(parts)[(at - jnp.asarray(place)) % count]
    source_term, target_term = by_point(back)
    return (
        jnp.log(source_mass / row_three),
        jnp.log(target_mass[0] / col_three)[None],
        source_cotangent / source_mass + source_term * (1 / COT_SCALE),
        (target_cotangent[0] / target_mass[0] + target_term * (1 / COT_SCALE))[None],
    )


def solution(mesh):
    return jax.shard_map(
        local,
        mesh=mesh,
        in_specs=(
            P(("grp", "src"), "tgt"),
            P("tgt", ("grp", "src"), None),
            P(("grp", "src"), "tgt", None, None),
            P(("grp", "src"), "tgt"),
            P(("grp", "src"), "tgt"),
            P(("grp", "src"), "tgt"),
            P("tgt", ("grp", "src"), None),
        ),
        out_specs=(
            P(("grp", "src"), "tgt"),
            P("tgt", ("grp", "src"), None),
            P(("grp", "src"), "tgt"),
            P("tgt", ("grp", "src"), None),
        ),
        check_vma=False,
    )
```

```python
import functools

import jax
import jax.numpy as jnp
import numpy as np
from jax import lax
from jax.experimental import pallas as pl
from jax.experimental.pallas import tpu as pltpu
from jax.sharding import PartitionSpec as P

CB_DEV = 2
HALF = jnp.float16
COT_SCALE = 256.0
VMEM = 56 * 1024 * 1024


def ring_order(count):
    if count == 8:
        return [0, 2, 4, 6, 7, 5, 3, 1]
    return list(range(count))


def dense_blocks(kernel_tiles, tile_cols, tile_count):
    keep = kernel_tiles.shape[1]
    live = jnp.arange(keep, dtype=jnp.int32)[None, :] < tile_count
    hits = (tile_cols[:, :, None] == jnp.arange(CB_DEV, dtype=jnp.int32)) & live[:, :, None]
    blocks = jnp.einsum(
        "rkc,rkab->racb",
        hits.astype(jnp.bfloat16),
        kernel_tiles,
        preferred_element_type=jnp.float32,
    )
    rows, cols = blocks.shape[0] * blocks.shape[1], blocks.shape[2] * blocks.shape[3]
    return blocks.astype(jnp.bfloat16).reshape(rows, cols)


def nt(x, y):
    return lax.dot_general(x, y, (((1,), (1,)), ((), ())), preferred_element_type=jnp.float32)


def nn(x, y):
    return jnp.dot(x, y, preferred_element_type=jnp.float32)


class Shape:
    def __init__(self, count, rows, cols, hists, share):
        self.count = count
        self.rows = rows
        self.cols = cols
        self.hists = hists
        self.share = share
        self.lanes = rows + 2 * share
        self.units = []
        for d in range(count):
            if 2 * d == count:
                self.units += [(d, 0, rows // 2), (d, rows // 2, rows // 2)]
            else:
                self.units.append((d, 0, rows))


def load_matrix(s, units, matrix, sems):
    copies = []
    for k, (d, start, size) in enumerate(s.units):
        for t in range(2):
            copy = pltpu.make_async_copy(
                units[2 * k + t],
                matrix.at[d, pl.ds(start, size), pl.ds(t * s.cols, s.cols)],
                sems.at[d],
            )
            copy.start()
            copies.append(copy)
    return copies


def gather_targets(s, pieces):
    parts = []
    for t in range(2):
        lo = s.rows + t * s.share
        parts += [pieces[i, :, lo : lo + s.share] for i in range(s.count)]
    return jnp.concatenate(parts, axis=1)


def scatter_targets(s, out, values):
    for i in range(s.count):
        out[i, :, s.rows : s.lanes] = jnp.concatenate(
            [
                values[:, t * s.cols + i * s.share : t * s.cols + (i + 1) * s.share]
                for t in range(2)
            ],
            axis=1,
        )


def each(count, body, init):
    if count <= 8:
        for d in range(count):
            init = body(d, init)
        return init
    return lax.fori_loop(0, count, body, init)


def forward_kernel(s, table, mass, *refs):
    given = 2 * len(s.units)
    units = refs[:given]
    row_two, thirds, col_one_out, col_two_out, row_one, matrix, sems = refs[given:]
    copies = load_matrix(s, units, matrix, sems)
    zero = jnp.zeros((s.hists, 2 * s.cols), jnp.float32)
    target = gather_targets(s, mass)
    for copy in copies:
        copy.wait()
    ones = jnp.ones((8, 2 * s.cols), jnp.bfloat16)

    def first(d, total):
        sums = nt(ones, matrix[d])
        row_one[d] = sums
        left = mass[table[d], :, : s.rows] / sums[0:1]
        return total + nn(left.astype(jnp.bfloat16), matrix[d])

    col_one = each(s.count, first, zero)
    col_one_out[...] = col_one
    panel = (target / col_one).astype(jnp.bfloat16)

    def second(d, total):
        row = nt(panel, matrix[d])
        row_two[d] = row
        left = mass[table[d], :, : s.rows] / row
        return total + nn(left.astype(jnp.bfloat16), matrix[d])

    col_two = each(s.count, second, zero)
    col_two_out[...] = col_two
    panel = (target / col_two).astype(jnp.bfloat16)

    def third(d, total):
        row = nt(panel, matrix[d])
        k = table[d]
        thirds[k, :, : s.rows] = row
        left = mass[table[d], :, : s.rows] / row
        return total + nn(left.astype(jnp.bfloat16), matrix[d])

    col_three = each(s.count, third, zero)
    scatter_targets(s, thirds, col_three)


def backward_kernel(s, table, mass, cot, row_two, thirds, col_one, col_two, row_one, *refs):
    given = 2 * len(s.units)
    units = refs[:given]
    out, matrix, sems = refs[given:]
    copies = load_matrix(s, units, matrix, sems)
    zero = jnp.zeros((s.hists, 2 * s.cols), jnp.float32)
    target = gather_targets(s, mass)
    target_cot = gather_targets(s, cot)
    col_three = gather_targets(s, thirds)
    right_one = target / col_one[...]
    right_two = target / col_two[...]
    for copy in copies:
        copy.wait()
    panel = (-target_cot / col_three).astype(jnp.bfloat16)

    def third(d, total):
        k = table[d]
        grad = nt(panel, matrix[d])
        row = thirds[k, :, : s.rows]
        left = mass[table[d], :, : s.rows] / row
        term = grad / row
        out[table[d], :, : s.rows] = term
        rowgrad = -(cot[k, :, : s.rows] / row + term * left)
        return total + nn(rowgrad.astype(jnp.bfloat16), matrix[d])

    term_two = each(s.count, third, zero) / col_two[...]
    panel = (-term_two * right_two).astype(jnp.bfloat16)

    def second(d, total):
        row = row_two[d]
        term = nt(panel, matrix[d]) / row
        out[table[d], :, : s.rows] += term
        rowgrad = -term * (mass[table[d], :, : s.rows] / row)
        return total + nn(rowgrad.astype(jnp.bfloat16), matrix[d])

    term_one = each(s.count, second, zero) / col_one[...]
    panel = (-term_one * right_one).astype(jnp.bfloat16)

    def first(d, carry):
        out[table[d], :, : s.rows] += nt(panel, matrix[d]) / row_one[d, 0:1]
        return carry

    each(s.count, first, 0)
    scatter_targets(s, out, term_two + term_one)


def call(kernel, s, outs, table, arrays, units):
    return pl.pallas_call(
        functools.partial(kernel, s),
        out_shape=outs,
        in_specs=[pl.BlockSpec(memory_space=pltpu.SMEM)]
        + [pl.BlockSpec(memory_space=pltpu.VMEM)] * len(arrays)
        + [pl.BlockSpec(memory_space=pl.ANY)] * len(units),
        scratch_shapes=[
            pltpu.VMEM((s.count, s.rows, 2 * s.cols), jnp.bfloat16),
            pltpu.SemaphoreType.DMA((s.count,)),
        ],
        cost_estimate=pl.CostEstimate(
            flops=6 * 2 * s.count * s.rows * 2 * s.cols * 256,
            bytes_accessed=s.count * s.rows * 2 * s.cols * 4,
            transcendentals=0,
        ),
        compiler_params=pltpu.CompilerParams(vmem_limit_bytes=VMEM),
    )(table, *arrays, *units)


def swap_cores(x):
    return lax.ppermute(x, "tgt", [(0, 1), (1, 0)])


def local(
    source_mass,
    target_mass,
    kernel_tiles,
    tile_cols,
    tile_count,
    source_cotangent,
    target_cotangent,
):
    count = lax.axis_size("src")
    rows, cols_here = source_mass.shape
    share = target_mass.shape[1]
    s = Shape(count, rows, CB_DEV * kernel_tiles.shape[2], cols_here // count, share)
    ring = np.array(ring_order(count), np.int32)
    place = np.argsort(ring).astype(np.int32)
    me = lax.axis_index("src")
    core = lax.axis_index("tgt")
    at = jnp.asarray(place)[me]
    table = jnp.asarray(ring)[(at + jnp.arange(count, dtype=jnp.int32)) % count]

    def shift(x, distance):
        pairs = [(int(ring[p]), int(ring[(p + distance) % count])) for p in range(count)]
        return lax.ppermute(x, "src", pairs)

    def exchange(x):
        return lax.all_to_all(x, "src", 0, 0, tiled=True)

    def by_histogram(source, target):
        target = target.astype(HALF).reshape(share, 2, cols_here)
        mine = lax.dynamic_index_in_dim(target, core, 1, keepdims=False)
        other = lax.dynamic_index_in_dim(target, 1 - core, 1, keepdims=False)
        both = jnp.concatenate([mine, swap_cores(other)]).T
        return jnp.concatenate(
            [
                source.astype(HALF).T.reshape(count, s.hists, rows),
                both.reshape(count, s.hists, 2 * share),
            ],
            axis=2,
        )

    mass_message = by_histogram(source_mass, target_mass[0])
    cot_message = by_histogram(source_cotangent * COT_SCALE, target_cotangent[0] * COT_SCALE)
    mass = None

    ahead = behind = dense_blocks(kernel_tiles, tile_cols, tile_count)
    pieces = {(0, 0): ahead}
    swapped = {(0, 0): swap_cores(ahead)}
    before = []
    rounds = count // 2
    for step in range(1, rounds + 1):
        ready = [swapped[k] for k in before]
        if step == min(2, rounds):
            ready.append(mass_message)
        if step == rounds:
            mass = exchange(mass_message).astype(jnp.float32)
            ready += [mass, cot_message]
        (ahead, behind), ready = lax.optimization_barrier(((ahead, behind), ready))
        for k, piece in zip(before, ready):
            swapped[k] = piece
        if step == min(2, rounds):
            mass_message = ready[len(before)]
        if step == rounds:
            mass, cot_message = ready[-2:]
        if 2 * step == count:
            ahead, behind = ahead[: rows // 2], behind[rows // 2 :]
            new = {(step, 0): shift(ahead, -1), (step, rows // 2): shift(behind, 1)}
        else:
            ahead, behind = shift(ahead, -1), shift(behind, 1)
            new = {(step, 0): ahead, (count - step, 0): behind}
        before = list(new) if step > 1 else [(0, 0), *new]
        pieces.update(new)
        swapped.update({k: swap_cores(v) for k, v in new.items()})
    units = []
    for d, start, _ in s.units:
        units += [pieces[d, start], swapped[d, start]]
    cot = exchange(cot_message).astype(jnp.float32)

    panel = jax.ShapeDtypeStruct((count, s.hists, rows), jnp.float32)
    wide = jax.ShapeDtypeStruct((count, s.hists, s.lanes), jnp.float32)
    column = jax.ShapeDtypeStruct((s.hists, 2 * s.cols), jnp.float32)
    sums = jax.ShapeDtypeStruct((count, 8, rows), jnp.float32)
    row_two, thirds, col_one, col_two, row_one = call(
        forward_kernel, s, (panel, wide, column, column, sums), table, (mass,), units
    )
    grads = call(
        backward_kernel,
        s,
        wide,
        table,
        (mass, cot, row_two, thirds, col_one, col_two, row_one),
        units,
    )

    def by_point(pieces):
        flat = pieces.reshape(cols_here, s.lanes).astype(jnp.float32)
        target = flat[:, rows:].T.reshape(2, share, cols_here)
        other = swap_cores(target[1].astype(HALF)).astype(jnp.float32)
        own = target[0]
        halves = [jnp.where(core == t, own, other) for t in range(2)]
        return flat[:, :rows].T, jnp.concatenate(halves, axis=1)

    row_three, col_three = by_point(exchange(thirds.astype(HALF)))
    source_term, target_term = by_point(exchange(grads.astype(HALF)))
    return (
        jnp.log(source_mass / row_three),
        jnp.log(target_mass[0] / col_three)[None],
        source_cotangent / source_mass + source_term * (1 / COT_SCALE),
        (target_cotangent[0] / target_mass[0] + target_term * (1 / COT_SCALE))[None],
    )


def solution(mesh):
    return jax.shard_map(
        local,
        mesh=mesh,
        in_specs=(
            P(("grp", "src"), "tgt"),
            P("tgt", ("grp", "src"), None),
            P(("grp", "src"), "tgt", None, None),
            P(("grp", "src"), "tgt"),
            P(("grp", "src"), "tgt"),
            P(("grp", "src"), "tgt"),
            P("tgt", ("grp", "src"), None),
        ),
        out_specs=(
            P(("grp", "src"), "tgt"),
            P("tgt", ("grp", "src"), None),
            P(("grp", "src"), "tgt"),
            P("tgt", ("grp", "src"), None),
        ),
        check_vma=False,
    )
```

```python
import functools

import jax
import jax.numpy as jnp
import numpy as np
from jax import lax
from jax.experimental import pallas as pl
from jax.experimental.pallas import tpu as pltpu
from jax.sharding import PartitionSpec as P

CB_DEV = 2
HALF = jnp.float16
COT_SCALE = 256.0
VMEM_REST = 16 * 1024 * 1024


def ring_order(count):
    if count == 8:
        return [0, 2, 4, 6, 7, 5, 3, 1]
    return list(range(count))


def dense_blocks(kernel_tiles, tile_cols, tile_count):
    keep = kernel_tiles.shape[1]
    live = jnp.arange(keep, dtype=jnp.int32)[None, :] < tile_count
    hits = (tile_cols[:, :, None] == jnp.arange(CB_DEV, dtype=jnp.int32)) & live[:, :, None]
    blocks = jnp.einsum(
        "rkc,rkab->racb",
        hits.astype(jnp.bfloat16),
        kernel_tiles,
        preferred_element_type=jnp.float32,
    )
    rows, cols = blocks.shape[0] * blocks.shape[1], blocks.shape[2] * blocks.shape[3]
    return blocks.astype(jnp.bfloat16).reshape(rows, cols)


def nt(x, y):
    return lax.dot_general(x, y, (((1,), (1,)), ((), ())), preferred_element_type=jnp.float32)


def nn(x, y):
    return jnp.dot(x, y, preferred_element_type=jnp.float32)


class Shape:
    def __init__(self, count, rows, cols, hists, share):
        self.count = count
        self.rows = rows
        self.cols = cols
        self.hists = hists
        self.share = share
        self.lanes = rows + 2 * share
        self.units = []
        for d in range(count):
            if 2 * d == count:
                self.units += [(d, 0, rows // 2), (d, rows // 2, rows // 2)]
            else:
                self.units.append((d, 0, rows))


def load_matrix(s, units, matrix, sems):
    copies = {}
    for k, (d, start, size) in enumerate(s.units):
        for t in range(2):
            copy = pltpu.make_async_copy(
                units[2 * k + t],
                matrix.at[d, pl.ds(start, size), pl.ds(t * s.cols, s.cols)],
                sems.at[d],
            )
            copy.start()
            copies.setdefault(d, []).append(copy)
    return copies


def arrived(s, copies, d):
    if s.count > 8:
        if d is not None:
            return
        waited = range(s.count)
    else:
        waited = () if d is None else (d,)
    for k in waited:
        for copy in copies[k]:
            copy.wait()


def gather_targets(s, pieces, core, part):
    lo = part * s.share
    return jnp.concatenate(
        [
            pieces[2 * i + side, :, lo : lo + s.share]
            for side in (core, 1 - core)
            for i in range(s.count)
        ],
        axis=1,
    )


def scatter_targets(s, out, values):
    for i in range(s.count):
        out[i, :, s.rows : s.lanes] = jnp.concatenate(
            [
                values[:, t * s.cols + i * s.share : t * s.cols + (i + 1) * s.share]
                for t in range(2)
            ],
            axis=1,
        )


def each(count, body, init):
    if count <= 8:
        for d in range(count):
            init = body(d, init)
        return init
    return lax.fori_loop(0, count, body, init)


def forward_kernel(s, table, mass, points, *refs):
    given = 2 * len(s.units)
    units = refs[:given]
    row_two, thirds, col_one_out, col_two_out, col_three_out, row_one, matrix, sems = refs[given:]
    copies = load_matrix(s, units, matrix, sems)
    zero = jnp.zeros((s.hists, 2 * s.cols), jnp.float32)
    target = gather_targets(s, points, table[s.count], 0)
    arrived(s, copies, None)
    ones = jnp.ones((8, 2 * s.cols), jnp.bfloat16)

    def first(d, total):
        arrived(s, copies, d)
        sums = nt(ones, matrix[d])
        row_one[d] = sums
        left = mass[table[d]] / sums[0:1]
        return total + nn(left.astype(jnp.bfloat16), matrix[d])

    col_one = each(s.count, first, zero)
    col_one_out[...] = col_one
    panel = (target / col_one).astype(jnp.bfloat16)

    def second(d, total):
        row = nt(panel, matrix[d])
        row_two[d] = row
        left = mass[table[d]] / row
        return total + nn(left.astype(jnp.bfloat16), matrix[d])

    col_two = each(s.count, second, zero)
    col_two_out[...] = col_two
    panel = (target / col_two).astype(jnp.bfloat16)

    def third(d, total):
        row = nt(panel, matrix[d])
        k = table[d]
        thirds[k, :, : s.rows] = row
        left = mass[table[d]] / row
        return total + nn(left.astype(jnp.bfloat16), matrix[d])

    col_three = each(s.count, third, zero)
    col_three_out[...] = col_three
    scatter_targets(s, thirds, col_three)


def backward_kernel(
    s, table, mass, points, cot, row_two, thirds, col_one, col_two, col_three, row_one, *refs
):
    given = 2 * len(s.units)
    units = refs[:given]
    out, matrix, sems = refs[given:]
    copies = load_matrix(s, units, matrix, sems)
    zero = jnp.zeros((s.hists, 2 * s.cols), jnp.float32)
    target = gather_targets(s, points, table[s.count], 0)
    target_cot = gather_targets(s, points, table[s.count], 1)
    right_one = target / col_one[...]
    right_two = target / col_two[...]
    arrived(s, copies, None)
    panel = (-target_cot / col_three[...]).astype(jnp.bfloat16)

    def third(d, total):
        arrived(s, copies, d)
        k = table[d]
        grad = nt(panel, matrix[d])
        row = thirds[k, :, : s.rows]
        left = mass[table[d]] / row
        term = grad / row
        out[table[d], :, : s.rows] = term
        rowgrad = -(cot[k] / row + term * left)
        return total + nn(rowgrad.astype(jnp.bfloat16), matrix[d])

    term_two = each(s.count, third, zero) / col_two[...]
    panel = (-term_two * right_two).astype(jnp.bfloat16)

    def second(d, total):
        row = row_two[d]
        term = nt(panel, matrix[d]) / row
        out[table[d], :, : s.rows] += term
        rowgrad = -term * (mass[table[d]] / row)
        return total + nn(rowgrad.astype(jnp.bfloat16), matrix[d])

    term_one = each(s.count, second, zero) / col_one[...]
    panel = (-term_one * right_one).astype(jnp.bfloat16)

    def first(d, carry):
        out[table[d], :, : s.rows] += nt(panel, matrix[d]) / row_one[d, 0:1]
        return carry

    each(s.count, first, 0)
    scatter_targets(s, out, term_two + term_one)


def call(kernel, s, outs, table, arrays, units):
    return pl.pallas_call(
        functools.partial(kernel, s),
        out_shape=outs,
        in_specs=[pl.BlockSpec(memory_space=pltpu.SMEM)]
        + [pl.BlockSpec(memory_space=pltpu.VMEM)] * len(arrays)
        + [pl.BlockSpec(memory_space=pl.ANY)] * len(units),
        scratch_shapes=[
            pltpu.VMEM((s.count, s.rows, 2 * s.cols), jnp.bfloat16),
            pltpu.SemaphoreType.DMA((s.count,)),
        ],
        cost_estimate=pl.CostEstimate(
            flops=6 * 2 * s.count * s.rows * 2 * s.cols * 256,
            bytes_accessed=s.count * s.rows * 2 * s.cols * 4,
            transcendentals=0,
        ),
        compiler_params=pltpu.CompilerParams(
            vmem_limit_bytes=VMEM_REST + s.count * s.rows * 2 * s.cols * 2
        ),
    )(table, *arrays, *units)


def swap_cores(x):
    return lax.ppermute(x, "tgt", [(0, 1), (1, 0)])


def local(
    source_mass,
    target_mass,
    kernel_tiles,
    tile_cols,
    tile_count,
    source_cotangent,
    target_cotangent,
):
    count = lax.axis_size("src")
    rows, cols_here = source_mass.shape
    share = target_mass.shape[1]
    s = Shape(count, rows, CB_DEV * kernel_tiles.shape[2], cols_here // count, share)
    ring = np.array(ring_order(count), np.int32)
    place = np.argsort(ring).astype(np.int32)
    me = lax.axis_index("src")
    core = lax.axis_index("tgt")
    at = jnp.asarray(place)[me]
    table = jnp.asarray(ring)[(at + jnp.arange(count, dtype=jnp.int32)) % count]
    table = jnp.concatenate([table, core[None]]).astype(jnp.int32)

    def shift(x, distance):
        pairs = [(int(ring[p]), int(ring[(p + distance) % count])) for p in range(count)]
        return lax.ppermute(x, "src", pairs)

    def exchange(x):
        return lax.all_to_all(x, "src", 0, 0, tiled=True)

    def by_histogram(source):
        return source.astype(HALF).T.reshape(count, s.hists, rows)

    unit = dense_blocks(kernel_tiles, tile_cols, tile_count)
    mass_message = by_histogram(source_mass)
    cot_message = by_histogram(source_cotangent * COT_SCALE)
    both = jnp.stack([target_mass[0], target_cotangent[0] * COT_SCALE]).astype(HALF)
    both = both.reshape(2, share, 2, count, s.hists).transpose(3, 2, 4, 0, 1)
    points_message = both.reshape(2 * count, s.hists, 2 * share)

    pieces = {(0, 0): unit}
    swapped = {(0, 0): swap_cores(unit)}
    ahead = behind = unit
    before = {}
    last = count // 2
    for step in range(1, last + 1):
        due = before.get(step - 2, [])
        extra = [swapped[key] for key in due]
        if step == 2:
            extra += [mass_message, points_message, table]
        if step == last:
            mass = exchange(mass_message).astype(jnp.float32)
            points = lax.all_to_all(points_message, ("src", "tgt"), 0, 0, tiled=True)
            extra += [mass, points.astype(jnp.float32), cot_message]
        ahead, behind, extra = lax.optimization_barrier((ahead, behind, extra))
        swapped.update(zip(due, extra))
        if step == 2:
            mass_message, points_message, table = extra[-3:]
        if step == last:
            mass, points, cot_message = extra[-3:]
        if 2 * step == count:
            middle = rows // 2
            new = {
                (step, 0): shift(ahead[:middle], -1),
                (step, middle): shift(behind[middle:], 1),
            }
        else:
            ahead, behind = shift(ahead, -1), shift(behind, 1)
            new = {(step, 0): ahead, (count - step, 0): behind}
        pieces.update(new)
        swapped.update({key: swap_cores(piece) for key, piece in new.items()})
        before[step] = list(new) + ([(0, 0)] if step == 1 else [])
    units = []
    for d, start, _ in s.units:
        units += [pieces[d, start], swapped[d, start]]
    cot = exchange(cot_message).astype(jnp.float32)

    panel = jax.ShapeDtypeStruct((count, s.hists, rows), jnp.float32)
    wide = jax.ShapeDtypeStruct((count, s.hists, s.lanes), jnp.float32)
    column = jax.ShapeDtypeStruct((s.hists, 2 * s.cols), jnp.float32)
    sums = jax.ShapeDtypeStruct((count, 8, rows), jnp.float32)
    row_two, thirds, col_one, col_two, col_three, row_one = call(
        forward_kernel,
        s,
        (panel, wide, column, column, column, sums),
        table,
        (mass, points),
        units,
    )
    grads = call(
        backward_kernel,
        s,
        wide,
        table,
        (mass, points, cot, row_two, thirds, col_one, col_two, col_three, row_one),
        units,
    )

    def by_point(pieces):
        flat = pieces.reshape(cols_here, s.lanes).astype(jnp.float32)
        target = flat[:, rows:].T.reshape(2, share, cols_here)
        other = swap_cores(target[1].astype(HALF)).astype(jnp.float32)
        own = target[0]
        halves = [jnp.where(core == t, own, other) for t in range(2)]
        return flat[:, :rows].T, jnp.concatenate(halves, axis=1)

    row_three, col_three = by_point(exchange(thirds.astype(HALF)))
    source_potential = jnp.log(source_mass / row_three)
    target_potential = jnp.log(target_mass[0] / col_three)
    back, source_potential, target_potential = lax.optimization_barrier(
        (exchange(grads.astype(HALF)), source_potential, target_potential)
    )
    source_term, target_term = by_point(back)
    return (
        source_potential,
        target_potential[None],
        source_cotangent / source_mass + source_term * (1 / COT_SCALE),
        (target_cotangent[0] / target_mass[0] + target_term * (1 / COT_SCALE))[None],
    )


def solution(mesh):
    return jax.shard_map(
        local,
        mesh=mesh,
        in_specs=(
            P(("grp", "src"), "tgt"),
            P("tgt", ("grp", "src"), None),
            P(("grp", "src"), "tgt", None, None),
            P(("grp", "src"), "tgt"),
            P(("grp", "src"), "tgt"),
            P(("grp", "src"), "tgt"),
            P("tgt", ("grp", "src"), None),
        ),
        out_specs=(
            P(("grp", "src"), "tgt"),
            P("tgt", ("grp", "src"), None),
            P(("grp", "src"), "tgt"),
            P("tgt", ("grp", "src"), None),
        ),
        check_vma=False,
    )
```

```python
import functools

import jax
import jax.numpy as jnp
import numpy as np
from jax import lax
from jax.experimental import pallas as pl
from jax.experimental.pallas import tpu as pltpu
from jax.sharding import PartitionSpec as P

CB_DEV = 2
HALF = jnp.float16
COT_SCALE = 256.0
VMEM = 56 * 1024 * 1024
STREAMS = 2


def ring_order(count):
    if count == 8:
        return [0, 2, 4, 6, 7, 5, 3, 1]
    return list(range(count))


def dense_blocks(kernel_tiles, tile_cols, tile_count):
    keep = kernel_tiles.shape[1]
    live = jnp.arange(keep, dtype=jnp.int32)[None, :] < tile_count
    hits = (tile_cols[:, :, None] == jnp.arange(CB_DEV, dtype=jnp.int32)) & live[:, :, None]
    blocks = jnp.einsum(
        "rkc,rkab->racb",
        hits.astype(jnp.bfloat16),
        kernel_tiles,
        preferred_element_type=jnp.float32,
    )
    rows, cols = blocks.shape[0] * blocks.shape[1], blocks.shape[2] * blocks.shape[3]
    return blocks.astype(jnp.bfloat16).reshape(rows, cols)


def nt(x, y):
    return lax.dot_general(x, y, (((1,), (1,)), ((), ())), preferred_element_type=jnp.float32)


def nn(x, y):
    return jnp.dot(x, y, preferred_element_type=jnp.float32)


class Shape:
    def __init__(self, count, rows, cols, hists, share):
        self.count = count
        self.rows = rows
        self.cols = cols
        self.hists = hists
        self.share = share
        self.lanes = rows + 2 * share
        streams = STREAMS if count <= 8 else 1
        self.streams = [(k * rows // streams, rows // streams) for k in range(streams)]
        self.units = []
        for d in range(count):
            for start, size in self.streams:
                if 2 * d == count and streams == 1:
                    self.units += [(d, 0, rows // 2), (d, rows // 2, rows // 2)]
                else:
                    self.units.append((d, start, size))


def load_matrix(s, units, matrix, sems):
    copies = {}
    for k, (d, start, size) in enumerate(s.units):
        for t in range(2):
            copy = pltpu.make_async_copy(
                units[2 * k + t],
                matrix.at[d, pl.ds(start, size), pl.ds(t * s.cols, s.cols)],
                sems.at[d],
            )
            copy.start()
            copies.setdefault(d, []).append(copy)
    return copies


def arrived(s, copies, d):
    if s.count > 8:
        if d is not None:
            return
        waited = range(s.count)
    else:
        waited = () if d is None else (d,)
    for k in waited:
        for copy in copies[k]:
            copy.wait()


def gather_targets(s, pieces, core, part):
    lo = part * s.share
    return jnp.concatenate(
        [
            pieces[2 * i + side, :, lo : lo + s.share]
            for side in (core, 1 - core)
            for i in range(s.count)
        ],
        axis=1,
    )


def scatter_targets(s, out, values):
    for i in range(s.count):
        out[i, :, s.rows : s.lanes] = jnp.concatenate(
            [
                values[:, t * s.cols + i * s.share : t * s.cols + (i + 1) * s.share]
                for t in range(2)
            ],
            axis=1,
        )


def each(count, body, init):
    if count <= 8:
        for d in range(count):
            init = body(d, init)
        return init
    return lax.fori_loop(0, count, body, init)


def forward_kernel(s, table, mass, points, *refs):
    given = 2 * len(s.units)
    units = refs[:given]
    row_two, thirds, col_one_out, col_two_out, col_three_out, row_one, matrix, sems = refs[given:]
    copies = load_matrix(s, units, matrix, sems)
    zero = jnp.zeros((s.hists, 2 * s.cols), jnp.float32)
    target = gather_targets(s, points, table[s.count], 0)
    arrived(s, copies, None)
    ones = jnp.ones((8, 2 * s.cols), jnp.bfloat16)

    def first(d, total):
        arrived(s, copies, d)
        sums = nt(ones, matrix[d])
        row_one[d] = sums
        left = mass[table[d]] / sums[0:1]
        return total + nn(left.astype(jnp.bfloat16), matrix[d])

    col_one = each(s.count, first, zero)
    col_one_out[...] = col_one
    panel = (target / col_one).astype(jnp.bfloat16)

    def second(d, total):
        row = nt(panel, matrix[d])
        row_two[d] = row
        left = mass[table[d]] / row
        return total + nn(left.astype(jnp.bfloat16), matrix[d])

    col_two = each(s.count, second, zero)
    col_two_out[...] = col_two
    panel = (target / col_two).astype(jnp.bfloat16)

    def third(d, total):
        row = nt(panel, matrix[d])
        k = table[d]
        thirds[k, :, : s.rows] = row
        left = mass[table[d]] / row
        return total + nn(left.astype(jnp.bfloat16), matrix[d])

    col_three = each(s.count, third, zero)
    col_three_out[...] = col_three
    scatter_targets(s, thirds, col_three)


def backward_kernel(
    s, table, mass, points, cot, row_two, thirds, col_one, col_two, col_three, row_one, *refs
):
    given = 2 * len(s.units)
    units = refs[:given]
    out, matrix, sems = refs[given:]
    copies = load_matrix(s, units, matrix, sems)
    zero = jnp.zeros((s.hists, 2 * s.cols), jnp.float32)
    target = gather_targets(s, points, table[s.count], 0)
    target_cot = gather_targets(s, points, table[s.count], 1)
    right_one = target / col_one[...]
    right_two = target / col_two[...]
    arrived(s, copies, None)
    panel = (-target_cot / col_three[...]).astype(jnp.bfloat16)

    def third(d, total):
        arrived(s, copies, d)
        k = table[d]
        grad = nt(panel, matrix[d])
        row = thirds[k, :, : s.rows]
        left = mass[table[d]] / row
        term = grad / row
        out[table[d], :, : s.rows] = term
        rowgrad = -(cot[k] / row + term * left)
        return total + nn(rowgrad.astype(jnp.bfloat16), matrix[d])

    term_two = each(s.count, third, zero) / col_two[...]
    panel = (-term_two * right_two).astype(jnp.bfloat16)

    def second(d, total):
        row = row_two[d]
        term = nt(panel, matrix[d]) / row
        out[table[d], :, : s.rows] += term
        rowgrad = -term * (mass[table[d]] / row)
        return total + nn(rowgrad.astype(jnp.bfloat16), matrix[d])

    term_one = each(s.count, second, zero) / col_one[...]
    panel = (-term_one * right_one).astype(jnp.bfloat16)

    def first(d, carry):
        out[table[d], :, : s.rows] += nt(panel, matrix[d]) / row_one[d, 0:1]
        return carry

    each(s.count, first, 0)
    scatter_targets(s, out, term_two + term_one)


def call(kernel, s, outs, table, arrays, units):
    return pl.pallas_call(
        functools.partial(kernel, s),
        out_shape=outs,
        in_specs=[pl.BlockSpec(memory_space=pltpu.SMEM)]
        + [pl.BlockSpec(memory_space=pltpu.VMEM)] * len(arrays)
        + [pl.BlockSpec(memory_space=pl.ANY)] * len(units),
        scratch_shapes=[
            pltpu.VMEM((s.count, s.rows, 2 * s.cols), jnp.bfloat16),
            pltpu.SemaphoreType.DMA((s.count,)),
        ],
        cost_estimate=pl.CostEstimate(
            flops=6 * 2 * s.count * s.rows * 2 * s.cols * 256,
            bytes_accessed=s.count * s.rows * 2 * s.cols * 4,
            transcendentals=0,
        ),
        compiler_params=pltpu.CompilerParams(
            vmem_limit_bytes=VMEM
        ),
    )(table, *arrays, *units)


def swap_cores(x):
    return lax.ppermute(x, "tgt", [(0, 1), (1, 0)])


def local(
    source_mass,
    target_mass,
    kernel_tiles,
    tile_cols,
    tile_count,
    source_cotangent,
    target_cotangent,
):
    count = lax.axis_size("src")
    rows, cols_here = source_mass.shape
    share = target_mass.shape[1]
    s = Shape(count, rows, CB_DEV * kernel_tiles.shape[2], cols_here // count, share)
    ring = np.array(ring_order(count), np.int32)
    place = np.argsort(ring).astype(np.int32)
    me = lax.axis_index("src")
    core = lax.axis_index("tgt")
    at = jnp.asarray(place)[me]
    table = jnp.asarray(ring)[(at + jnp.arange(count, dtype=jnp.int32)) % count]
    table = jnp.concatenate([table, core[None]]).astype(jnp.int32)

    def shift(x, distance):
        pairs = [(int(ring[p]), int(ring[(p + distance) % count])) for p in range(count)]
        return lax.ppermute(x, "src", pairs)

    def exchange(x):
        return lax.all_to_all(x, "src", 0, 0, tiled=True)

    def by_histogram(source):
        return source.astype(HALF).T.reshape(count, s.hists, rows)

    unit = dense_blocks(kernel_tiles, tile_cols, tile_count)
    mass_message = by_histogram(source_mass)
    cot_message = by_histogram(source_cotangent * COT_SCALE)
    both = jnp.stack([target_mass[0], target_cotangent[0] * COT_SCALE]).astype(HALF)
    both = both.reshape(2, share, 2, count, s.hists).transpose(3, 2, 4, 0, 1)
    points_message = both.reshape(2 * count, s.hists, 2 * share)

    streams = s.streams
    pieces, swapped, heads, before = {}, {}, {}, {}
    for k, (start, size) in enumerate(streams):
        piece = unit[start : start + size]
        pieces[0, start] = piece
        heads[k] = {-1: piece, 1: piece}
        swapped[0, start] = swap_cores(piece)
        before[0, k] = [(0, start)]
    last = count // 2
    for step in range(1, last + 1):
        for k, (start, size) in enumerate(streams):
            if 2 * step < count:
                ways = {-1: (0, size), 1: (0, size)}
            elif len(streams) > 1:
                ways = {(-1, 1)[k % 2]: (0, size)}
            else:
                ways = {-1: (0, size // 2), 1: (size // 2, size // 2)}
            due = before.get((step - 2, k), [])
            extra = [swapped[key] for key in due]
            names = []
            if k == 0 and step == 2:
                mass = exchange(mass_message).astype(jnp.float32)
                names = ["mass", "table"]
                extra += [mass, table]
            if k == 0 and step == last - 1:
                points = lax.all_to_all(points_message, ("src", "tgt"), 0, 0, tiled=True)
                points = points.astype(jnp.float32)
                names = ["points"]
                extra += [points]
            if k == 0 and step == last:
                names = ["cot_message"]
                extra += [cot_message]
            now = [heads[k][way] for way in ways]
            now, extra = lax.optimization_barrier((now, extra))
            swapped.update(zip(due, extra))
            for name, value in zip(names, extra[len(due) :]):
                if name == "mass":
                    mass = value
                elif name == "table":
                    table = value
                elif name == "points":
                    points = value
                else:
                    cot_message = value
            new = {}
            for (way, (lo, some)), piece in zip(ways.items(), now):
                piece = heads[k][way] = shift(piece[lo : lo + some], way)
                new[(-way * step) % count, start + lo] = piece
            pieces.update(new)
            swapped.update({key: swap_cores(piece) for key, piece in new.items()})
            before[step, k] = list(new)
    units = []
    for d, start, _ in s.units:
        units += [pieces[d, start], swapped[d, start]]
    cot = exchange(cot_message).astype(jnp.float32)

    panel = jax.ShapeDtypeStruct((count, s.hists, rows), jnp.float32)
    wide = jax.ShapeDtypeStruct((count, s.hists, s.lanes), jnp.float32)
    column = jax.ShapeDtypeStruct((s.hists, 2 * s.cols), jnp.float32)
    sums = jax.ShapeDtypeStruct((count, 8, rows), jnp.float32)
    row_two, thirds, col_one, col_two, col_three, row_one = call(
        forward_kernel,
        s,
        (panel, wide, column, column, column, sums),
        table,
        (mass, points),
        units,
    )
    grads = call(
        backward_kernel,
        s,
        wide,
        table,
        (mass, points, cot, row_two, thirds, col_one, col_two, col_three, row_one),
        units,
    )

    def by_point(pieces):
        flat = pieces.reshape(cols_here, s.lanes).astype(jnp.float32)
        target = flat[:, rows:].T.reshape(2, share, cols_here)
        other = swap_cores(target[1].astype(HALF)).astype(jnp.float32)
        own = target[0]
        halves = [jnp.where(core == t, own, other) for t in range(2)]
        return flat[:, :rows].T, jnp.concatenate(halves, axis=1)

    row_three, col_three = by_point(exchange(thirds.astype(HALF)))
    source_potential = jnp.log(source_mass / row_three)
    target_potential = jnp.log(target_mass[0] / col_three)
    back, source_potential, target_potential = lax.optimization_barrier(
        (exchange(grads.astype(HALF)), source_potential, target_potential)
    )
    source_term, target_term = by_point(back)
    return (
        source_potential,
        target_potential[None],
        source_cotangent / source_mass + source_term * (1 / COT_SCALE),
        (target_cotangent[0] / target_mass[0] + target_term * (1 / COT_SCALE))[None],
    )


def solution(mesh):
    return jax.shard_map(
        local,
        mesh=mesh,
        in_specs=(
            P(("grp", "src"), "tgt"),
            P("tgt", ("grp", "src"), None),
            P(("grp", "src"), "tgt", None, None),
            P(("grp", "src"), "tgt"),
            P(("grp", "src"), "tgt"),
            P(("grp", "src"), "tgt"),
            P("tgt", ("grp", "src"), None),
        ),
        out_specs=(
            P(("grp", "src"), "tgt"),
            P("tgt", ("grp", "src"), None),
            P(("grp", "src"), "tgt"),
            P("tgt", ("grp", "src"), None),
        ),
        check_vma=False,
    )
```

```python
import functools

import jax
import jax.numpy as jnp
import numpy as np
from jax import lax
from jax.experimental import pallas as pl
from jax.experimental.pallas import tpu as pltpu
from jax.sharding import PartitionSpec as P

CB_DEV = 2
HALF = jnp.float16
COT_SCALE = 256.0
VMEM = 56 * 1024 * 1024
STREAMS = 2
GATHERED = 2


def ring_order(count):
    if count == 8:
        return [0, 2, 4, 6, 7, 5, 3, 1]
    return list(range(count))


def dense_blocks(kernel_tiles, tile_cols, tile_count):
    keep = kernel_tiles.shape[1]
    live = jnp.arange(keep, dtype=jnp.int32)[None, :] < tile_count
    hits = (tile_cols[:, :, None] == jnp.arange(CB_DEV, dtype=jnp.int32)) & live[:, :, None]
    blocks = jnp.einsum(
        "rkc,rkab->racb",
        hits.astype(jnp.bfloat16),
        kernel_tiles,
        preferred_element_type=jnp.float32,
    )
    rows, cols = blocks.shape[0] * blocks.shape[1], blocks.shape[2] * blocks.shape[3]
    return blocks.astype(jnp.bfloat16).reshape(rows, cols)


def nt(x, y):
    return lax.dot_general(x, y, (((1,), (1,)), ((), ())), preferred_element_type=jnp.float32)


def nn(x, y):
    return jnp.dot(x, y, preferred_element_type=jnp.float32)


class Shape:
    def __init__(self, count, rows, cols, hists, share):
        self.count = count
        self.rows = rows
        self.cols = cols
        self.hists = hists
        self.share = share
        self.lanes = rows + 2 * share
        streams = STREAMS if count <= 8 else 1
        self.streams = [(k * rows // streams, rows // streams) for k in range(streams)]
        self.units = []
        for d in range(count):
            for start, size in self.streams:
                if 2 * d == count and streams == 1:
                    self.units += [(d, 0, rows // 2), (d, rows // 2, rows // 2)]
                else:
                    self.units.append((d, start, size))
        self.given = sum(1 if self.whole(d) else 2 for d, _, _ in self.units)

    def whole(self, d):
        return min(d, self.count - d) <= GATHERED


def load_matrix(s, table, units, matrix, sems):
    copies = {}
    units = iter(units)
    for d, start, size in s.units:
        rows = pl.ds(start, size)
        if s.whole(d):
            pairs = [(next(units), matrix.at[d, rows])]
        else:
            pairs = []
            for side in (table[s.count], 1 - table[s.count]):
                columns = pl.ds(pl.multiple_of(side * s.cols, s.cols), s.cols)
                pairs.append((next(units), matrix.at[d, rows, columns]))
        for source, target in pairs:
            copy = pltpu.make_async_copy(source, target, sems.at[d])
            copy.start()
            copies.setdefault(d, []).append(copy)
    return copies


def arrived(s, copies, d):
    if s.count > 8:
        if d is not None:
            return
        waited = range(s.count)
    else:
        waited = () if d is None else (d,)
    for k in waited:
        for copy in copies[k]:
            copy.wait()


def gather_targets(s, pieces, part):
    lo = part * s.share
    return jnp.concatenate(
        [
            pieces[2 * i + side, :, lo : lo + s.share]
            for side in range(2)
            for i in range(s.count)
        ],
        axis=1,
    )


def scatter_targets(s, out, values):
    for i in range(s.count):
        out[i, :, s.rows : s.lanes] = jnp.concatenate(
            [
                values[:, t * s.cols + i * s.share : t * s.cols + (i + 1) * s.share]
                for t in range(2)
            ],
            axis=1,
        )


def each(count, body, init):
    if count <= 8:
        for d in range(count):
            init = body(d, init)
        return init
    return lax.fori_loop(0, count, body, init)


def forward_kernel(s, table, mass, points, *refs):
    given = s.given
    units = refs[:given]
    row_two, thirds, col_one_out, col_two_out, col_three_out, row_one, matrix, sems = refs[given:]
    copies = load_matrix(s, table, units, matrix, sems)
    zero = jnp.zeros((s.hists, 2 * s.cols), jnp.float32)
    target = gather_targets(s, points, 0)
    arrived(s, copies, None)
    ones = jnp.ones((8, 2 * s.cols), jnp.bfloat16)

    def first(d, total):
        arrived(s, copies, d)
        sums = nt(ones, matrix[d])
        row_one[d] = sums
        left = mass[table[d]] / sums[0:1]
        return total + nn(left.astype(jnp.bfloat16), matrix[d])

    col_one = each(s.count, first, zero)
    col_one_out[...] = col_one
    panel = (target / col_one).astype(jnp.bfloat16)

    def second(d, total):
        row = nt(panel, matrix[d])
        row_two[d] = row
        left = mass[table[d]] / row
        return total + nn(left.astype(jnp.bfloat16), matrix[d])

    col_two = each(s.count, second, zero)
    col_two_out[...] = col_two
    panel = (target / col_two).astype(jnp.bfloat16)

    def third(d, total):
        row = nt(panel, matrix[d])
        k = table[d]
        thirds[k, :, : s.rows] = row
        left = mass[table[d]] / row
        return total + nn(left.astype(jnp.bfloat16), matrix[d])

    col_three = each(s.count, third, zero)
    col_three_out[...] = col_three
    scatter_targets(s, thirds, col_three)


def backward_kernel(
    s, table, mass, points, cot, row_two, thirds, col_one, col_two, col_three, row_one, *refs
):
    given = s.given
    units = refs[:given]
    out, matrix, sems = refs[given:]
    copies = load_matrix(s, table, units, matrix, sems)
    zero = jnp.zeros((s.hists, 2 * s.cols), jnp.float32)
    target = gather_targets(s, points, 0)
    target_cot = gather_targets(s, points, 1)
    right_one = target / col_one[...]
    right_two = target / col_two[...]
    arrived(s, copies, None)
    panel = (-target_cot / col_three[...]).astype(jnp.bfloat16)

    def third(d, total):
        arrived(s, copies, d)
        k = table[d]
        grad = nt(panel, matrix[d])
        row = thirds[k, :, : s.rows]
        left = mass[table[d]] / row
        term = grad / row
        out[table[d], :, : s.rows] = term
        rowgrad = -(cot[k] / row + term * left)
        return total + nn(rowgrad.astype(jnp.bfloat16), matrix[d])

    term_two = each(s.count, third, zero) / col_two[...]
    panel = (-term_two * right_two).astype(jnp.bfloat16)

    def second(d, total):
        row = row_two[d]
        term = nt(panel, matrix[d]) / row
        out[table[d], :, : s.rows] += term
        rowgrad = -term * (mass[table[d]] / row)
        return total + nn(rowgrad.astype(jnp.bfloat16), matrix[d])

    term_one = each(s.count, second, zero) / col_one[...]
    panel = (-term_one * right_one).astype(jnp.bfloat16)

    def first(d, carry):
        out[table[d], :, : s.rows] += nt(panel, matrix[d]) / row_one[d, 0:1]
        return carry

    each(s.count, first, 0)
    scatter_targets(s, out, term_two + term_one)


def call(kernel, s, outs, table, arrays, units):
    return pl.pallas_call(
        functools.partial(kernel, s),
        out_shape=outs,
        in_specs=[pl.BlockSpec(memory_space=pltpu.SMEM)]
        + [pl.BlockSpec(memory_space=pltpu.VMEM)] * len(arrays)
        + [pl.BlockSpec(memory_space=pl.ANY)] * len(units),
        scratch_shapes=[
            pltpu.VMEM((s.count, s.rows, 2 * s.cols), jnp.bfloat16),
            pltpu.SemaphoreType.DMA((s.count,)),
        ],
        cost_estimate=pl.CostEstimate(
            flops=6 * 2 * s.count * s.rows * 2 * s.cols * 256,
            bytes_accessed=s.count * s.rows * 2 * s.cols * 4,
            transcendentals=0,
        ),
        compiler_params=pltpu.CompilerParams(
            vmem_limit_bytes=VMEM
        ),
    )(table, *arrays, *units)


def both_sets(x):
    return lax.all_gather(x, "tgt", axis=1, tiled=True)


def swap_cores(x):
    return lax.ppermute(x, "tgt", [(0, 1), (1, 0)])


def local(
    source_mass,
    target_mass,
    kernel_tiles,
    tile_cols,
    tile_count,
    source_cotangent,
    target_cotangent,
):
    count = lax.axis_size("src")
    rows, cols_here = source_mass.shape
    share = target_mass.shape[1]
    s = Shape(count, rows, CB_DEV * kernel_tiles.shape[2], cols_here // count, share)
    ring = np.array(ring_order(count), np.int32)
    place = np.argsort(ring).astype(np.int32)
    me = lax.axis_index("src")
    core = lax.axis_index("tgt")
    at = jnp.asarray(place)[me]
    table = jnp.asarray(ring)[(at + jnp.arange(count, dtype=jnp.int32)) % count]
    table = jnp.concatenate([table, core[None]]).astype(jnp.int32)

    def shift(x, distance):
        pairs = [(int(ring[p]), int(ring[(p + distance) % count])) for p in range(count)]
        return lax.ppermute(x, "src", pairs)

    def exchange(x):
        return lax.all_to_all(x, "src", 0, 0, tiled=True)

    def by_histogram(source):
        return source.astype(HALF).T.reshape(count, s.hists, rows)

    unit = dense_blocks(kernel_tiles, tile_cols, tile_count)
    mass_message = by_histogram(source_mass)
    cot_message = by_histogram(source_cotangent * COT_SCALE)
    both = jnp.stack([target_mass[0], target_cotangent[0] * COT_SCALE]).astype(HALF)
    both = both.reshape(2, share, 2, count, s.hists).transpose(3, 2, 4, 0, 1)
    points_message = both.reshape(2 * count, s.hists, 2 * share)

    streams = s.streams
    pieces, swapped, heads, before = {}, {}, {}, {}
    for k, (start, size) in enumerate(streams):
        piece = unit[start : start + size]
        pieces[0, start] = piece
        heads[k] = {-1: piece, 1: piece}
        swapped[0, start] = both_sets(piece)
    last = count // 2
    for step in range(1, last + 1):
        for k, (start, size) in enumerate(streams):
            if 2 * step < count:
                ways = {-1: (0, size), 1: (0, size)}
            elif len(streams) > 1:
                ways = {(-1, 1)[k % 2]: (0, size)}
            else:
                ways = {-1: (0, size // 2), 1: (size // 2, size // 2)}
            due = before.get((step - 2, k), [])
            extra = [swapped[key] for key in due]
            names = []
            if k == 0 and step == last - 1:
                mass = exchange(mass_message).astype(jnp.float32)
                names = ["mass", "table"]
                extra += [mass, table]
            if k == 0 and step == last:
                points = lax.all_to_all(points_message, ("src", "tgt"), 0, 0, tiled=True)
                points = points.astype(jnp.float32)
                names = ["points", "cot_message"]
                extra += [points, cot_message]
            now = [heads[k][way] for way in ways]
            now, extra = lax.optimization_barrier((now, extra))
            swapped.update(zip(due, extra))
            for name, value in zip(names, extra[len(due) :]):
                if name == "mass":
                    mass = value
                elif name == "table":
                    table = value
                elif name == "points":
                    points = value
                else:
                    cot_message = value
            new = {}
            for (way, (lo, some)), piece in zip(ways.items(), now):
                piece = heads[k][way] = shift(piece[lo : lo + some], way)
                new[(-way * step) % count, start + lo] = piece
            pieces.update(new)
            for key, piece in new.items():
                swapped[key] = both_sets(piece) if s.whole(key[0]) else swap_cores(piece)
            before[step, k] = [key for key in new if not s.whole(key[0])]
    units = []
    for d, start, _ in s.units:
        units += [swapped[d, start]] if s.whole(d) else [pieces[d, start], swapped[d, start]]
    cot = exchange(cot_message).astype(jnp.float32)

    panel = jax.ShapeDtypeStruct((count, s.hists, rows), jnp.float32)
    wide = jax.ShapeDtypeStruct((count, s.hists, s.lanes), jnp.float32)
    column = jax.ShapeDtypeStruct((s.hists, 2 * s.cols), jnp.float32)
    sums = jax.ShapeDtypeStruct((count, 8, rows), jnp.float32)
    row_two, thirds, col_one, col_two, col_three, row_one = call(
        forward_kernel,
        s,
        (panel, wide, column, column, column, sums),
        table,
        (mass, points),
        units,
    )
    grads = call(
        backward_kernel,
        s,
        wide,
        table,
        (mass, points, cot, row_two, thirds, col_one, col_two, col_three, row_one),
        units,
    )

    def by_point(pieces):
        flat = pieces.reshape(cols_here, s.lanes).astype(jnp.float32)
        target = flat[:, rows:].T.reshape(2, share, cols_here)
        own = lax.dynamic_index_in_dim(target, core, 0, keepdims=False)
        other = lax.dynamic_index_in_dim(target, 1 - core, 0, keepdims=False)
        other = swap_cores(other.astype(HALF)).astype(jnp.float32)
        halves = [jnp.where(core == t, own, other) for t in range(2)]
        return flat[:, :rows].T, jnp.concatenate(halves, axis=1)

    row_three, col_three = by_point(exchange(thirds.astype(HALF)))
    source_potential = jnp.log(source_mass / row_three)
    target_potential = jnp.log(target_mass[0] / col_three)
    back, source_potential, target_potential = lax.optimization_barrier(
        (exchange(grads.astype(HALF)), source_potential, target_potential)
    )
    source_term, target_term = by_point(back)
    return (
        source_potential,
        target_potential[None],
        source_cotangent / source_mass + source_term * (1 / COT_SCALE),
        (target_cotangent[0] / target_mass[0] + target_term * (1 / COT_SCALE))[None],
    )


def solution(mesh):
    return jax.shard_map(
        local,
        mesh=mesh,
        in_specs=(
            P(("grp", "src"), "tgt"),
            P("tgt", ("grp", "src"), None),
            P(("grp", "src"), "tgt", None, None),
            P(("grp", "src"), "tgt"),
            P(("grp", "src"), "tgt"),
            P(("grp", "src"), "tgt"),
            P("tgt", ("grp", "src"), None),
        ),
        out_specs=(
            P(("grp", "src"), "tgt"),
            P("tgt", ("grp", "src"), None),
            P(("grp", "src"), "tgt"),
            P("tgt", ("grp", "src"), None),
        ),
        check_vma=False,
    )
```

```python
import functools

import jax
import jax.numpy as jnp
import numpy as np
from jax import lax
from jax.experimental import pallas as pl
from jax.experimental.pallas import tpu as pltpu
from jax.sharding import PartitionSpec as P

CB_DEV = 2
HALF = jnp.float16
COT_SCALE = 256.0
VMEM_REST = 16 * 1024 * 1024
STREAMS = 2


def ring_order(count):
    if count == 8:
        return [0, 2, 4, 6, 7, 5, 3, 1]
    return list(range(count))


def dense_blocks(kernel_tiles, tile_cols, tile_count):
    keep = kernel_tiles.shape[1]
    live = jnp.arange(keep, dtype=jnp.int32)[None, :] < tile_count
    hits = (tile_cols[:, :, None] == jnp.arange(CB_DEV, dtype=jnp.int32)) & live[:, :, None]
    blocks = jnp.einsum(
        "rkc,rkab->racb",
        hits.astype(jnp.bfloat16),
        kernel_tiles,
        preferred_element_type=jnp.float32,
    )
    rows, cols = blocks.shape[0] * blocks.shape[1], blocks.shape[2] * blocks.shape[3]
    return blocks.astype(jnp.bfloat16).reshape(rows, cols)


def nt(x, y):
    return lax.dot_general(x, y, (((1,), (1,)), ((), ())), preferred_element_type=jnp.float32)


def nn(x, y):
    return jnp.dot(x, y, preferred_element_type=jnp.float32)


class Shape:
    def __init__(self, count, rows, cols, hists, share):
        self.count = count
        self.rows = rows
        self.cols = cols
        self.hists = hists
        self.share = share
        self.lanes = rows + 2 * share
        streams = STREAMS if count <= 8 else 1
        self.streams = [(k * rows // streams, rows // streams) for k in range(streams)]
        self.units = []
        for d in range(count):
            for start, size in self.streams:
                if 2 * d == count and streams == 1:
                    self.units += [(d, 0, rows // 2), (d, rows // 2, rows // 2)]
                else:
                    self.units.append((d, start, size))


def load_matrix(s, units, matrix, sems):
    copies = {}
    for k, (d, start, size) in enumerate(s.units):
        for t in range(2):
            copy = pltpu.make_async_copy(
                units[2 * k + t],
                matrix.at[d, pl.ds(start, size), pl.ds(t * s.cols, s.cols)],
                sems.at[d],
            )
            copy.start()
            copies.setdefault(d, []).append(copy)
    return copies


def arrived(s, copies, d):
    if s.count > 8:
        if d is not None:
            return
        waited = range(s.count)
    else:
        waited = () if d is None else (d,)
    for k in waited:
        for copy in copies[k]:
            copy.wait()


def gather_targets(s, pieces):
    return jnp.concatenate(
        [
            pieces[i, :, s.rows + t * s.share : s.rows + (t + 1) * s.share]
            for t in range(2)
            for i in range(s.count)
        ],
        axis=1,
    )


def scatter_targets(s, out, values):
    for i in range(s.count):
        out[i, :, s.rows : s.lanes] = jnp.concatenate(
            [
                values[:, t * s.cols + i * s.share : t * s.cols + (i + 1) * s.share]
                for t in range(2)
            ],
            axis=1,
        )


def each(count, body, init):
    if count <= 8:
        for d in range(count):
            init = body(d, init)
        return init
    return lax.fori_loop(0, count, body, init)


def forward_kernel(s, table, mass, *refs):
    units = refs[: 2 * len(s.units)]
    thirds, state_out, refs = refs[len(units)], refs[len(units) + 1 : len(units) + 6], refs[len(units) + 6 :]
    matrix, sems, state, state_sems = refs[0], refs[1], refs[2:7], refs[7]
    row_two, row_one, col_one, col_two, col_three = state
    copies = load_matrix(s, units, matrix, sems)
    zero = jnp.zeros((s.hists, 2 * s.cols), jnp.float32)
    target = gather_targets(s, mass)
    arrived(s, copies, None)
    ones = jnp.ones((8, 2 * s.cols), jnp.bfloat16)

    def first(d, total):
        arrived(s, copies, d)
        sums = nt(ones, matrix[d])
        row_one[d] = sums
        left = mass[table[d], :, : s.rows] / sums[0:1]
        return total + nn(left.astype(jnp.bfloat16), matrix[d])

    total = each(s.count, first, zero)
    col_one[...] = total
    panel = (target / total).astype(jnp.bfloat16)

    def second(d, total):
        row = nt(panel, matrix[d])
        row_two[d] = row
        left = mass[table[d], :, : s.rows] / row
        return total + nn(left.astype(jnp.bfloat16), matrix[d])

    total = each(s.count, second, zero)
    col_two[...] = total
    leaving = [
        pltpu.make_async_copy(state[k], state_out[k], state_sems.at[k]) for k in range(len(state))
    ]
    for copy in leaving[:-1]:
        copy.start()
    panel = (target / total).astype(jnp.bfloat16)

    def third(d, total):
        row = nt(panel, matrix[d])
        thirds[table[d], :, : s.rows] = row
        left = mass[table[d], :, : s.rows] / row
        return total + nn(left.astype(jnp.bfloat16), matrix[d])

    total = each(s.count, third, zero)
    col_three[...] = total
    leaving[-1].start()
    scatter_targets(s, thirds, total)
    for copy in leaving:
        copy.wait()


def backward_kernel(s, table, mass, cot, thirds, *refs):
    state_in, refs = refs[:5], refs[5:]
    units, refs = refs[: 2 * len(s.units)], refs[2 * len(s.units) :]
    out, matrix, sems, state, state_sems = refs[0], refs[1], refs[2], refs[3:8], refs[8]
    row_two, row_one, col_one, col_two, col_three = state
    arriving = [
        pltpu.make_async_copy(state_in[k], state[k], state_sems.at[k]) for k in range(len(state))
    ]
    arriving[-1].start()
    copies = load_matrix(s, units, matrix, sems)
    for copy in arriving[:-1]:
        copy.start()
    zero = jnp.zeros((s.hists, 2 * s.cols), jnp.float32)
    target = gather_targets(s, mass)
    target_cot = gather_targets(s, cot)
    arriving[-1].wait()
    panel = (-target_cot / col_three[...]).astype(jnp.bfloat16)
    arrived(s, copies, None)

    def third(d, total):
        arrived(s, copies, d)
        k = table[d]
        grad = nt(panel, matrix[d])
        row = thirds[k, :, : s.rows]
        left = mass[k, :, : s.rows] / row
        term = grad / row
        out[k, :, : s.rows] = term
        rowgrad = -(cot[k, :, : s.rows] / row + term * left)
        return total + nn(rowgrad.astype(jnp.bfloat16), matrix[d])

    total = each(s.count, third, zero)
    for copy in arriving[:-1]:
        copy.wait()
    term_two = total / col_two[...]
    panel = (-term_two * (target / col_two[...])).astype(jnp.bfloat16)

    def second(d, total):
        k = table[d]
        row = row_two[d]
        term = nt(panel, matrix[d]) / row
        out[k, :, : s.rows] += term
        rowgrad = -term * (mass[k, :, : s.rows] / row)
        return total + nn(rowgrad.astype(jnp.bfloat16), matrix[d])

    term_one = each(s.count, second, zero) / col_one[...]
    panel = (-term_one * (target / col_one[...])).astype(jnp.bfloat16)

    def first(d, carry):
        out[table[d], :, : s.rows] += nt(panel, matrix[d]) / row_one[d, 0:1]
        return carry

    each(s.count, first, 0)
    scatter_targets(s, out, term_two + term_one)


def call(kernel, s, outs, states, table, arrays, units):
    out_shape, out_specs = list(outs), [pl.BlockSpec(memory_space=pltpu.VMEM)] * len(outs)
    forward = len(arrays) == 1
    if forward:
        out_shape += states
        out_specs += [pl.BlockSpec(memory_space=pltpu.HBM)] * len(states)
    taken = len(units) + (0 if forward else len(states))
    return pl.pallas_call(
        functools.partial(kernel, s),
        out_shape=out_shape,
        in_specs=[pl.BlockSpec(memory_space=pltpu.SMEM)]
        + [pl.BlockSpec(memory_space=pltpu.VMEM)] * (len(arrays) - (taken - len(units)))
        + [pl.BlockSpec(memory_space=pltpu.HBM)] * taken,
        out_specs=out_specs,
        scratch_shapes=[
            pltpu.VMEM((s.count, s.rows, 2 * s.cols), jnp.bfloat16),
            pltpu.SemaphoreType.DMA((s.count,)),
            *[pltpu.VMEM(state.shape, state.dtype) for state in states],
            pltpu.SemaphoreType.DMA((len(states),)),
        ],
        cost_estimate=pl.CostEstimate(
            flops=6 * 2 * s.count * s.rows * 2 * s.cols * 256,
            bytes_accessed=s.count * s.rows * 2 * s.cols * 4,
            transcendentals=0,
        ),
        compiler_params=pltpu.CompilerParams(
            vmem_limit_bytes=VMEM_REST + s.count * s.rows * 2 * s.cols * 2
        ),
    )(table, *arrays, *units)


def swap_cores(x):
    return lax.ppermute(x, "tgt", [(0, 1), (1, 0)])


def local(
    source_mass,
    target_mass,
    kernel_tiles,
    tile_cols,
    tile_count,
    source_cotangent,
    target_cotangent,
):
    count = lax.axis_size("src")
    rows, cols_here = source_mass.shape
    share = target_mass.shape[1]
    s = Shape(count, rows, CB_DEV * kernel_tiles.shape[2], cols_here // count, share)
    ring = np.array(ring_order(count), np.int32)
    place = np.argsort(ring).astype(np.int32)
    me = lax.axis_index("src")
    core = lax.axis_index("tgt")
    at = jnp.asarray(place)[me]
    table = jnp.asarray(ring)[(at + jnp.arange(count, dtype=jnp.int32)) % count]

    def shift(x, distance):
        pairs = [(int(ring[p]), int(ring[(p + distance) % count])) for p in range(count)]
        return lax.ppermute(x, "src", pairs)

    def exchange(x):
        return lax.all_to_all(x, "src", 0, 0, tiled=True)

    def by_histogram(source, target):
        target = target.astype(HALF).reshape(share, 2, cols_here)
        mine = lax.dynamic_index_in_dim(target, core, 1, keepdims=False)
        other = lax.dynamic_index_in_dim(target, 1 - core, 1, keepdims=False)
        both = jnp.concatenate([mine, swap_cores(other)]).T
        return jnp.concatenate(
            [
                source.astype(HALF).T.reshape(count, s.hists, rows),
                both.reshape(count, s.hists, 2 * share),
            ],
            axis=2,
        )

    unit = dense_blocks(kernel_tiles, tile_cols, tile_count)

    streams = s.streams
    pieces, swapped, heads, before = {}, {}, {}, {}
    for k, (start, size) in enumerate(streams):
        piece = unit[start : start + size]
        pieces[0, start] = piece
        heads[k] = {-1: piece, 1: piece}
        swapped[0, start] = swap_cores(piece)
        before[0, k] = [(0, start)]
    last = count // 2
    for step in range(1, last + 1):
        for k, (start, size) in enumerate(streams):
            if 2 * step < count:
                ways = {-1: (0, size), 1: (0, size)}
            elif len(streams) > 1:
                ways = {(-1, 1)[k % 2]: (0, size)}
            else:
                ways = {-1: (0, size // 2), 1: (size // 2, size // 2)}
            due = before.get((step - 2, k), [])
            now, ready = [heads[k][way] for way in ways], [swapped[key] for key in due]
            if k == 0 and step == max(last - 1, 2):
                mass = exchange(mass_message).astype(jnp.float32)
                now, ready, mass, table = lax.optimization_barrier((now, ready, mass, table))
            elif k == 0 and step == last:
                now, ready, cot_message = lax.optimization_barrier((now, ready, cot_message))
            else:
                now, ready = lax.optimization_barrier((now, ready))
            swapped.update(zip(due, ready))
            new = {}
            for (way, (lo, some)), piece in zip(ways.items(), now):
                piece = heads[k][way] = shift(piece[lo : lo + some], way)
                new[(-way * step) % count, start + lo] = piece
            pieces.update(new)
            swapped.update({key: swap_cores(piece) for key, piece in new.items()})
            before[step, k] = list(new)
            if k == 0 and step == 1:
                head, mass_here, points_here = lax.optimization_barrier(
                    (heads[0][-1], source_mass, target_mass)
                )
                heads[0][-1] = pieces[1 % count, start] = head
                mass_message = by_histogram(mass_here, points_here[0])
            if k == 0 and step == max(last - 2, 1):
                cot_message = by_histogram(
                    source_cotangent * COT_SCALE, target_cotangent[0] * COT_SCALE
                )
    units = []
    for d, start, _ in s.units:
        units += [pieces[d, start], swapped[d, start]]
    cot = exchange(cot_message).astype(jnp.float32)

    wide = jax.ShapeDtypeStruct((count, s.hists, s.lanes), jnp.float32)
    column = jax.ShapeDtypeStruct((s.hists, 2 * s.cols), jnp.float32)
    states = [
        jax.ShapeDtypeStruct((count, s.hists, rows), jnp.float32),
        jax.ShapeDtypeStruct((count, 8, rows), jnp.float32),
        column,
        column,
        column,
    ]
    thirds, *state = call(forward_kernel, s, [wide], states, table, (mass,), units)
    (grads,) = call(
        backward_kernel, s, [wide], states, table, (mass, cot, thirds, *state), units
    )

    def by_point(pieces):
        flat = pieces.reshape(cols_here, s.lanes).astype(jnp.float32)
        target = flat[:, rows:].T.reshape(2, share, cols_here)
        other = swap_cores(target[1].astype(HALF)).astype(jnp.float32)
        own = target[0]
        halves = [jnp.where(core == t, own, other) for t in range(2)]
        return flat[:, :rows].T, jnp.concatenate(halves, axis=1)

    row_three, col_three = by_point(exchange(thirds.astype(HALF)))
    source_potential = jnp.log(source_mass / row_three)
    target_potential = jnp.log(target_mass[0] / col_three)
    source_known = source_cotangent / source_mass
    target_known = target_cotangent[0] / target_mass[0]
    back, source_potential, target_potential, source_known, target_known = lax.optimization_barrier(
        (
            exchange(grads.astype(HALF)),
            source_potential,
            target_potential,
            source_known,
            target_known,
        )
    )
    source_term, target_term = by_point(back)
    return (
        source_potential,
        target_potential[None],
        source_known + source_term * (1 / COT_SCALE),
        (target_known + target_term * (1 / COT_SCALE))[None],
    )


def solution(mesh):
    return jax.shard_map(
        local,
        mesh=mesh,
        in_specs=(
            P(("grp", "src"), "tgt"),
            P("tgt", ("grp", "src"), None),
            P(("grp", "src"), "tgt", None, None),
            P(("grp", "src"), "tgt"),
            P(("grp", "src"), "tgt"),
            P(("grp", "src"), "tgt"),
            P("tgt", ("grp", "src"), None),
        ),
        out_specs=(
            P(("grp", "src"), "tgt"),
            P("tgt", ("grp", "src"), None),
            P(("grp", "src"), "tgt"),
            P("tgt", ("grp", "src"), None),
        ),
        check_vma=False,
    )
```

```python
import copy
import functools

import jax
import jax.numpy as jnp
import numpy as np
from jax import lax
from jax.experimental import pallas as pl
from jax.experimental.pallas import tpu as pltpu
from jax.sharding import PartitionSpec as P

CB_DEV = 2
HALF = jnp.float16
COT_SCALE = 256.0
VMEM = 56 * 1024 * 1024


def ring_order(count):
    if count == 8:
        return [0, 2, 4, 6, 7, 5, 3, 1]
    return list(range(count))


def dense_blocks(kernel_tiles, tile_cols, tile_count):
    keep = kernel_tiles.shape[1]
    live = jnp.arange(keep, dtype=jnp.int32)[None, :] < tile_count
    hits = (tile_cols[:, :, None] == jnp.arange(CB_DEV, dtype=jnp.int32)) & live[:, :, None]
    blocks = jnp.einsum(
        "rkc,rkab->racb",
        hits.astype(jnp.bfloat16),
        kernel_tiles,
        preferred_element_type=jnp.float32,
    )
    rows, cols = blocks.shape[0] * blocks.shape[1], blocks.shape[2] * blocks.shape[3]
    return blocks.astype(jnp.bfloat16).reshape(rows, cols)


def nt(x, y):
    return lax.dot_general(x, y, (((1,), (1,)), ((), ())), preferred_element_type=jnp.float32)


def nn(x, y):
    return jnp.dot(x, y, preferred_element_type=jnp.float32)


class Shape:
    def only(self, units):
        kept = copy.copy(self)
        kept.units = units
        return kept

    def __init__(self, count, rows, cols, hists, share):
        self.count = count
        self.rows = rows
        self.cols = cols
        self.hists = hists
        self.share = share
        self.lanes = rows + 2 * share
        self.opposite = count // 2
        self.units = []
        for d in range(count):
            if d == self.opposite:
                self.units += [(d, 0, rows // 2), (d, rows // 2, rows // 2)]
            else:
                self.units.append((d, 0, rows))


def load_matrix(s, units, matrix, sems):
    copies = {}
    units = iter(units)
    for d, start, size in s.units:
        for t in range(2):
            copy = pltpu.make_async_copy(
                next(units),
                matrix.at[d, pl.ds(start, size), pl.ds(t * s.cols, s.cols)],
                sems.at[d],
            )
            copy.start()
            copies.setdefault(d, []).append(copy)

    def arrived(d):
        for piece in copies.pop(d, []):
            piece.wait()

    if s.count > 8:
        for d in range(s.count):
            arrived(d)
        return lambda d: None
    return arrived


def load(sources, targets, sems):
    copies = [
        pltpu.make_async_copy(source, target, sems.at[k])
        for k, (source, target) in enumerate(zip(sources, targets))
    ]
    for copy in copies:
        copy.start()
    return copies


def gather_targets(s, pieces):
    return jnp.concatenate(
        [
            pieces[i, :, s.rows + t * s.share : s.rows + (t + 1) * s.share]
            for t in range(2)
            for i in range(s.count)
        ],
        axis=1,
    )


def scatter_targets(s, out, values):
    for i in range(s.count):
        out[i, :, s.rows : s.lanes] = jnp.concatenate(
            [
                values[:, t * s.cols + i * s.share : t * s.cols + (i + 1) * s.share]
                for t in range(2)
            ],
            axis=1,
        )


def each(count, body, init):
    if count <= 8:
        for d in range(count):
            init = body(d, init)
        return init
    return lax.fori_loop(0, count, body, init)


def first_step(s, table, mass, matrix, row_one, d):
    sums = nt(jnp.ones((8, 2 * s.cols), jnp.bfloat16), matrix[d])
    row_one[d] = sums
    left = mass[table[d], :, : s.rows] / sums[0:1]
    return nn(left.astype(jnp.bfloat16), matrix[d])


def first_kernel(s, table, mass_in, *refs):
    units, (row_one, col_one, mass, matrix, sems, more_sems) = refs[:-6], refs[-6:]
    arriving = load([mass_in], [mass], more_sems)
    own = [unit for unit in s.units if unit[0] != s.opposite]
    arrived = load_matrix(s.only(own), units, matrix, sems)
    arriving[0].wait()

    def step(k, total):
        d = k + (k >= s.opposite)
        arrived(d)
        return total + first_step(s, table, mass, matrix, row_one, d)

    zero = jnp.zeros((s.hists, 2 * s.cols), jnp.float32)
    col_one[...] = each(s.count - 1, step, zero)


def forward_kernel(s, table, mass_in, row_one_in, col_one_in, *refs):
    units, refs = refs[: 2 * len(s.units)], refs[2 * len(s.units) :]
    thirds, leaving, (mass, matrix, sems, more_sems), state = refs[0], refs[1:6], refs[6:10], refs[10:]
    row_two, row_one, col_one, col_two, col_three = state
    arriving = load(
        [mass_in, row_one_in, col_one_in], [mass, row_one, col_one], more_sems
    )
    arrived = load_matrix(s, units, matrix, sems)
    for copy in arriving:
        copy.wait()
    target = gather_targets(s, mass)
    arrived(s.opposite)
    total = col_one[...] + first_step(s, table, mass, matrix, row_one, s.opposite)
    col_one[...] = total
    panel = (target / total).astype(jnp.bfloat16)
    zero = jnp.zeros((s.hists, 2 * s.cols), jnp.float32)

    def second(d, total):
        arrived(d)
        row = nt(panel, matrix[d])
        row_two[d] = row
        left = mass[table[d], :, : s.rows] / row
        return total + nn(left.astype(jnp.bfloat16), matrix[d])

    total = each(s.count, second, zero)
    col_two[...] = total
    started = load(state[:4], leaving[:4], more_sems)
    panel = (target / total).astype(jnp.bfloat16)

    def third(d, total):
        row = nt(panel, matrix[d])
        thirds[table[d], :, : s.rows] = row
        left = mass[table[d], :, : s.rows] / row
        return total + nn(left.astype(jnp.bfloat16), matrix[d])

    total = each(s.count, third, zero)
    col_three[...] = total
    last = pltpu.make_async_copy(col_three, leaving[4], more_sems.at[4])
    last.start()
    scatter_targets(s, thirds, total)
    for copy in [*started, last]:
        copy.wait()


def backward_kernel(s, table, mass_in, cot_in, thirds_in, *refs):
    state_in, units, refs = refs[:5], refs[5 : 5 + 2 * len(s.units)], refs[5 + 2 * len(s.units) :]
    out, (mass, matrix, sems, more_sems), state, (cot, thirds) = (
        refs[0],
        refs[1:5],
        refs[5:10],
        refs[10:],
    )
    row_two, row_one, col_one, col_two, col_three = state
    sources = [state_in[4], cot_in, thirds_in, mass_in]
    early = load(sources, [col_three, cot, thirds, mass], more_sems)
    arrived = load_matrix(s, units, matrix, sems)
    late = [
        pltpu.make_async_copy(state_in[k], state[k], more_sems.at[4 + k]) for k in range(4)
    ]
    for copy in late:
        copy.start()
    for copy in early:
        copy.wait()
    target = gather_targets(s, mass)
    target_cot = gather_targets(s, cot)
    panel = (-target_cot / col_three[...]).astype(jnp.bfloat16)
    zero = jnp.zeros((s.hists, 2 * s.cols), jnp.float32)

    def third(d, total):
        arrived(d)
        k = table[d]
        grad = nt(panel, matrix[d])
        row = thirds[k, :, : s.rows]
        left = mass[k, :, : s.rows] / row
        term = grad / row
        out[k, :, : s.rows] = term
        rowgrad = -(cot[k, :, : s.rows] / row + term * left)
        return total + nn(rowgrad.astype(jnp.bfloat16), matrix[d])

    total = each(s.count, third, zero)
    for copy in late:
        copy.wait()
    term_two = total / col_two[...]
    panel = (-term_two * (target / col_two[...])).astype(jnp.bfloat16)

    def second(d, total):
        k = table[d]
        row = row_two[d]
        term = nt(panel, matrix[d]) / row
        out[k, :, : s.rows] += term
        rowgrad = -term * (mass[k, :, : s.rows] / row)
        return total + nn(rowgrad.astype(jnp.bfloat16), matrix[d])

    term_one = each(s.count, second, zero) / col_one[...]
    panel = (-term_one * (target / col_one[...])).astype(jnp.bfloat16)

    def first(d, carry):
        out[table[d], :, : s.rows] += nt(panel, matrix[d]) / row_one[d, 0:1]
        return carry

    each(s.count, first, 0)
    scatter_targets(s, out, term_two + term_one)


def call(kernel, s, products, vmem_outs, hbm_outs, table, arrays, scratch):
    return pl.pallas_call(
        functools.partial(kernel, s),
        out_shape=[*vmem_outs, *hbm_outs],
        in_specs=[pl.BlockSpec(memory_space=pltpu.SMEM)]
        + [pl.BlockSpec(memory_space=pl.ANY)] * len(arrays),
        out_specs=[pl.BlockSpec(memory_space=pltpu.VMEM)] * len(vmem_outs)
        + [pl.BlockSpec(memory_space=pl.ANY)] * len(hbm_outs),
        scratch_shapes=[
            pltpu.VMEM((s.count, s.hists, s.lanes), jnp.float32),
            pltpu.VMEM((s.count, s.rows, 2 * s.cols), jnp.bfloat16),
            pltpu.SemaphoreType.DMA((s.count,)),
            pltpu.SemaphoreType.DMA((8,)),
            *[pltpu.VMEM(state.shape, state.dtype) for state in scratch],
        ],
        cost_estimate=pl.CostEstimate(
            flops=products * 2 * s.count * s.rows * 2 * s.cols * 256,
            bytes_accessed=s.count * s.rows * 2 * s.cols * 4,
            transcendentals=0,
        ),
        compiler_params=pltpu.CompilerParams(vmem_limit_bytes=VMEM),
    )(table, *arrays)


def swap_cores(x):
    return lax.ppermute(x, "tgt", [(0, 1), (1, 0)])


def local(
    source_mass,
    target_mass,
    kernel_tiles,
    tile_cols,
    tile_count,
    source_cotangent,
    target_cotangent,
):
    count = lax.axis_size("src")
    rows, cols_here = source_mass.shape
    share = target_mass.shape[1]
    s = Shape(count, rows, CB_DEV * kernel_tiles.shape[2], cols_here // count, share)
    ring = np.array(ring_order(count), np.int32)
    place = np.argsort(ring).astype(np.int32)
    me = lax.axis_index("src")
    core = lax.axis_index("tgt")
    at = jnp.asarray(place)[me]
    table = jnp.asarray(ring)[(at + jnp.arange(count, dtype=jnp.int32)) % count]

    def shift(x, distance):
        pairs = [(int(ring[p]), int(ring[(p + distance) % count])) for p in range(count)]
        return lax.ppermute(x, "src", pairs)

    def exchange(x):
        return lax.all_to_all(x, "src", 0, 0, tiled=True)

    def by_histogram(source, target):
        target = target.astype(HALF).reshape(share, 2, cols_here)
        mine = lax.dynamic_index_in_dim(target, core, 1, keepdims=False)
        other = lax.dynamic_index_in_dim(target, 1 - core, 1, keepdims=False)
        both = jnp.concatenate([mine, swap_cores(other)]).T
        return jnp.concatenate(
            [
                source.astype(HALF).T.reshape(count, s.hists, rows),
                both.reshape(count, s.hists, 2 * share),
            ],
            axis=2,
        )

    unit = dense_blocks(kernel_tiles, tile_cols, tile_count)

    pieces, before = {(0, 0): unit}, {0: [(0, 0)]}
    swapped = {(0, 0): swap_cores(unit)}
    ahead = behind = unit
    last = count // 2
    swapped[0, 0], mass_here, points_here = lax.optimization_barrier(
        (swapped[0, 0], source_mass, target_mass)
    )
    mass_message = by_histogram(mass_here, points_here[0])
    for step in range(1, last + 1):
        due = before.get(step - 2, [])
        ready = [swapped[key] for key in due]
        if step == 2:
            mass = exchange(mass_message).astype(jnp.float32)
            ahead, behind, ready, mass, table = lax.optimization_barrier(
                (ahead, behind, ready, mass, table)
            )
        elif step == last:
            ahead, behind, ready, cot_message = lax.optimization_barrier(
                (ahead, behind, ready, cot_message)
            )
        else:
            ahead, behind, ready = lax.optimization_barrier((ahead, behind, ready))
        swapped.update(zip(due, ready))
        if 2 * step == count:
            middle = rows // 2
            new = {
                (step, 0): shift(ahead[:middle], -1),
                (step, middle): shift(behind[middle:], 1),
            }
        else:
            ahead, behind = shift(ahead, -1), shift(behind, 1)
            new = {(step, 0): ahead, (count - step, 0): behind}
        pieces.update(new)
        swapped.update({key: swap_cores(piece) for key, piece in new.items()})
        before[step] = list(new)
        if step == max(last - 2, 1):
            head, cot_here, points_here = lax.optimization_barrier(
                (ahead, source_cotangent, target_cotangent)
            )
            ahead = pieces[step, 0] = head
            cot_message = by_histogram(cot_here * COT_SCALE, points_here[0] * COT_SCALE)
    units = []
    near = []
    for d, start, _ in s.units:
        units += [pieces[d, start], swapped[d, start]]
        near += [] if d == s.opposite else units[-2:]

    wide = jax.ShapeDtypeStruct((count, s.hists, s.lanes), jnp.float32)
    panel = jax.ShapeDtypeStruct((count, s.hists, rows), jnp.float32)
    sums = jax.ShapeDtypeStruct((count, 8, rows), jnp.float32)
    column = jax.ShapeDtypeStruct((s.hists, 2 * s.cols), jnp.float32)
    states = [panel, sums, column, column, column]
    row_one, col_one = call(first_kernel, s, 2, [sums, column], [], table, [mass, *near], [])
    cot = exchange(cot_message).astype(jnp.float32)
    thirds, *state = call(
        forward_kernel, s, 5, [wide], states, table, [mass, row_one, col_one, *units], states
    )
    (grads,) = call(
        backward_kernel,
        s,
        5,
        [wide],
        [],
        table,
        [mass, cot, thirds, *state, *units],
        [*states, wide, wide],
    )

    def by_point(pieces):
        flat = pieces.reshape(cols_here, s.lanes).astype(jnp.float32)
        target = flat[:, rows:].T.reshape(2, share, cols_here)
        other = swap_cores(target[1].astype(HALF)).astype(jnp.float32)
        own = target[0]
        halves = [jnp.where(core == t, own, other) for t in range(2)]
        return flat[:, :rows].T, jnp.concatenate(halves, axis=1)

    row_three, col_three = by_point(exchange(thirds.astype(HALF)))
    source_potential = jnp.log(source_mass / row_three)
    target_potential = jnp.log(target_mass[0] / col_three)
    source_known = source_cotangent / source_mass
    target_known = target_cotangent[0] / target_mass[0]
    back, source_potential, target_potential, source_known, target_known = lax.optimization_barrier(
        (
            exchange(grads.astype(HALF)),
            source_potential,
            target_potential,
            source_known,
            target_known,
        )
    )
    source_term, target_term = by_point(back)
    return (
        source_potential,
        target_potential[None],
        source_known + source_term * (1 / COT_SCALE),
        (target_known + target_term * (1 / COT_SCALE))[None],
    )


def solution(mesh):
    return jax.shard_map(
        local,
        mesh=mesh,
        in_specs=(
            P(("grp", "src"), "tgt"),
            P("tgt", ("grp", "src"), None),
            P(("grp", "src"), "tgt", None, None),
            P(("grp", "src"), "tgt"),
            P(("grp", "src"), "tgt"),
            P(("grp", "src"), "tgt"),
            P("tgt", ("grp", "src"), None),
        ),
        out_specs=(
            P(("grp", "src"), "tgt"),
            P("tgt", ("grp", "src"), None),
            P(("grp", "src"), "tgt"),
            P("tgt", ("grp", "src"), None),
        ),
        check_vma=False,
    )
```

```python
import functools

import jax
import jax.numpy as jnp
import numpy as np
from jax import lax
from jax.experimental import pallas as pl
from jax.experimental.pallas import tpu as pltpu
from jax.sharding import PartitionSpec as P

CB_DEV = 2
HALF = jnp.float16
COT_SCALE = 256.0
VMEM = 56 * 1024 * 1024
AHEAD = 3


def ring_order(count):
    if count == 8:
        return [0, 2, 4, 6, 7, 5, 3, 1]
    return list(range(count))


def dense_blocks(kernel_tiles, tile_cols, tile_count):
    keep = kernel_tiles.shape[1]
    live = jnp.arange(keep, dtype=jnp.int32)[None, :] < tile_count
    hits = (tile_cols[:, :, None] == jnp.arange(CB_DEV, dtype=jnp.int32)) & live[:, :, None]
    blocks = jnp.einsum(
        "rkc,rkab->racb",
        hits.astype(jnp.bfloat16),
        kernel_tiles,
        preferred_element_type=jnp.float32,
    )
    rows, cols = blocks.shape[0] * blocks.shape[1], blocks.shape[2] * blocks.shape[3]
    return blocks.astype(jnp.bfloat16).reshape(rows, cols)


def nt(x, y):
    return lax.dot_general(x, y, (((1,), (1,)), ((), ())), preferred_element_type=jnp.float32)


def nn(x, y):
    return jnp.dot(x, y, preferred_element_type=jnp.float32)


class Shape:
    def __init__(self, count, rows, cols, hists, share):
        self.count = count
        self.rows = rows
        self.cols = cols
        self.hists = hists
        self.share = share
        self.lanes = rows + 2 * share
        self.opposite = count // 2
        self.units = []
        for d in range(count):
            if d == self.opposite:
                self.units += [(d, 0, rows // 2), (d, rows // 2, rows // 2)]
            else:
                self.units.append((d, 0, rows))


class Arrivals:
    def __init__(self, s, table, units, matrix, sems, paired):
        self.count, self.copies = s.count, {d: [] for d in range(s.count)}
        units = iter(units)
        for d, start, size in s.units:
            for t in range(2):
                target = matrix.at[d, pl.ds(start, size), pl.ds(t * s.cols, s.cols)]
                self.copies[d].append(pltpu.make_async_copy(next(units), target, sems.at[d]))
        for d in range(s.count):
            k = table[d]
            for source, target in paired:
                self.copies[d].append(
                    pltpu.make_async_copy(source.at[k], target.at[k], sems.at[d])
                )
        self.ahead = AHEAD if s.count <= 8 else s.count
        for d in range(min(self.ahead, s.count)):
            self.start(d)
        if s.count > 8:
            for d in range(s.count):
                self.wait(d)

    def start(self, d):
        for piece in self.copies[d]:
            piece.start()

    def wait(self, d):
        for piece in self.copies[d]:
            piece.wait()

    def __call__(self, d):
        if self.count <= 8:
            self.wait(d)
            if d + self.ahead < self.count:
                self.start(d + self.ahead)


def load(sources, targets, sems):
    copies = [
        pltpu.make_async_copy(source, target, sems.at[k])
        for k, (source, target) in enumerate(zip(sources, targets))
    ]
    for copy in copies:
        copy.start()
    return copies


def gather_targets(s, pieces):
    return jnp.concatenate(
        [
            pieces[i, :, s.rows + t * s.share : s.rows + (t + 1) * s.share]
            for t in range(2)
            for i in range(s.count)
        ],
        axis=1,
    )


def scatter_targets(s, out, values):
    for i in range(s.count):
        out[i, :, s.rows : s.lanes] = jnp.concatenate(
            [
                values[:, t * s.cols + i * s.share : t * s.cols + (i + 1) * s.share]
                for t in range(2)
            ],
            axis=1,
        )


def each(count, body, init):
    if count <= 8:
        for d in range(count):
            init = body(d, init)
        return init
    return lax.fori_loop(0, count, body, init)


def forward_kernel(s, table, mass_in, *refs):
    units, refs = refs[: 2 * len(s.units)], refs[2 * len(s.units) :]
    thirds, leaving, (mass, matrix, sems, more_sems), state = refs[0], refs[1:6], refs[6:10], refs[10:]
    row_two, row_one, col_one, col_two, col_three = state
    arrived = Arrivals(s, table, units, matrix, sems, [(mass_in, mass)])
    ones = jnp.ones((8, 2 * s.cols), jnp.bfloat16)
    zero = jnp.zeros((s.hists, 2 * s.cols), jnp.float32)

    def first(d, total):
        arrived(d)
        sums = nt(ones, matrix[d])
        row_one[d] = sums
        left = mass[table[d], :, : s.rows] / sums[0:1]
        return total + nn(left.astype(jnp.bfloat16), matrix[d])

    total = each(s.count, first, zero)
    col_one[...] = total
    target = gather_targets(s, mass)
    panel = (target / total).astype(jnp.bfloat16)

    def second(d, total):
        row = nt(panel, matrix[d])
        row_two[d] = row
        left = mass[table[d], :, : s.rows] / row
        return total + nn(left.astype(jnp.bfloat16), matrix[d])

    total = each(s.count, second, zero)
    col_two[...] = total
    started = load(state[:4], leaving[:4], more_sems)
    panel = (target / total).astype(jnp.bfloat16)

    def third(d, total):
        row = nt(panel, matrix[d])
        thirds[table[d], :, : s.rows] = row
        left = mass[table[d], :, : s.rows] / row
        return total + nn(left.astype(jnp.bfloat16), matrix[d])

    total = each(s.count, third, zero)
    col_three[...] = total
    last = pltpu.make_async_copy(col_three, leaving[4], more_sems.at[4])
    last.start()
    scatter_targets(s, thirds, total)
    for copy in [*started, last]:
        copy.wait()


def backward_kernel(s, table, mass_in, cot_in, thirds_in, *refs):
    state_in, units, refs = refs[:5], refs[5 : 5 + 2 * len(s.units)], refs[5 + 2 * len(s.units) :]
    out, (mass, matrix, sems, more_sems), state, (cot, thirds) = (
        refs[0],
        refs[1:5],
        refs[5:10],
        refs[10:],
    )
    row_two, row_one, col_one, col_two, col_three = state
    early = load([state_in[4], cot_in], [col_three, cot], more_sems)
    paired = [(mass_in, mass), (thirds_in, thirds)]
    arrived = Arrivals(s, table, units, matrix, sems, paired)
    late = [
        pltpu.make_async_copy(state_in[k], state[k], more_sems.at[2 + k]) for k in range(4)
    ]
    for copy in early:
        copy.wait()
    target_cot = gather_targets(s, cot)
    panel = (-target_cot / col_three[...]).astype(jnp.bfloat16)
    zero = jnp.zeros((s.hists, 2 * s.cols), jnp.float32)

    def third(d, total):
        arrived(d)
        if s.count <= 8 and d == s.count - AHEAD:
            for copy in late:
                copy.start()
        k = table[d]
        grad = nt(panel, matrix[d])
        row = thirds[k, :, : s.rows]
        left = mass[k, :, : s.rows] / row
        term = grad / row
        out[k, :, : s.rows] = term
        rowgrad = -(cot[k, :, : s.rows] / row + term * left)
        return total + nn(rowgrad.astype(jnp.bfloat16), matrix[d])

    total = each(s.count, third, zero)
    for copy in late:
        if s.count > 8:
            copy.start()
        copy.wait()
    target = gather_targets(s, mass)
    term_two = total / col_two[...]
    panel = (-term_two * (target / col_two[...])).astype(jnp.bfloat16)

    def second(d, total):
        k = table[d]
        row = row_two[d]
        term = nt(panel, matrix[d]) / row
        out[k, :, : s.rows] += term
        rowgrad = -term * (mass[k, :, : s.rows] / row)
        return total + nn(rowgrad.astype(jnp.bfloat16), matrix[d])

    term_one = each(s.count, second, zero) / col_one[...]
    panel = (-term_one * (target / col_one[...])).astype(jnp.bfloat16)

    def first(d, carry):
        out[table[d], :, : s.rows] += nt(panel, matrix[d]) / row_one[d, 0:1]
        return carry

    each(s.count, first, 0)
    scatter_targets(s, out, term_two + term_one)


def call(kernel, s, products, vmem_outs, hbm_outs, table, arrays, scratch):
    return pl.pallas_call(
        functools.partial(kernel, s),
        out_shape=[*vmem_outs, *hbm_outs],
        in_specs=[pl.BlockSpec(memory_space=pltpu.SMEM)]
        + [pl.BlockSpec(memory_space=pl.ANY)] * len(arrays),
        out_specs=[pl.BlockSpec(memory_space=pltpu.VMEM)] * len(vmem_outs)
        + [pl.BlockSpec(memory_space=pl.ANY)] * len(hbm_outs),
        scratch_shapes=[
            pltpu.VMEM((s.count, s.hists, s.lanes), jnp.float32),
            pltpu.VMEM((s.count, s.rows, 2 * s.cols), jnp.bfloat16),
            pltpu.SemaphoreType.DMA((s.count,)),
            pltpu.SemaphoreType.DMA((8,)),
            *[pltpu.VMEM(state.shape, state.dtype) for state in scratch],
        ],
        cost_estimate=pl.CostEstimate(
            flops=products * 2 * s.count * s.rows * 2 * s.cols * 256,
            bytes_accessed=s.count * s.rows * 2 * s.cols * 4,
            transcendentals=0,
        ),
        compiler_params=pltpu.CompilerParams(vmem_limit_bytes=VMEM),
    )(table, *arrays)


def swap_cores(x):
    return lax.ppermute(x, "tgt", [(0, 1), (1, 0)])


def local(
    source_mass,
    target_mass,
    kernel_tiles,
    tile_cols,
    tile_count,
    source_cotangent,
    target_cotangent,
):
    count = lax.axis_size("src")
    rows, cols_here = source_mass.shape
    share = target_mass.shape[1]
    s = Shape(count, rows, CB_DEV * kernel_tiles.shape[2], cols_here // count, share)
    ring = np.array(ring_order(count), np.int32)
    place = np.argsort(ring).astype(np.int32)
    me = lax.axis_index("src")
    core = lax.axis_index("tgt")
    at = jnp.asarray(place)[me]
    table = jnp.asarray(ring)[(at + jnp.arange(count, dtype=jnp.int32)) % count]

    def shift(x, distance):
        pairs = [(int(ring[p]), int(ring[(p + distance) % count])) for p in range(count)]
        return lax.ppermute(x, "src", pairs)

    def exchange(x):
        return lax.all_to_all(x, "src", 0, 0, tiled=True)

    def by_histogram(source, target):
        target = target.astype(HALF).reshape(share, 2, cols_here)
        mine = lax.dynamic_index_in_dim(target, core, 1, keepdims=False)
        other = lax.dynamic_index_in_dim(target, 1 - core, 1, keepdims=False)
        both = jnp.concatenate([mine, swap_cores(other)]).T
        return jnp.concatenate(
            [
                source.astype(HALF).T.reshape(count, s.hists, rows),
                both.reshape(count, s.hists, 2 * share),
            ],
            axis=2,
        )

    unit = dense_blocks(kernel_tiles, tile_cols, tile_count)

    pieces, before = {(0, 0): unit}, {0: [(0, 0)]}
    swapped = {(0, 0): swap_cores(unit)}
    ahead = behind = unit
    last = count // 2
    mass_message = by_histogram(source_mass, target_mass[0])
    cot_message = by_histogram(source_cotangent * COT_SCALE, target_cotangent[0] * COT_SCALE)
    for step in range(1, last + 1):
        due = before.get(step - 2, [])
        ready = [swapped[key] for key in due]
        if step == 2:
            ahead, behind, ready, mass_message, table = lax.optimization_barrier(
                (ahead, behind, ready, mass_message, table)
            )
        elif step == last:
            mass = exchange(mass_message).astype(jnp.float32)
            ahead, behind, ready, mass, cot_message = lax.optimization_barrier(
                (ahead, behind, ready, mass, cot_message)
            )
        else:
            ahead, behind, ready = lax.optimization_barrier((ahead, behind, ready))
        swapped.update(zip(due, ready))
        if 2 * step == count:
            middle = rows // 2
            new = {
                (step, 0): shift(ahead[:middle], -1),
                (step, middle): shift(behind[middle:], 1),
            }
        else:
            ahead, behind = shift(ahead, -1), shift(behind, 1)
            new = {(step, 0): ahead, (count - step, 0): behind}
        pieces.update(new)
        swapped.update({key: swap_cores(piece) for key, piece in new.items()})
        before[step] = list(new)
    units = []
    for d, start, _ in s.units:
        units += [pieces[d, start], swapped[d, start]]

    wide = jax.ShapeDtypeStruct((count, s.hists, s.lanes), jnp.float32)
    panel = jax.ShapeDtypeStruct((count, s.hists, rows), jnp.float32)
    sums = jax.ShapeDtypeStruct((count, 8, rows), jnp.float32)
    column = jax.ShapeDtypeStruct((s.hists, 2 * s.cols), jnp.float32)
    states = [panel, sums, column, column, column]
    cot = exchange(cot_message).astype(jnp.float32)
    thirds, *state = call(
        forward_kernel, s, 7, [wide], states, table, [mass, *units], states
    )
    (grads,) = call(
        backward_kernel,
        s,
        5,
        [wide],
        [],
        table,
        [mass, cot, thirds, *state, *units],
        [*states, wide, wide],
    )

    def by_point(pieces):
        flat = pieces.reshape(cols_here, s.lanes).astype(jnp.float32)
        target = flat[:, rows:].T.reshape(2, share, cols_here)
        other = swap_cores(target[1].astype(HALF)).astype(jnp.float32)
        own = target[0]
        halves = [jnp.where(core == t, own, other) for t in range(2)]
        return flat[:, :rows].T, jnp.concatenate(halves, axis=1)

    row_three, col_three = by_point(exchange(thirds.astype(HALF)))
    source_potential = jnp.log(source_mass / row_three)
    target_potential = jnp.log(target_mass[0] / col_three)
    source_known = source_cotangent / source_mass
    target_known = target_cotangent[0] / target_mass[0]
    back, source_potential, target_potential, source_known, target_known = lax.optimization_barrier(
        (
            exchange(grads.astype(HALF)),
            source_potential,
            target_potential,
            source_known,
            target_known,
        )
    )
    source_term, target_term = by_point(back)
    return (
        source_potential,
        target_potential[None],
        source_known + source_term * (1 / COT_SCALE),
        (target_known + target_term * (1 / COT_SCALE))[None],
    )


def solution(mesh):
    return jax.shard_map(
        local,
        mesh=mesh,
        in_specs=(
            P(("grp", "src"), "tgt"),
            P("tgt", ("grp", "src"), None),
            P(("grp", "src"), "tgt", None, None),
            P(("grp", "src"), "tgt"),
            P(("grp", "src"), "tgt"),
            P(("grp", "src"), "tgt"),
            P("tgt", ("grp", "src"), None),
        ),
        out_specs=(
            P(("grp", "src"), "tgt"),
            P("tgt", ("grp", "src"), None),
            P(("grp", "src"), "tgt"),
            P("tgt", ("grp", "src"), None),
        ),
        check_vma=False,
    )
```

```python
import functools

import jax
import jax.numpy as jnp
import numpy as np
from jax import lax
from jax.experimental import pallas as pl
from jax.experimental.pallas import tpu as pltpu
from jax.sharding import PartitionSpec as P

CB_DEV = 2
HALF = jnp.float16
COT_SCALE = 256.0
VMEM = 56 * 1024 * 1024
AHEAD = 3


def ring_order(count):
    if count == 8:
        return [0, 2, 4, 6, 7, 5, 3, 1]
    return list(range(count))


def dense_blocks(kernel_tiles, tile_cols, tile_count):
    keep = kernel_tiles.shape[1]
    live = jnp.arange(keep, dtype=jnp.int32)[None, :] < tile_count
    hits = (tile_cols[:, :, None] == jnp.arange(CB_DEV, dtype=jnp.int32)) & live[:, :, None]
    blocks = jnp.einsum(
        "rkc,rkab->racb",
        hits.astype(jnp.bfloat16),
        kernel_tiles,
        preferred_element_type=jnp.float32,
    )
    rows, cols = blocks.shape[0] * blocks.shape[1], blocks.shape[2] * blocks.shape[3]
    return blocks.astype(jnp.bfloat16).reshape(rows, cols)


def nt(x, y):
    return lax.dot_general(x, y, (((1,), (1,)), ((), ())), preferred_element_type=jnp.float32)


def nn(x, y):
    return jnp.dot(x, y, preferred_element_type=jnp.float32)


class Shape:
    def __init__(self, count, rows, cols, hists, share):
        self.count = count
        self.rows = rows
        self.cols = cols
        self.hists = hists
        self.share = share
        self.lanes = rows + 2 * share
        self.opposite = count // 2


class Arrivals:
    def __init__(self, s, table, units, matrix, sems, paired):
        self.count = s.count
        self.copies = {
            d: [pltpu.make_async_copy(units[d], matrix.at[d], sems.at[d])]
            for d in range(s.count - 1)
        }
        half, d = s.rows // 2, s.count - 1
        self.copies[d] = []
        for unit, side in zip(units[d:], (table[s.count], 1 - table[s.count])):
            target = matrix.at[d, pl.ds(pl.multiple_of(side * half, half), half)]
            self.copies[d].append(pltpu.make_async_copy(unit, target, sems.at[d]))
        for d in range(s.count):
            k = table[d]
            for source, target in paired:
                self.copies[d].append(
                    pltpu.make_async_copy(source.at[k], target.at[k], sems.at[d])
                )
        self.ahead = AHEAD if s.count <= 8 else s.count
        for d in range(min(self.ahead, s.count)):
            self.start(d)
        if s.count > 8:
            for d in range(s.count):
                self.wait(d)

    def start(self, d):
        for piece in self.copies[d]:
            piece.start()

    def wait(self, d):
        for piece in self.copies[d]:
            piece.wait()

    def __call__(self, d):
        if self.count <= 8:
            self.wait(d)
            if d + self.ahead < self.count:
                self.start(d + self.ahead)


def load(sources, targets, sems):
    copies = [
        pltpu.make_async_copy(source, target, sems.at[k])
        for k, (source, target) in enumerate(zip(sources, targets))
    ]
    for copy in copies:
        copy.start()
    return copies


def gather_targets(s, pieces):
    return jnp.concatenate(
        [
            pieces[i, :, s.rows + t * s.share : s.rows + (t + 1) * s.share]
            for t in range(2)
            for i in range(s.count)
        ],
        axis=1,
    )


def scatter_targets(s, out, values):
    for i in range(s.count):
        out[i, :, s.rows : s.lanes] = jnp.concatenate(
            [
                values[:, t * s.cols + i * s.share : t * s.cols + (i + 1) * s.share]
                for t in range(2)
            ],
            axis=1,
        )


def chain(count, product, use, total):
    if count > 8:
        return lax.fori_loop(0, count, lambda d, t: use(d, product(d), t), total)
    ready = product(0)
    for d in range(count):
        later = product(d + 1) if d + 1 < count else None
        total = use(d, ready, total)
        ready = later
    return total


def forward_kernel(s, table, mass_in, *refs):
    units, refs = refs[: s.count + 1], refs[s.count + 1 :]
    thirds, leaving, (mass, matrix, sems, more_sems), state = refs[0], refs[1:6], refs[6:10], refs[10:]
    row_two, row_one, col_one, col_two, col_three = state
    arrived = Arrivals(s, table, units, matrix, sems, [(mass_in, mass)])
    ones = jnp.ones((8, 2 * s.cols), jnp.bfloat16)
    zero = jnp.zeros((s.hists, 2 * s.cols), jnp.float32)

    def sums(d):
        arrived(d)
        return nt(ones, matrix[d])

    def first(d, row, total):
        row_one[d] = row
        left = mass[table[d], :, : s.rows] / row[0:1]
        return total + nn(left.astype(jnp.bfloat16), matrix[d])

    total = chain(s.count, sums, first, zero)
    col_one[...] = total
    target = gather_targets(s, mass)
    panel = (target / total).astype(jnp.bfloat16)

    def second(d, row, total):
        row_two[d] = row
        left = mass[table[d], :, : s.rows] / row
        return total + nn(left.astype(jnp.bfloat16), matrix[d])

    total = chain(s.count, lambda d: nt(panel, matrix[d]), second, zero)
    col_two[...] = total
    started = load(state[:4], leaving[:4], more_sems)
    last_panel = (target / total).astype(jnp.bfloat16)

    def third(d, row, total):
        thirds[table[d], :, : s.rows] = row
        left = mass[table[d], :, : s.rows] / row
        return total + nn(left.astype(jnp.bfloat16), matrix[d])

    total = chain(s.count, lambda d: nt(last_panel, matrix[d]), third, zero)
    col_three[...] = total
    last = pltpu.make_async_copy(col_three, leaving[4], more_sems.at[4])
    last.start()
    scatter_targets(s, thirds, total)
    for copy in [*started, last]:
        copy.wait()


def backward_kernel(s, table, mass_in, cot_in, thirds_in, *refs):
    state_in, units, refs = refs[:5], refs[5 : 6 + s.count], refs[6 + s.count :]
    out, (mass, matrix, sems, more_sems), state, (cot, thirds) = (
        refs[0],
        refs[1:5],
        refs[5:10],
        refs[10:],
    )
    row_two, row_one, col_one, col_two, col_three = state
    early = load([state_in[4], cot_in], [col_three, cot], more_sems)
    paired = [(mass_in, mass), (thirds_in, thirds)]
    arrived = Arrivals(s, table, units, matrix, sems, paired)
    late = [
        pltpu.make_async_copy(state_in[k], state[k], more_sems.at[2 + k]) for k in range(4)
    ]
    for copy in early:
        copy.wait()
    target_cot = gather_targets(s, cot)
    panel = (-target_cot / col_three[...]).astype(jnp.bfloat16)
    zero = jnp.zeros((s.hists, 2 * s.cols), jnp.float32)

    def first_product(d):
        arrived(d)
        if s.count <= 8 and d == s.count - AHEAD:
            for copy in late:
                copy.start()
        return nt(panel, matrix[d])

    def third(d, grad, total):
        k = table[d]
        row = thirds[k, :, : s.rows]
        left = mass[k, :, : s.rows] / row
        term = grad / row
        out[k, :, : s.rows] = term
        rowgrad = -(cot[k, :, : s.rows] / row + term * left)
        return total + nn(rowgrad.astype(jnp.bfloat16), matrix[d])

    total = chain(s.count, first_product, third, zero)
    for copy in late:
        if s.count > 8:
            copy.start()
        copy.wait()
    target = gather_targets(s, mass)
    term_two = total / col_two[...]
    panel_two = (-term_two * (target / col_two[...])).astype(jnp.bfloat16)

    def second(d, grad, total):
        k = table[d]
        row = row_two[d]
        term = grad / row
        out[k, :, : s.rows] += term
        rowgrad = -term * (mass[k, :, : s.rows] / row)
        return total + nn(rowgrad.astype(jnp.bfloat16), matrix[d])

    total = chain(s.count, lambda d: nt(panel_two, matrix[d]), second, zero)
    term_one = total / col_one[...]
    panel_one = (-term_one * (target / col_one[...])).astype(jnp.bfloat16)

    def first(d, grad, carry):
        out[table[d], :, : s.rows] += grad / row_one[d, 0:1]
        return carry

    chain(s.count, lambda d: nt(panel_one, matrix[d]), first, 0)
    scatter_targets(s, out, term_two + term_one)


def call(kernel, s, products, vmem_outs, hbm_outs, table, arrays, scratch):
    return pl.pallas_call(
        functools.partial(kernel, s),
        out_shape=[*vmem_outs, *hbm_outs],
        in_specs=[pl.BlockSpec(memory_space=pltpu.SMEM)]
        + [pl.BlockSpec(memory_space=pl.ANY)] * len(arrays),
        out_specs=[pl.BlockSpec(memory_space=pltpu.VMEM)] * len(vmem_outs)
        + [pl.BlockSpec(memory_space=pl.ANY)] * len(hbm_outs),
        scratch_shapes=[
            pltpu.VMEM((s.count, s.hists, s.lanes), jnp.float32),
            pltpu.VMEM((s.count, s.rows, 2 * s.cols), jnp.bfloat16),
            pltpu.SemaphoreType.DMA((s.count,)),
            pltpu.SemaphoreType.DMA((8,)),
            *[pltpu.VMEM(state.shape, state.dtype) for state in scratch],
        ],
        cost_estimate=pl.CostEstimate(
            flops=products * 2 * s.count * s.rows * 2 * s.cols * 256,
            bytes_accessed=s.count * s.rows * 2 * s.cols * 4,
            transcendentals=0,
        ),
        compiler_params=pltpu.CompilerParams(vmem_limit_bytes=VMEM),
    )(table, *arrays)


def swap_cores(x):
    return lax.ppermute(x, "tgt", [(0, 1), (1, 0)])


def local(
    source_mass,
    target_mass,
    kernel_tiles,
    tile_cols,
    tile_count,
    source_cotangent,
    target_cotangent,
):
    count = lax.axis_size("src")
    rows, cols_here = source_mass.shape
    share = target_mass.shape[1]
    s = Shape(count, rows, CB_DEV * kernel_tiles.shape[2], cols_here // count, share)
    ring = np.array(ring_order(count), np.int32)
    place = np.argsort(ring).astype(np.int32)
    me = lax.axis_index("src")
    core = lax.axis_index("tgt")
    at = jnp.asarray(place)[me]
    last = count // 2
    away = 2 * core - 1
    steps = [0] + [sign * k for k in range(1, last) for sign in (1, -1)] + [last]
    slots = (at + away * jnp.asarray(steps, jnp.int32)) % count
    table = jnp.concatenate([jnp.asarray(ring)[slots], core[None]]).astype(jnp.int32)

    def onward(x):
        pairs = []
        for p in range(count):
            pairs.append((int(ring[p]) * 2, int(ring[(p + 1) % count]) * 2))
            pairs.append((int(ring[p]) * 2 + 1, int(ring[(p - 1) % count]) * 2 + 1))
        return lax.ppermute(x, ("src", "tgt"), pairs)

    def exchange(x):
        return lax.all_to_all(x, "src", 0, 0, tiled=True)

    def in_order(mine, other, axis):
        return jnp.concatenate(
            [jnp.where(core == 0, mine, other), jnp.where(core == 0, other, mine)], axis=axis
        )

    def by_histogram(source, target):
        target = target.astype(HALF).reshape(share, 2, cols_here)
        mine = lax.dynamic_index_in_dim(target, core, 1, keepdims=False)
        other = lax.dynamic_index_in_dim(target, 1 - core, 1, keepdims=False)
        both = in_order(mine, swap_cores(other), 0).T
        return jnp.concatenate(
            [
                source.astype(HALF).T.reshape(count, s.hists, rows),
                both.reshape(count, s.hists, 2 * share),
            ],
            axis=2,
        )

    mine = dense_blocks(kernel_tiles, tile_cols, tile_count)
    unit = in_order(mine, swap_cores(mine), 1)
    mass_message = by_histogram(source_mass, target_mass[0])
    cot_message = by_histogram(source_cotangent * COT_SCALE, target_cotangent[0] * COT_SCALE)
    units = [unit]
    for step in range(1, last + 1):
        if step == 2:
            unit, table = lax.optimization_barrier((unit, table))
            units[-1], mass_message = lax.optimization_barrier((units[-1], mass_message))
        elif step == last:
            mass = exchange(mass_message).astype(jnp.float32)
            unit, units[-3], mass, cot_message = lax.optimization_barrier(
                (unit, units[-3], mass, cot_message)
            )
        elif step > 2:
            unit, units[-3] = lax.optimization_barrier((unit, units[-3]))
        if step == last:
            unit = lax.dynamic_slice_in_dim(unit, core * (rows // 2), rows // 2, 0)
        unit = onward(unit)
        units += [unit, swap_cores(unit)]
    cot = exchange(cot_message).astype(jnp.float32)

    wide = jax.ShapeDtypeStruct((count, s.hists, s.lanes), jnp.float32)
    panel = jax.ShapeDtypeStruct((count, s.hists, rows), jnp.float32)
    sums = jax.ShapeDtypeStruct((count, 8, rows), jnp.float32)
    column = jax.ShapeDtypeStruct((s.hists, 2 * s.cols), jnp.float32)
    states = [panel, sums, column, column, column]
    thirds, *state = call(
        forward_kernel, s, 7, [wide], states, table, [mass, *units], states
    )
    (grads,) = call(
        backward_kernel,
        s,
        5,
        [wide],
        [],
        table,
        [mass, cot, thirds, *state, *units],
        [*states, wide, wide],
    )

    def by_point(pieces):
        flat = pieces.reshape(cols_here, s.lanes).astype(jnp.float32)
        target = flat[:, rows:].T.reshape(2, share, cols_here)
        own = lax.dynamic_index_in_dim(target, core, 0, keepdims=False)
        other = lax.dynamic_index_in_dim(target, 1 - core, 0, keepdims=False)
        other = swap_cores(other.astype(HALF)).astype(jnp.float32)
        return flat[:, :rows].T, in_order(own, other, 1)

    row_three, col_three = by_point(exchange(thirds.astype(HALF)))
    source_potential = jnp.log(source_mass / row_three)
    target_potential = jnp.log(target_mass[0] / col_three)
    source_known = source_cotangent / source_mass
    target_known = target_cotangent[0] / target_mass[0]
    back, source_potential, target_potential, source_known, target_known = lax.optimization_barrier(
        (
            exchange(grads.astype(HALF)),
            source_potential,
            target_potential,
            source_known,
            target_known,
        )
    )
    source_term, target_term = by_point(back)
    return (
        source_potential,
        target_potential[None],
        source_known + source_term * (1 / COT_SCALE),
        (target_known + target_term * (1 / COT_SCALE))[None],
    )


def solution(mesh):
    return jax.shard_map(
        local,
        mesh=mesh,
        in_specs=(
            P(("grp", "src"), "tgt"),
            P("tgt", ("grp", "src"), None),
            P(("grp", "src"), "tgt", None, None),
            P(("grp", "src"), "tgt"),
            P(("grp", "src"), "tgt"),
            P(("grp", "src"), "tgt"),
            P("tgt", ("grp", "src"), None),
        ),
        out_specs=(
            P(("grp", "src"), "tgt"),
            P("tgt", ("grp", "src"), None),
            P(("grp", "src"), "tgt"),
            P("tgt", ("grp", "src"), None),
        ),
        check_vma=False,
    )
```

```python
import functools

import jax
import jax.numpy as jnp
import numpy as np
from jax import lax
from jax.experimental import pallas as pl
from jax.experimental.pallas import tpu as pltpu
from jax.sharding import PartitionSpec as P

CB_DEV = 2
HALF = jnp.float16
COT_SCALE = 256.0
VMEM = 56 * 1024 * 1024
AHEAD = 3


def ring_order(count):
    if count == 8:
        return [0, 2, 4, 6, 7, 5, 3, 1]
    return list(range(count))


def dense_kernel(cols, live, tiles, out):
    keep = tiles.shape[1]
    for r in range(tiles.shape[0]):
        for c in range(CB_DEV):
            block = jnp.zeros(tiles.shape[2:], jnp.float32)
            for k in range(keep):
                hit = jnp.logical_and(cols[r, k] == c, k < live[r, 0])
                block += jnp.where(hit, 1.0, 0.0) * tiles[r, k].astype(jnp.float32)
            side = tiles.shape[2]
            out[r * side : (r + 1) * side, c * side : (c + 1) * side] = block.astype(jnp.bfloat16)


def dense_blocks(kernel_tiles, tile_cols, tile_count):
    blocks, _, side, _ = kernel_tiles.shape
    return pl.pallas_call(
        dense_kernel,
        out_shape=jax.ShapeDtypeStruct((blocks * side, CB_DEV * side), jnp.bfloat16),
        in_specs=[pl.BlockSpec(memory_space=pltpu.SMEM)] * 2
        + [pl.BlockSpec(memory_space=pltpu.VMEM)],
        out_specs=pl.BlockSpec(memory_space=pltpu.VMEM),
    )(tile_cols, tile_count, kernel_tiles)


def nt(x, y):
    return lax.dot_general(x, y, (((1,), (1,)), ((), ())), preferred_element_type=jnp.float32)


def nn(x, y):
    return jnp.dot(x, y, preferred_element_type=jnp.float32)


class Shape:
    def __init__(self, count, rows, cols, hists, share):
        self.count = count
        self.rows = rows
        self.cols = cols
        self.hists = hists
        self.share = share
        self.lanes = rows + 2 * share
        self.halves = 2 if count <= 8 else 1


class Arrivals:
    def __init__(self, s, table, units, matrix, sems, paired):
        self.count = s.count
        self.copies = {d: [] for d in range(s.count)}
        units = iter(units)
        for d in range(s.count - 1):
            parts = s.halves if d else 1
            for part in range(parts):
                size = s.rows // parts
                target = matrix.at[d, pl.ds(part * size, size)]
                self.copies[d].append(pltpu.make_async_copy(next(units), target, sems.at[d]))
        half, d = s.rows // 2, s.count - 1
        for side in (table[s.count], 1 - table[s.count]):
            target = matrix.at[d, pl.ds(pl.multiple_of(side * half, half), half)]
            self.copies[d].append(pltpu.make_async_copy(next(units), target, sems.at[d]))
        for d in range(s.count):
            k = table[d]
            for source, target in paired:
                self.copies[d].append(
                    pltpu.make_async_copy(source.at[k], target.at[k], sems.at[d])
                )
        self.ahead = AHEAD if s.count <= 8 else s.count
        for d in range(min(self.ahead, s.count)):
            self.start(d)
        if s.count > 8:
            for d in range(s.count):
                self.wait(d)

    def start(self, d):
        for piece in self.copies[d]:
            piece.start()

    def wait(self, d):
        for piece in self.copies[d]:
            piece.wait()

    def __call__(self, d):
        if self.count <= 8:
            self.wait(d)
            if d + self.ahead < self.count:
                self.start(d + self.ahead)


def load(sources, targets, sems):
    copies = [
        pltpu.make_async_copy(source, target, sems.at[k])
        for k, (source, target) in enumerate(zip(sources, targets))
    ]
    for copy in copies:
        copy.start()
    return copies


def gather_targets(s, pieces):
    return jnp.concatenate(
        [
            pieces[i, :, s.rows + t * s.share : s.rows + (t + 1) * s.share]
            for t in range(2)
            for i in range(s.count)
        ],
        axis=1,
    )


def scatter_targets(s, out, values):
    for i in range(s.count):
        out[i, :, s.rows : s.lanes] = jnp.concatenate(
            [
                values[:, t * s.cols + i * s.share : t * s.cols + (i + 1) * s.share]
                for t in range(2)
            ],
            axis=1,
        )


def chain(count, product, use, total):
    if count > 8:
        return lax.fori_loop(0, count, lambda d, t: use(d, product(d), t), total)
    ready = product(0)
    for d in range(count):
        later = product(d + 1) if d + 1 < count else None
        total = use(d, ready, total)
        ready = later
    return total


def forward_kernel(s, table, mass_in, *refs):
    given = 3 + (s.count - 2) * s.halves
    units, refs = refs[:given], refs[given:]
    thirds, leaving, (mass, matrix, sems, more_sems), state = refs[0], refs[1:6], refs[6:10], refs[10:]
    row_two, row_one, col_one, col_two, col_three = state
    arrived = Arrivals(s, table, units, matrix, sems, [(mass_in, mass)])
    ones = jnp.ones((8, 2 * s.cols), jnp.bfloat16)
    zero = jnp.zeros((s.hists, 2 * s.cols), jnp.float32)

    def sums(d):
        arrived(d)
        return nt(ones, matrix[d])

    def first(d, row, total):
        row_one[d] = row
        left = mass[table[d], :, : s.rows] / row[0:1]
        return total + nn(left.astype(jnp.bfloat16), matrix[d])

    total = chain(s.count, sums, first, zero)
    col_one[...] = total
    target = gather_targets(s, mass)
    panel = (target / total).astype(jnp.bfloat16)

    def second(d, row, total):
        row_two[d] = row
        left = mass[table[d], :, : s.rows] / row
        return total + nn(left.astype(jnp.bfloat16), matrix[d])

    total = chain(s.count, lambda d: nt(panel, matrix[d]), second, zero)
    col_two[...] = total
    started = load(state[:4], leaving[:4], more_sems)
    last_panel = (target / total).astype(jnp.bfloat16)

    def third(d, row, total):
        thirds[table[d], :, : s.rows] = row
        left = mass[table[d], :, : s.rows] / row
        return total + nn(left.astype(jnp.bfloat16), matrix[d])

    total = chain(s.count, lambda d: nt(last_panel, matrix[d]), third, zero)
    col_three[...] = total
    last = pltpu.make_async_copy(col_three, leaving[4], more_sems.at[4])
    last.start()
    scatter_targets(s, thirds, total)
    for copy in [*started, last]:
        copy.wait()


def backward_kernel(s, table, mass_in, cot_in, thirds_in, *refs):
    given = 3 + (s.count - 2) * s.halves
    state_in, units, refs = refs[:5], refs[5 : 5 + given], refs[5 + given :]
    out, (mass, matrix, sems, more_sems), state, (cot, thirds) = (
        refs[0],
        refs[1:5],
        refs[5:10],
        refs[10:],
    )
    row_two, row_one, col_one, col_two, col_three = state
    early = load([state_in[4], cot_in], [col_three, cot], more_sems)
    paired = [(mass_in, mass), (thirds_in, thirds)]
    arrived = Arrivals(s, table, units, matrix, sems, paired)
    late = [
        pltpu.make_async_copy(state_in[k], state[k], more_sems.at[2 + k]) for k in range(4)
    ]
    for copy in early:
        copy.wait()
    target_cot = gather_targets(s, cot)
    panel = (-target_cot / col_three[...]).astype(jnp.bfloat16)
    zero = jnp.zeros((s.hists, 2 * s.cols), jnp.float32)

    def first_product(d):
        arrived(d)
        if s.count <= 8 and d == s.count - AHEAD:
            for copy in late:
                copy.start()
        return nt(panel, matrix[d])

    def third(d, grad, total):
        k = table[d]
        row = thirds[k, :, : s.rows]
        left = mass[k, :, : s.rows] / row
        term = grad / row
        out[k, :, : s.rows] = term
        rowgrad = -(cot[k, :, : s.rows] / row + term * left)
        return total + nn(rowgrad.astype(jnp.bfloat16), matrix[d])

    total = chain(s.count, first_product, third, zero)
    for copy in late:
        if s.count > 8:
            copy.start()
        copy.wait()
    target = gather_targets(s, mass)
    term_two = total / col_two[...]
    panel_two = (-term_two * (target / col_two[...])).astype(jnp.bfloat16)

    def second(d, grad, total):
        k = table[d]
        row = row_two[d]
        term = grad / row
        out[k, :, : s.rows] += term
        rowgrad = -term * (mass[k, :, : s.rows] / row)
        return total + nn(rowgrad.astype(jnp.bfloat16), matrix[d])

    total = chain(s.count, lambda d: nt(panel_two, matrix[d]), second, zero)
    term_one = total / col_one[...]
    panel_one = (-term_one * (target / col_one[...])).astype(jnp.bfloat16)

    def first(d, grad, carry):
        out[table[d], :, : s.rows] += grad / row_one[d, 0:1]
        return carry

    chain(s.count, lambda d: nt(panel_one, matrix[d]), first, 0)
    scatter_targets(s, out, term_two + term_one)


def call(kernel, s, products, vmem_outs, hbm_outs, table, arrays, scratch):
    return pl.pallas_call(
        functools.partial(kernel, s),
        out_shape=[*vmem_outs, *hbm_outs],
        in_specs=[pl.BlockSpec(memory_space=pltpu.SMEM)]
        + [pl.BlockSpec(memory_space=pl.ANY)] * len(arrays),
        out_specs=[pl.BlockSpec(memory_space=pltpu.VMEM)] * len(vmem_outs)
        + [pl.BlockSpec(memory_space=pl.ANY)] * len(hbm_outs),
        scratch_shapes=[
            pltpu.VMEM((s.count, s.hists, s.lanes), jnp.float32),
            pltpu.VMEM((s.count, s.rows, 2 * s.cols), jnp.bfloat16),
            pltpu.SemaphoreType.DMA((s.count,)),
            pltpu.SemaphoreType.DMA((8,)),
            *[pltpu.VMEM(state.shape, state.dtype) for state in scratch],
        ],
        cost_estimate=pl.CostEstimate(
            flops=products * 2 * s.count * s.rows * 2 * s.cols * s.hists,
            bytes_accessed=s.count * s.rows * 2 * s.cols * 4,
            transcendentals=0,
        ),
        compiler_params=pltpu.CompilerParams(vmem_limit_bytes=VMEM),
    )(table, *arrays)


def swap_cores(x):
    return lax.ppermute(x, "tgt", [(0, 1), (1, 0)])


def local(
    source_mass,
    target_mass,
    kernel_tiles,
    tile_cols,
    tile_count,
    source_cotangent,
    target_cotangent,
):
    count = lax.axis_size("src")
    rows, cols_here = source_mass.shape
    share = target_mass.shape[1]
    s = Shape(count, rows, CB_DEV * kernel_tiles.shape[2], cols_here // count, share)
    ring = np.array(ring_order(count), np.int32)
    place = np.argsort(ring).astype(np.int32)
    me = lax.axis_index("src")
    core = lax.axis_index("tgt")
    at = jnp.asarray(place)[me]
    last = count // 2
    away = 2 * core - 1
    steps = [0] + [sign * k for k in range(1, last) for sign in (1, -1)] + [last]
    slots = (at + away * jnp.asarray(steps, jnp.int32)) % count
    table = jnp.concatenate([jnp.asarray(ring)[slots], core[None]]).astype(jnp.int32)

    def onward(x):
        pairs = []
        for p in range(count):
            pairs.append((int(ring[p]) * 2, int(ring[(p + 1) % count]) * 2))
            pairs.append((int(ring[p]) * 2 + 1, int(ring[(p - 1) % count]) * 2 + 1))
        return lax.ppermute(x, ("src", "tgt"), pairs)

    def exchange(x):
        return lax.all_to_all(x, "src", 0, 0, tiled=True)

    def in_order(mine, other, axis):
        return jnp.concatenate(
            [jnp.where(core == 0, mine, other), jnp.where(core == 0, other, mine)], axis=axis
        )

    def by_histogram(source, target):
        target = target.astype(HALF).reshape(share, 2, cols_here)
        mine = lax.dynamic_index_in_dim(target, core, 1, keepdims=False)
        other = lax.dynamic_index_in_dim(target, 1 - core, 1, keepdims=False)
        both = in_order(mine, swap_cores(other), 0).T
        return jnp.concatenate(
            [
                source.astype(HALF).T.reshape(count, s.hists, rows),
                both.reshape(count, s.hists, 2 * share),
            ],
            axis=2,
        )

    mine = dense_blocks(kernel_tiles, tile_cols, tile_count)
    unit = in_order(mine, swap_cores(mine), 1)
    mass_message = by_histogram(source_mass, target_mass[0])
    cot_message = by_histogram(source_cotangent * COT_SCALE, target_cotangent[0] * COT_SCALE)
    half = rows // s.halves
    heads = [unit[k * half : (k + 1) * half] for k in range(s.halves)]
    came, swapped = {}, {}
    for step in range(1, last):
        for k in range(s.halves):
            if step > 2:
                heads[k], swapped[step - 2, k] = lax.optimization_barrier(
                    (heads[k], swapped[step - 2, k])
                )
            if step == 2 and k == 0:
                heads[k], table = lax.optimization_barrier((heads[k], table))
            came[step, k] = heads[k] = onward(heads[k])
            leaving = heads[k]
            if step == last - 1 and k == 0:
                mass_here = exchange(mass_message)
                mass = mass_here.astype(jnp.float32)
                leaving, mass = lax.optimization_barrier((leaving, mass))
            swapped[step, k] = swap_cores(leaving)
            if step == 1 and k == 0:
                swapped[step, k], mass_message = lax.optimization_barrier(
                    (swapped[step, k], mass_message)
                )
    if s.halves == 1:
        piece = lax.dynamic_slice_in_dim(heads[0], core * (rows // 2), rows // 2, 0)
    else:
        piece = jnp.where(core == 0, heads[0], heads[1])
    due = [swapped[last - 2, k] for k in range(s.halves)]
    piece, due, cot_message, mass_here = lax.optimization_barrier(
        (piece, due, cot_message, mass_here)
    )
    swapped.update({(last - 2, k): due[k] for k in range(s.halves)})
    piece = onward(piece)
    units = [unit]
    for step in range(1, last):
        for part in (came, swapped):
            units += [part[step, k] for k in range(s.halves)]
    units += [piece, swap_cores(piece)]
    cot = exchange(cot_message).astype(jnp.float32)

    wide = jax.ShapeDtypeStruct((count, s.hists, s.lanes), jnp.float32)
    panel = jax.ShapeDtypeStruct((count, s.hists, rows), jnp.float32)
    sums = jax.ShapeDtypeStruct((count, 8, rows), jnp.float32)
    column = jax.ShapeDtypeStruct((s.hists, 2 * s.cols), jnp.float32)
    states = [panel, sums, column, column, column]
    thirds, *state = call(
        forward_kernel, s, 7, [wide], states, table, [mass, *units], states
    )
    (grads,) = call(
        backward_kernel,
        s,
        20,
        [wide],
        [],
        table,
        [mass, cot, thirds, *state, *units],
        [*states, wide, wide],
    )

    def by_point(pieces):
        flat = pieces.reshape(cols_here, s.lanes).astype(jnp.float32)
        target = flat[:, rows:].T.reshape(2, share, cols_here)
        own = lax.dynamic_index_in_dim(target, core, 0, keepdims=False)
        other = lax.dynamic_index_in_dim(target, 1 - core, 0, keepdims=False)
        other = swap_cores(other.astype(HALF)).astype(jnp.float32)
        return flat[:, :rows].T, in_order(own, other, 1)

    row_three, col_three = by_point(exchange(thirds.astype(HALF)))
    source_potential = jnp.log(source_mass / row_three)
    target_potential = jnp.log(target_mass[0] / col_three)
    source_known = source_cotangent / source_mass
    target_known = target_cotangent[0] / target_mass[0]
    back, source_potential, target_potential, source_known, target_known = lax.optimization_barrier(
        (
            exchange(grads.astype(HALF)),
            source_potential,
            target_potential,
            source_known,
            target_known,
        )
    )
    source_term, target_term = by_point(back)
    return (
        source_potential,
        target_potential[None],
        source_known + source_term * (1 / COT_SCALE),
        (target_known + target_term * (1 / COT_SCALE))[None],
    )


def solution(mesh):
    return jax.shard_map(
        local,
        mesh=mesh,
        in_specs=(
            P(("grp", "src"), "tgt"),
            P("tgt", ("grp", "src"), None),
            P(("grp", "src"), "tgt", None, None),
            P(("grp", "src"), "tgt"),
            P(("grp", "src"), "tgt"),
            P(("grp", "src"), "tgt"),
            P("tgt", ("grp", "src"), None),
        ),
        out_specs=(
            P(("grp", "src"), "tgt"),
            P("tgt", ("grp", "src"), None),
            P(("grp", "src"), "tgt"),
            P("tgt", ("grp", "src"), None),
        ),
        check_vma=False,
    )
```

```python
import functools

import jax
import jax.numpy as jnp
import numpy as np
from jax import lax
from jax.experimental import pallas as pl
from jax.experimental.pallas import tpu as pltpu
from jax.sharding import PartitionSpec as P

CB_DEV = 2
HALF = jnp.float16
COT_SCALE = 256.0
VMEM = 56 * 1024 * 1024
AHEAD = 3


def ring_order(count):
    if count == 8:
        return [0, 2, 4, 6, 7, 5, 3, 1]
    return list(range(count))


def dense_blocks(kernel_tiles, tile_cols, tile_count):
    keep = kernel_tiles.shape[1]
    live = jnp.arange(keep, dtype=jnp.int32)[None, :] < tile_count
    hits = (tile_cols[:, :, None] == jnp.arange(CB_DEV, dtype=jnp.int32)) & live[:, :, None]
    blocks = jnp.einsum(
        "rkc,rkab->racb",
        hits.astype(jnp.bfloat16),
        kernel_tiles,
        preferred_element_type=jnp.float32,
    )
    rows, cols = blocks.shape[0] * blocks.shape[1], blocks.shape[2] * blocks.shape[3]
    return blocks.astype(jnp.bfloat16).reshape(rows, cols)


def nt(x, y):
    return lax.dot_general(x, y, (((1,), (1,)), ((), ())), preferred_element_type=jnp.float32)


def nn(x, y):
    return jnp.dot(x, y, preferred_element_type=jnp.float32)


class Shape:
    def __init__(self, count, rows, cols, hists, share):
        self.count = count
        self.rows = rows
        self.cols = cols
        self.hists = hists
        self.share = share
        self.lanes = rows + 2 * share
        self.halves = 2 if count <= 8 else 1


class Arrivals:
    def __init__(self, s, table, units, matrix, sems, paired):
        self.count = s.count
        self.copies = {d: [] for d in range(s.count)}
        units = iter(units)
        for d in range(s.count - 1):
            parts = s.halves if d else 1
            for part in range(parts):
                size = s.rows // parts
                target = matrix.at[d, pl.ds(part * size, size)]
                self.copies[d].append(pltpu.make_async_copy(next(units), target, sems.at[d]))
        half, d = s.rows // 2, s.count - 1
        for side in (table[s.count], 1 - table[s.count]):
            target = matrix.at[d, pl.ds(pl.multiple_of(side * half, half), half)]
            self.copies[d].append(pltpu.make_async_copy(next(units), target, sems.at[d]))
        for d in range(s.count):
            k = table[d]
            for source, target in paired:
                self.copies[d].append(
                    pltpu.make_async_copy(source.at[k], target.at[k], sems.at[d])
                )
        self.ahead = AHEAD if s.count <= 8 else s.count
        for d in range(min(self.ahead, s.count)):
            self.start(d)
        if s.count > 8:
            for d in range(s.count):
                self.wait(d)

    def start(self, d):
        for piece in self.copies[d]:
            piece.start()

    def wait(self, d):
        for piece in self.copies[d]:
            piece.wait()

    def __call__(self, d):
        if self.count <= 8:
            self.wait(d)
            if d + self.ahead < self.count:
                self.start(d + self.ahead)


def load(sources, targets, sems):
    copies = [
        pltpu.make_async_copy(source, target, sems.at[k])
        for k, (source, target) in enumerate(zip(sources, targets))
    ]
    for copy in copies:
        copy.start()
    return copies


def gather_targets(s, pieces):
    return jnp.concatenate(
        [
            pieces[i, :, s.rows + t * s.share : s.rows + (t + 1) * s.share]
            for t in range(2)
            for i in range(s.count)
        ],
        axis=1,
    )


def scatter_targets(s, out, values):
    for i in range(s.count):
        out[i, :, s.rows : s.lanes] = jnp.concatenate(
            [
                values[:, t * s.cols + i * s.share : t * s.cols + (i + 1) * s.share]
                for t in range(2)
            ],
            axis=1,
        )


def chain(count, product, use, total):
    if count > 8:
        return lax.fori_loop(0, count, lambda d, t: use(d, product(d), t), total)
    ready = product(0)
    for d in range(count):
        later = product(d + 1) if d + 1 < count else None
        total = use(d, ready, total)
        ready = later
    return total


def forward_kernel(s, table, mass_in, *refs):
    given = 3 + (s.count - 2) * s.halves
    units, refs = refs[:given], refs[given:]
    thirds, leaving, (mass, matrix, sems, more_sems), state = refs[0], refs[1:6], refs[6:10], refs[10:]
    row_two, row_one, col_one, col_two, col_three = state
    arrived = Arrivals(s, table, units, matrix, sems, [(mass_in, mass)])
    ones = jnp.ones((2 * s.cols, 128), jnp.bfloat16)
    zero = jnp.zeros((s.hists, 2 * s.cols), jnp.float32)

    def sums(d):
        arrived(d)
        return nn(matrix[d], ones).T[0:8]

    def times(panel):
        turned = panel.T
        return lambda d: nn(matrix[d], turned).T

    def first(d, row, total):
        row_one[d] = row
        left = mass[table[d], :, : s.rows] * (1 / row[0:1])
        return total + nn(left.astype(jnp.bfloat16), matrix[d])

    total = chain(s.count, sums, first, zero)
    col_one[...] = total
    target = gather_targets(s, mass)
    panel = (target / total).astype(jnp.bfloat16)

    def second(d, row, total):
        row_two[d] = row
        left = mass[table[d], :, : s.rows] / row
        return total + nn(left.astype(jnp.bfloat16), matrix[d])

    total = chain(s.count, times(panel), second, zero)
    col_two[...] = total
    started = load(state[:4], leaving[:4], more_sems)
    last_panel = (target / total).astype(jnp.bfloat16)

    def third(d, row, total):
        thirds[table[d], :, : s.rows] = row
        left = mass[table[d], :, : s.rows] / row
        return total + nn(left.astype(jnp.bfloat16), matrix[d])

    total = chain(s.count, times(last_panel), third, zero)
    col_three[...] = total
    last = pltpu.make_async_copy(col_three, leaving[4], more_sems.at[4])
    last.start()
    scatter_targets(s, thirds, total)
    for copy in [*started, last]:
        copy.wait()


def backward_kernel(s, table, mass_in, cot_in, thirds_in, *refs):
    given = 3 + (s.count - 2) * s.halves
    state_in, units, refs = refs[:5], refs[5 : 5 + given], refs[5 + given :]
    out, (mass, matrix, sems, more_sems), state, (cot, thirds) = (
        refs[0],
        refs[1:5],
        refs[5:10],
        refs[10:],
    )
    row_two, row_one, col_one, col_two, col_three = state
    early = load([state_in[4], cot_in], [col_three, cot], more_sems)
    paired = [(mass_in, mass), (thirds_in, thirds)]
    arrived = Arrivals(s, table, units, matrix, sems, paired)
    late = [
        pltpu.make_async_copy(state_in[k], state[k], more_sems.at[2 + k]) for k in range(4)
    ]
    for copy in early:
        copy.wait()
    target_cot = gather_targets(s, cot)
    panel = (-target_cot / col_three[...]).astype(jnp.bfloat16)
    zero = jnp.zeros((s.hists, 2 * s.cols), jnp.float32)

    def first_product(d):
        arrived(d)
        if s.count <= 8 and d == s.count - AHEAD:
            for copy in late:
                copy.start()
        return nt(panel, matrix[d])

    def third(d, grad, total):
        k = table[d]
        over = 1 / thirds[k, :, : s.rows]
        term = grad * over
        out[k, :, : s.rows] = term
        rowgrad = -over * (cot[k, :, : s.rows] + term * mass[k, :, : s.rows])
        return total + nn(rowgrad.astype(jnp.bfloat16), matrix[d])

    total = chain(s.count, first_product, third, zero)
    for copy in late:
        if s.count > 8:
            copy.start()
        copy.wait()
    target = gather_targets(s, mass)
    term_two = total / col_two[...]
    panel_two = (-term_two * (target / col_two[...])).astype(jnp.bfloat16)

    def second(d, grad, total):
        k = table[d]
        over = 1 / row_two[d]
        term = grad * over
        out[k, :, : s.rows] += term
        rowgrad = -term * (mass[k, :, : s.rows] * over)
        return total + nn(rowgrad.astype(jnp.bfloat16), matrix[d])

    total = chain(s.count, lambda d: nt(panel_two, matrix[d]), second, zero)
    term_one = total / col_one[...]
    panel_one = (-term_one * (target / col_one[...])).astype(jnp.bfloat16)

    def first(d, grad, carry):
        out[table[d], :, : s.rows] += grad * (1 / row_one[d, 0:1])
        return carry

    chain(s.count, lambda d: nt(panel_one, matrix[d]), first, 0)
    scatter_targets(s, out, term_two + term_one)


def call(kernel, s, products, vmem_outs, hbm_outs, table, arrays, scratch):
    return pl.pallas_call(
        functools.partial(kernel, s),
        out_shape=[*vmem_outs, *hbm_outs],
        in_specs=[pl.BlockSpec(memory_space=pltpu.SMEM)]
        + [pl.BlockSpec(memory_space=pl.ANY)] * len(arrays),
        out_specs=[pl.BlockSpec(memory_space=pltpu.VMEM)] * len(vmem_outs)
        + [pl.BlockSpec(memory_space=pl.ANY)] * len(hbm_outs),
        scratch_shapes=[
            pltpu.VMEM((s.count, s.hists, s.lanes), jnp.float32),
            pltpu.VMEM((s.count, s.rows, 2 * s.cols), jnp.bfloat16),
            pltpu.SemaphoreType.DMA((s.count,)),
            pltpu.SemaphoreType.DMA((8,)),
            *[pltpu.VMEM(state.shape, state.dtype) for state in scratch],
        ],
        cost_estimate=pl.CostEstimate(
            flops=products * 2 * s.count * s.rows * 2 * s.cols * 256,
            bytes_accessed=s.count * s.rows * 2 * s.cols * 4,
            transcendentals=0,
        ),
        compiler_params=pltpu.CompilerParams(vmem_limit_bytes=VMEM),
    )(table, *arrays)


def swap_cores(x):
    return lax.ppermute(x, "tgt", [(0, 1), (1, 0)])


def local(
    source_mass,
    target_mass,
    kernel_tiles,
    tile_cols,
    tile_count,
    source_cotangent,
    target_cotangent,
):
    count = lax.axis_size("src")
    rows, cols_here = source_mass.shape
    share = target_mass.shape[1]
    s = Shape(count, rows, CB_DEV * kernel_tiles.shape[2], cols_here // count, share)
    ring = np.array(ring_order(count), np.int32)
    place = np.argsort(ring).astype(np.int32)
    me = lax.axis_index("src")
    core = lax.axis_index("tgt")
    at = jnp.asarray(place)[me]
    last = count // 2
    away = 2 * core - 1
    steps = [0] + [sign * k for k in range(1, last) for sign in (1, -1)] + [last]
    slots = (at + away * jnp.asarray(steps, jnp.int32)) % count
    table = jnp.concatenate([jnp.asarray(ring)[slots], core[None]]).astype(jnp.int32)

    def onward(x):
        pairs = []
        for p in range(count):
            pairs.append((int(ring[p]) * 2, int(ring[(p + 1) % count]) * 2))
            pairs.append((int(ring[p]) * 2 + 1, int(ring[(p - 1) % count]) * 2 + 1))
        return lax.ppermute(x, ("src", "tgt"), pairs)

    def exchange(x):
        return lax.all_to_all(x, "src", 0, 0, tiled=True)

    def in_order(mine, other, axis):
        return jnp.concatenate(
            [jnp.where(core == 0, mine, other), jnp.where(core == 0, other, mine)], axis=axis
        )

    def by_histogram(source, target):
        target = target.astype(HALF).reshape(share, 2, cols_here)
        mine = lax.dynamic_index_in_dim(target, core, 1, keepdims=False)
        other = lax.dynamic_index_in_dim(target, 1 - core, 1, keepdims=False)
        both = in_order(mine, swap_cores(other), 0).T
        return jnp.concatenate(
            [
                source.astype(HALF).T.reshape(count, s.hists, rows),
                both.reshape(count, s.hists, 2 * share),
            ],
            axis=2,
        )

    mine = dense_blocks(kernel_tiles, tile_cols, tile_count)
    unit = in_order(mine, swap_cores(mine), 1)
    unit, mass_here, points_here, cot_here, cot_points = lax.optimization_barrier(
        (unit, source_mass, target_mass[0], source_cotangent, target_cotangent[0])
    )
    mass_message = by_histogram(mass_here, points_here)
    cot_message = by_histogram(cot_here * COT_SCALE, cot_points * COT_SCALE)
    half = rows // s.halves
    heads = [unit[k * half : (k + 1) * half] for k in range(s.halves)]
    came, swapped = {}, {}
    for step in range(1, last):
        for k in range(s.halves):
            if step > 2:
                heads[k], swapped[step - 2, k] = lax.optimization_barrier(
                    (heads[k], swapped[step - 2, k])
                )
            if step == 2 and k == 0:
                heads[k], table = lax.optimization_barrier((heads[k], table))
            came[step, k] = heads[k] = onward(heads[k])
            leaving = heads[k]
            if step == last - 1 and k == 0:
                mass_here = exchange(mass_message)
                mass = mass_here.astype(jnp.float32)
                leaving, mass = lax.optimization_barrier((leaving, mass))
            swapped[step, k] = swap_cores(leaving)
            if step == 1 and k == 0:
                swapped[step, k], mass_message = lax.optimization_barrier(
                    (swapped[step, k], mass_message)
                )
    if s.halves == 1:
        piece = lax.dynamic_slice_in_dim(heads[0], core * (rows // 2), rows // 2, 0)
    else:
        piece = jnp.where(core == 0, heads[0], heads[1])
    due = [swapped[last - 2, k] for k in range(s.halves)]
    piece, due, cot_message, mass_here = lax.optimization_barrier(
        (piece, due, cot_message, mass_here)
    )
    swapped.update({(last - 2, k): due[k] for k in range(s.halves)})
    piece = onward(piece)
    units = [unit]
    for step in range(1, last):
        for part in (came, swapped):
            units += [part[step, k] for k in range(s.halves)]
    units += [piece, swap_cores(piece)]
    cot = exchange(cot_message).astype(jnp.float32)

    wide = jax.ShapeDtypeStruct((count, s.hists, s.lanes), jnp.float32)
    panel = jax.ShapeDtypeStruct((count, s.hists, rows), jnp.float32)
    sums = jax.ShapeDtypeStruct((count, 8, rows), jnp.float32)
    column = jax.ShapeDtypeStruct((s.hists, 2 * s.cols), jnp.float32)
    states = [panel, sums, column, column, column]
    thirds, *state = call(
        forward_kernel, s, 7, [wide], states, table, [mass, *units], states
    )
    (grads,) = call(
        backward_kernel,
        s,
        5,
        [wide],
        [],
        table,
        [mass, cot, thirds, *state, *units],
        [*states, wide, wide],
    )

    def by_point(pieces):
        flat = pieces.reshape(cols_here, s.lanes).astype(jnp.float32)
        target = flat[:, rows:].T.reshape(2, share, cols_here)
        own = lax.dynamic_index_in_dim(target, core, 0, keepdims=False)
        other = lax.dynamic_index_in_dim(target, 1 - core, 0, keepdims=False)
        other = swap_cores(other.astype(HALF)).astype(jnp.float32)
        return flat[:, :rows].T, in_order(own, other, 1)

    row_three, col_three = by_point(exchange(thirds.astype(HALF)))
    source_potential = jnp.log(source_mass / row_three)
    target_potential = jnp.log(target_mass[0] / col_three)
    source_known = source_cotangent / source_mass
    target_known = target_cotangent[0] / target_mass[0]
    back, source_potential, target_potential, source_known, target_known = lax.optimization_barrier(
        (
            exchange(grads.astype(HALF)),
            source_potential,
            target_potential,
            source_known,
            target_known,
        )
    )
    source_term, target_term = by_point(back)
    return (
        source_potential,
        target_potential[None],
        source_known + source_term * (1 / COT_SCALE),
        (target_known + target_term * (1 / COT_SCALE))[None],
    )


def solution(mesh):
    return jax.shard_map(
        local,
        mesh=mesh,
        in_specs=(
            P(("grp", "src"), "tgt"),
            P("tgt", ("grp", "src"), None),
            P(("grp", "src"), "tgt", None, None),
            P(("grp", "src"), "tgt"),
            P(("grp", "src"), "tgt"),
            P(("grp", "src"), "tgt"),
            P("tgt", ("grp", "src"), None),
        ),
        out_specs=(
            P(("grp", "src"), "tgt"),
            P("tgt", ("grp", "src"), None),
            P(("grp", "src"), "tgt"),
            P("tgt", ("grp", "src"), None),
        ),
        check_vma=False,
    )
```

```python
import functools

import jax
import jax.numpy as jnp
import numpy as np
from jax import lax
from jax.experimental import pallas as pl
from jax.experimental.pallas import tpu as pltpu
from jax.sharding import PartitionSpec as P

CB_DEV = 2
HALF = jnp.float16
COT_SCALE = 256.0
VMEM = 56 * 1024 * 1024
AHEAD = 3


def ring_order(count):
    if count == 8:
        return [0, 2, 4, 6, 7, 5, 3, 1]
    return list(range(count))


def dense_blocks(kernel_tiles, tile_cols, tile_count):
    keep = kernel_tiles.shape[1]
    live = jnp.arange(keep, dtype=jnp.int32)[None, :] < tile_count
    hits = (tile_cols[:, :, None] == jnp.arange(CB_DEV, dtype=jnp.int32)) & live[:, :, None]
    blocks = jnp.einsum(
        "rkc,rkab->racb",
        hits.astype(jnp.bfloat16),
        kernel_tiles,
        preferred_element_type=jnp.float32,
    )
    rows, cols = blocks.shape[0] * blocks.shape[1], blocks.shape[2] * blocks.shape[3]
    return blocks.astype(jnp.bfloat16).reshape(rows, cols)


def nt(x, y):
    return lax.dot_general(x, y, (((1,), (1,)), ((), ())), preferred_element_type=jnp.float32)


def nn(x, y):
    return jnp.dot(x, y, preferred_element_type=jnp.float32)


class Shape:
    def __init__(self, count, rows, cols, hists, share):
        self.count = count
        self.rows = rows
        self.cols = cols
        self.hists = hists
        self.share = share
        self.lanes = rows + 2 * share
        self.halves = 2 if count <= 8 else 1


class Arrivals:
    def __init__(self, s, table, units, matrix, sems, paired):
        self.count = s.count
        self.copies = {d: [] for d in range(s.count)}
        units = iter(units)
        for d in range(s.count - 1):
            parts = s.halves if d else 1
            for part in range(parts):
                size = s.rows // parts
                target = matrix.at[d, pl.ds(part * size, size)]
                self.copies[d].append(pltpu.make_async_copy(next(units), target, sems.at[d]))
        half, d = s.rows // 2, s.count - 1
        for side in (table[s.count], 1 - table[s.count]):
            target = matrix.at[d, pl.ds(pl.multiple_of(side * half, half), half)]
            self.copies[d].append(pltpu.make_async_copy(next(units), target, sems.at[d]))
        for d in range(s.count):
            k = table[d]
            for source, target in paired:
                self.copies[d].append(
                    pltpu.make_async_copy(source.at[k], target.at[k], sems.at[d])
                )
        self.ahead = AHEAD if s.count <= 8 else s.count
        for d in range(min(self.ahead, s.count)):
            self.start(d)
        if s.count > 8:
            for d in range(s.count):
                self.wait(d)

    def start(self, d):
        for piece in self.copies[d]:
            piece.start()

    def wait(self, d):
        for piece in self.copies[d]:
            piece.wait()

    def __call__(self, d):
        if self.count <= 8:
            self.wait(d)
            if d + self.ahead < self.count:
                self.start(d + self.ahead)


def load(sources, targets, sems):
    copies = [
        pltpu.make_async_copy(source, target, sems.at[k])
        for k, (source, target) in enumerate(zip(sources, targets))
    ]
    for copy in copies:
        copy.start()
    return copies


def gather_targets(s, pieces):
    return jnp.concatenate(
        [
            pieces[i, :, s.rows + t * s.share : s.rows + (t + 1) * s.share]
            for t in range(2)
            for i in range(s.count)
        ],
        axis=1,
    )


def scatter_targets(s, out, values, here=0):
    for i in range(s.count):
        out[i ^ here, :, s.rows : s.lanes] = jnp.concatenate(
            [
                values[:, t * s.cols + i * s.share : t * s.cols + (i + 1) * s.share]
                for t in range(2)
            ],
            axis=1,
        )


def chain(count, product, use, total):
    if count > 8:
        return lax.fori_loop(0, count, lambda d, t: use(d, product(d), t), total)
    ready = product(0)
    for d in range(count):
        later = product(d + 1) if d + 1 < count else None
        total = use(d, ready, total)
        ready = later
    return total


def forward_kernel(s, table, mass_in, *refs):
    given = 3 + (s.count - 2) * s.halves
    units, refs = refs[:given], refs[given:]
    thirds, leaving, (mass, matrix, sems, more_sems), state = refs[0], refs[1:6], refs[6:10], refs[10:]
    row_two, row_one, col_one, col_two, col_three = state
    arrived = Arrivals(s, table, units, matrix, sems, [(mass_in, mass)])
    ones = jnp.ones((8, 2 * s.cols), jnp.bfloat16)
    zero = jnp.zeros((s.hists, 2 * s.cols), jnp.float32)

    def sums(d):
        arrived(d)
        return nt(ones, matrix[d])

    def times(panel):
        return lambda d: nt(panel, matrix[d])

    def first(d, row, total):
        row_one[d] = row
        left = mass[table[d], :, : s.rows] * (1 / row[0:1])
        return total + nn(left.astype(jnp.bfloat16), matrix[d])

    total = chain(s.count, sums, first, zero)
    col_one[...] = total
    target = gather_targets(s, mass)
    panel = (target / total).astype(jnp.bfloat16)

    def second(d, row, total):
        row_two[d] = row
        left = mass[table[d], :, : s.rows] / row
        return total + nn(left.astype(jnp.bfloat16), matrix[d])

    total = chain(s.count, times(panel), second, zero)
    col_two[...] = total
    started = load(state[:4], leaving[:4], more_sems)
    last_panel = (target / total).astype(jnp.bfloat16)

    def third(d, row, total):
        thirds[table[d], :, : s.rows] = row
        left = mass[table[d], :, : s.rows] / row
        return total + nn(left.astype(jnp.bfloat16), matrix[d])

    total = chain(s.count, times(last_panel), third, zero)
    col_three[...] = total
    last = pltpu.make_async_copy(col_three, leaving[4], more_sems.at[4])
    last.start()
    scatter_targets(s, thirds, total)
    for copy in [*started, last]:
        copy.wait()


def backward_kernel(s, table, mass_in, cot_in, thirds_in, *refs):
    given = 3 + (s.count - 2) * s.halves
    state_in, units, refs = refs[:5], refs[5 : 5 + given], refs[5 + given :]
    out, (mass, matrix, sems, more_sems), state, (cot, thirds) = (
        refs[0],
        refs[1:5],
        refs[5:10],
        refs[10:],
    )
    row_two, row_one, col_one, col_two, col_three = state
    here = table[0]
    early = load([state_in[4], cot_in], [col_three, cot], more_sems)
    paired = [(mass_in, mass), (thirds_in, thirds)]
    arrived = Arrivals(s, table, units, matrix, sems, paired)
    late = [
        pltpu.make_async_copy(state_in[k], state[k], more_sems.at[2 + k]) for k in range(4)
    ]
    for copy in early:
        copy.wait()
    target_cot = gather_targets(s, cot)
    panel = (-target_cot / col_three[...]).astype(jnp.bfloat16)
    zero = jnp.zeros((s.hists, 2 * s.cols), jnp.float32)

    def first_product(d):
        arrived(d)
        if s.count <= 8 and d == s.count - AHEAD:
            for copy in late:
                copy.start()
        return nt(panel, matrix[d])

    def third(d, grad, total):
        k = table[d]
        over = 1 / thirds[k, :, : s.rows]
        term = grad * over
        out[k ^ here, :, : s.rows] = term
        rowgrad = -over * (cot[k, :, : s.rows] + term * mass[k, :, : s.rows])
        return total + nn(rowgrad.astype(jnp.bfloat16), matrix[d])

    total = chain(s.count, first_product, third, zero)
    for copy in late:
        if s.count > 8:
            copy.start()
        copy.wait()
    target = gather_targets(s, mass)
    term_two = total / col_two[...]
    panel_two = (-term_two * (target / col_two[...])).astype(jnp.bfloat16)

    def second(d, grad, total):
        k = table[d]
        over = 1 / row_two[d]
        term = grad * over
        out[k ^ here, :, : s.rows] += term
        rowgrad = -term * (mass[k, :, : s.rows] * over)
        return total + nn(rowgrad.astype(jnp.bfloat16), matrix[d])

    total = chain(s.count, lambda d: nt(panel_two, matrix[d]), second, zero)
    term_one = total / col_one[...]
    panel_one = (-term_one * (target / col_one[...])).astype(jnp.bfloat16)

    def first(d, grad, carry):
        out[table[d] ^ here, :, : s.rows] += grad * (1 / row_one[d, 0:1])
        return carry

    chain(s.count, lambda d: nt(panel_one, matrix[d]), first, 0)
    scatter_targets(s, out, term_two + term_one, here)


def call(kernel, s, products, vmem_outs, hbm_outs, table, arrays, scratch):
    return pl.pallas_call(
        functools.partial(kernel, s),
        out_shape=[*vmem_outs, *hbm_outs],
        in_specs=[pl.BlockSpec(memory_space=pltpu.SMEM)]
        + [pl.BlockSpec(memory_space=pl.ANY)] * len(arrays),
        out_specs=[pl.BlockSpec(memory_space=pltpu.VMEM)] * len(vmem_outs)
        + [pl.BlockSpec(memory_space=pl.ANY)] * len(hbm_outs),
        scratch_shapes=[
            pltpu.VMEM((s.count, s.hists, s.lanes), jnp.float32),
            pltpu.VMEM((s.count, s.rows, 2 * s.cols), jnp.bfloat16),
            pltpu.SemaphoreType.DMA((s.count,)),
            pltpu.SemaphoreType.DMA((8,)),
            *[pltpu.VMEM(state.shape, state.dtype) for state in scratch],
        ],
        cost_estimate=pl.CostEstimate(
            flops=products * 2 * s.count * s.rows * 2 * s.cols * 256,
            bytes_accessed=s.count * s.rows * 2 * s.cols * 4,
            transcendentals=0,
        ),
        compiler_params=pltpu.CompilerParams(vmem_limit_bytes=VMEM),
    )(table, *arrays)


def swap_cores(x):
    return lax.ppermute(x, "tgt", [(0, 1), (1, 0)])


def local(
    source_mass,
    target_mass,
    kernel_tiles,
    tile_cols,
    tile_count,
    source_cotangent,
    target_cotangent,
):
    count = lax.axis_size("src")
    rows, cols_here = source_mass.shape
    share = target_mass.shape[1]
    s = Shape(count, rows, CB_DEV * kernel_tiles.shape[2], cols_here // count, share)
    ring = np.array(ring_order(count), np.int32)
    place = np.argsort(ring).astype(np.int32)
    me = lax.axis_index("src")
    core = lax.axis_index("tgt")
    at = jnp.asarray(place)[me]
    last = count // 2
    away = 2 * core - 1
    steps = [0] + [sign * k for k in range(1, last) for sign in (1, -1)] + [last]
    slots = (at + away * jnp.asarray(steps, jnp.int32)) % count
    table = jnp.concatenate([jnp.asarray(ring)[slots], core[None]]).astype(jnp.int32)

    def onward(x):
        pairs = []
        for p in range(count):
            pairs.append((int(ring[p]) * 2, int(ring[(p + 1) % count]) * 2))
            pairs.append((int(ring[p]) * 2 + 1, int(ring[(p - 1) % count]) * 2 + 1))
        return lax.ppermute(x, ("src", "tgt"), pairs)

    def exchange(x):
        return lax.all_to_all(x, "src", 0, 0, tiled=True)

    def in_order(mine, other, axis):
        return jnp.concatenate(
            [jnp.where(core == 0, mine, other), jnp.where(core == 0, other, mine)], axis=axis
        )

    def by_histogram(source, target):
        target = target.astype(HALF).reshape(share, 2, cols_here)
        mine = lax.dynamic_index_in_dim(target, core, 1, keepdims=False)
        other = lax.dynamic_index_in_dim(target, 1 - core, 1, keepdims=False)
        both = in_order(mine, swap_cores(other), 0).T
        return jnp.concatenate(
            [
                source.astype(HALF).T.reshape(count, s.hists, rows),
                both.reshape(count, s.hists, 2 * share),
            ],
            axis=2,
        )

    mine = dense_blocks(kernel_tiles, tile_cols, tile_count)
    unit = in_order(mine, swap_cores(mine), 1)
    unit, mass_here, points_here, cot_here, cot_points = lax.optimization_barrier(
        (unit, source_mass, target_mass[0], source_cotangent, target_cotangent[0])
    )
    mass_message = by_histogram(mass_here, points_here)
    cot_message = by_histogram(cot_here * COT_SCALE, cot_points * COT_SCALE)
    half = rows // s.halves
    heads = [unit[k * half : (k + 1) * half] for k in range(s.halves)]
    came, swapped = {}, {}
    for step in range(1, last):
        for k in range(s.halves):
            if step > 2:
                heads[k], swapped[step - 2, k] = lax.optimization_barrier(
                    (heads[k], swapped[step - 2, k])
                )
            if step == 2 and k == 0:
                heads[k], table = lax.optimization_barrier((heads[k], table))
            came[step, k] = heads[k] = onward(heads[k])
            leaving = heads[k]
            if step == last - 1 and k == 0:
                mass_here = exchange(mass_message)
                mass = mass_here.astype(jnp.float32)
                leaving, mass = lax.optimization_barrier((leaving, mass))
            swapped[step, k] = swap_cores(leaving)
            if step == 1 and k == 0:
                swapped[step, k], mass_message = lax.optimization_barrier(
                    (swapped[step, k], mass_message)
                )
    if s.halves == 1:
        piece = lax.dynamic_slice_in_dim(heads[0], core * (rows // 2), rows // 2, 0)
    else:
        piece = jnp.where(core == 0, heads[0], heads[1])
    due = [swapped[last - 2, k] for k in range(s.halves)]
    piece, due, cot_message, mass_here = lax.optimization_barrier(
        (piece, due, cot_message, mass_here)
    )
    swapped.update({(last - 2, k): due[k] for k in range(s.halves)})
    piece = onward(piece)
    units = [unit]
    for step in range(1, last):
        for part in (came, swapped):
            units += [part[step, k] for k in range(s.halves)]
    units += [piece, swap_cores(piece)]
    cot = exchange(cot_message).astype(jnp.float32)

    wide = jax.ShapeDtypeStruct((count, s.hists, s.lanes), jnp.float32)
    panel = jax.ShapeDtypeStruct((count, s.hists, rows), jnp.float32)
    sums = jax.ShapeDtypeStruct((count, 8, rows), jnp.float32)
    column = jax.ShapeDtypeStruct((s.hists, 2 * s.cols), jnp.float32)
    states = [panel, sums, column, column, column]
    thirds, *state = call(
        forward_kernel, s, 7, [wide], states, table, [mass, *units], states
    )
    (grads,) = call(
        backward_kernel,
        s,
        5,
        [wide],
        [],
        table,
        [mass, cot, thirds, *state, *units],
        [*states, wide, wide],
    )

    def exchange_by_pairs(x):
        parts = {0: x[0]}
        for k in reversed(range(1, count)):
            parts[k] = lax.ppermute(x[k], "src", [(i, i ^ k) for i in range(count)])
        whole = jnp.zeros_like(x)
        for k in (0, *reversed(range(1, count))):
            whole = lax.dynamic_update_index_in_dim(whole, parts[k], me ^ k, 0)
        return whole

    def by_point(pieces):
        turned = pieces.reshape(cols_here, s.lanes).astype(jnp.float32).T
        target = turned[rows:].reshape(2, share, cols_here)
        own = lax.dynamic_index_in_dim(target, core, 0, keepdims=False)
        other = lax.dynamic_index_in_dim(target, 1 - core, 0, keepdims=False)
        other = swap_cores(other.astype(HALF)).astype(jnp.float32)
        return turned[:rows], in_order(own, other, 1)

    row_three, col_three = by_point(exchange(thirds.astype(HALF)))
    source_potential = jnp.log(source_mass / row_three)
    target_potential = jnp.log(target_mass[0] / col_three)
    source_known = source_cotangent / source_mass
    target_known = target_cotangent[0] / target_mass[0]
    back, source_potential, target_potential, source_known, target_known = lax.optimization_barrier(
        (
            exchange_by_pairs(grads.astype(HALF)),
            source_potential,
            target_potential,
            source_known,
            target_known,
        )
    )
    source_term, target_term = by_point(back)
    return (
        source_potential,
        target_potential[None],
        source_known + source_term * (1 / COT_SCALE),
        (target_known + target_term * (1 / COT_SCALE))[None],
    )


def solution(mesh):
    return jax.shard_map(
        local,
        mesh=mesh,
        in_specs=(
            P(("grp", "src"), "tgt"),
            P("tgt", ("grp", "src"), None),
            P(("grp", "src"), "tgt", None, None),
            P(("grp", "src"), "tgt"),
            P(("grp", "src"), "tgt"),
            P(("grp", "src"), "tgt"),
            P("tgt", ("grp", "src"), None),
        ),
        out_specs=(
            P(("grp", "src"), "tgt"),
            P("tgt", ("grp", "src"), None),
            P(("grp", "src"), "tgt"),
            P("tgt", ("grp", "src"), None),
        ),
        check_vma=False,
    )
```

```python
import functools

import jax
import jax.numpy as jnp
import numpy as np
from jax import lax
from jax.experimental import pallas as pl
from jax.experimental.pallas import tpu as pltpu
from jax.sharding import PartitionSpec as P

CB_DEV = 2
HALF = jnp.float16
COT_SCALE = 256.0
VMEM = 56 * 1024 * 1024
AHEAD = 3


def ring_order(count):
    if count == 8:
        return [0, 2, 4, 6, 7, 5, 3, 1]
    return list(range(count))


def dense_blocks(kernel_tiles, tile_cols, tile_count):
    keep = kernel_tiles.shape[1]
    live = jnp.arange(keep, dtype=jnp.int32)[None, :] < tile_count
    hits = (tile_cols[:, :, None] == jnp.arange(CB_DEV, dtype=jnp.int32)) & live[:, :, None]
    blocks = jnp.einsum(
        "rkc,rkab->racb",
        hits.astype(jnp.bfloat16),
        kernel_tiles,
        preferred_element_type=jnp.float32,
    )
    rows, cols = blocks.shape[0] * blocks.shape[1], blocks.shape[2] * blocks.shape[3]
    return blocks.astype(jnp.bfloat16).reshape(rows, cols)


def nt(x, y):
    return lax.dot_general(x, y, (((1,), (1,)), ((), ())), preferred_element_type=jnp.float32)


def nn(x, y):
    return jnp.dot(x, y, preferred_element_type=jnp.float32)


class Shape:
    def __init__(self, count, rows, cols, hists, share):
        self.count = count
        self.rows = rows
        self.cols = cols
        self.hists = hists
        self.share = share
        self.lanes = rows + 2 * share
        self.halves = 2 if count <= 8 else 1


class Arrivals:
    def __init__(self, s, table, units, matrix, sems, paired):
        self.count = s.count
        self.copies = {d: [] for d in range(s.count)}
        core = table[s.count]
        units = iter(units)
        for d in range(s.count):
            parts = 2 if d == s.count - 1 else s.halves
            size = s.rows // parts
            for part in range(parts):
                first = 1 - core if d and d % 2 == 0 else core
                side = first if part == 0 else 1 - first
                start = pl.multiple_of(side * size, size) if parts > 1 else 0
                target = matrix.at[d, pl.ds(start, size)]
                self.copies[d].append(pltpu.make_async_copy(next(units), target, sems.at[d]))
        for d in range(s.count):
            k = table[d]
            for source, target in paired:
                self.copies[d].append(
                    pltpu.make_async_copy(source.at[k], target.at[k], sems.at[d])
                )
        self.ahead = AHEAD if s.count <= 8 else s.count
        for d in range(min(self.ahead, s.count)):
            self.start(d)
        if s.count > 8:
            for d in range(s.count):
                self.wait(d)

    def start(self, d):
        for piece in self.copies[d]:
            piece.start()

    def wait(self, d):
        for piece in self.copies[d]:
            piece.wait()

    def __call__(self, d):
        if self.count <= 8:
            self.wait(d)
            if d + self.ahead < self.count:
                self.start(d + self.ahead)


def load(sources, targets, sems):
    copies = [
        pltpu.make_async_copy(source, target, sems.at[k])
        for k, (source, target) in enumerate(zip(sources, targets))
    ]
    for copy in copies:
        copy.start()
    return copies


def gather_targets(s, pieces):
    return jnp.concatenate(
        [
            pieces[i, :, s.rows + t * s.share : s.rows + (t + 1) * s.share]
            for t in range(2)
            for i in range(s.count)
        ],
        axis=1,
    )


def scatter_targets(s, out, values):
    for i in range(s.count):
        out[i, :, s.rows : s.lanes] = jnp.concatenate(
            [
                values[:, t * s.cols + i * s.share : t * s.cols + (i + 1) * s.share]
                for t in range(2)
            ],
            axis=1,
        )


def chain(count, product, use, total):
    if count > 8:
        return lax.fori_loop(0, count, lambda d, t: use(d, product(d), t), total)
    ready = product(0)
    for d in range(count):
        later = product(d + 1) if d + 1 < count else None
        total = use(d, ready, total)
        ready = later
    return total


def forward_kernel(s, table, mass_in, *refs):
    given = 2 + (s.count - 1) * s.halves
    units, refs = refs[:given], refs[given:]
    thirds, leaving, (mass, matrix, sems, more_sems), state = refs[0], refs[1:6], refs[6:10], refs[10:]
    row_two, row_one, col_one, col_two, col_three = state
    arrived = Arrivals(s, table, units, matrix, sems, [(mass_in, mass)])
    ones = jnp.ones((8, 2 * s.cols), jnp.bfloat16)
    zero = jnp.zeros((s.hists, 2 * s.cols), jnp.float32)

    def sums(d):
        arrived(d)
        return nt(ones, matrix[d])

    def times(panel):
        return lambda d: nt(panel, matrix[d])

    def first(d, row, total):
        row_one[d] = row
        left = mass[table[d], :, : s.rows] * (1 / row[0:1])
        return total + nn(left.astype(jnp.bfloat16), matrix[d])

    total = chain(s.count, sums, first, zero)
    col_one[...] = total
    target = gather_targets(s, mass)
    panel = (target / total).astype(jnp.bfloat16)

    def second(d, row, total):
        row_two[d] = row
        left = mass[table[d], :, : s.rows] / row
        return total + nn(left.astype(jnp.bfloat16), matrix[d])

    total = chain(s.count, times(panel), second, zero)
    col_two[...] = total
    started = load(state[:4], leaving[:4], more_sems)
    last_panel = (target / total).astype(jnp.bfloat16)

    def third(d, row, total):
        thirds[table[d], :, : s.rows] = row
        left = mass[table[d], :, : s.rows] / row
        return total + nn(left.astype(jnp.bfloat16), matrix[d])

    total = chain(s.count, times(last_panel), third, zero)
    col_three[...] = total
    last = pltpu.make_async_copy(col_three, leaving[4], more_sems.at[4])
    last.start()
    scatter_targets(s, thirds, total)
    for copy in [*started, last]:
        copy.wait()


def backward_kernel(s, table, mass_in, cot_in, thirds_in, *refs):
    given = 2 + (s.count - 1) * s.halves
    state_in, units, refs = refs[:5], refs[5 : 5 + given], refs[5 + given :]
    out, (mass, matrix, sems, more_sems), state, (cot, thirds) = (
        refs[0],
        refs[1:5],
        refs[5:10],
        refs[10:],
    )
    row_two, row_one, col_one, col_two, col_three = state
    early = load([state_in[4], cot_in], [col_three, cot], more_sems)
    paired = [(mass_in, mass), (thirds_in, thirds)]
    arrived = Arrivals(s, table, units, matrix, sems, paired)
    late = [
        pltpu.make_async_copy(state_in[k], state[k], more_sems.at[2 + k]) for k in range(4)
    ]
    for copy in early:
        copy.wait()
    target_cot = gather_targets(s, cot)
    panel = (-target_cot / col_three[...]).astype(jnp.bfloat16)
    zero = jnp.zeros((s.hists, 2 * s.cols), jnp.float32)

    def first_product(d):
        arrived(d)
        if s.count <= 8 and d == s.count - AHEAD:
            for copy in late:
                copy.start()
        return nt(panel, matrix[d])

    def third(d, grad, total):
        k = table[d]
        over = 1 / thirds[k, :, : s.rows]
        term = grad * over
        out[k, :, : s.rows] = term
        rowgrad = -over * (cot[k, :, : s.rows] + term * mass[k, :, : s.rows])
        return total + nn(rowgrad.astype(jnp.bfloat16), matrix[d])

    total = chain(s.count, first_product, third, zero)
    for copy in late:
        if s.count > 8:
            copy.start()
        copy.wait()
    target = gather_targets(s, mass)
    term_two = total / col_two[...]
    panel_two = (-term_two * (target / col_two[...])).astype(jnp.bfloat16)

    def second(d, grad, total):
        k = table[d]
        over = 1 / row_two[d]
        term = grad * over
        out[k, :, : s.rows] += term
        rowgrad = -term * (mass[k, :, : s.rows] * over)
        return total + nn(rowgrad.astype(jnp.bfloat16), matrix[d])

    total = chain(s.count, lambda d: nt(panel_two, matrix[d]), second, zero)
    term_one = total / col_one[...]
    panel_one = (-term_one * (target / col_one[...])).astype(jnp.bfloat16)

    def first(d, grad, carry):
        out[table[d], :, : s.rows] += grad * (1 / row_one[d, 0:1])
        return carry

    chain(s.count, lambda d: nt(panel_one, matrix[d]), first, 0)
    scatter_targets(s, out, term_two + term_one)


def call(kernel, s, products, vmem_outs, hbm_outs, table, arrays, scratch):
    return pl.pallas_call(
        functools.partial(kernel, s),
        out_shape=[*vmem_outs, *hbm_outs],
        in_specs=[pl.BlockSpec(memory_space=pltpu.SMEM)]
        + [pl.BlockSpec(memory_space=pl.ANY)] * len(arrays),
        out_specs=[pl.BlockSpec(memory_space=pltpu.VMEM)] * len(vmem_outs)
        + [pl.BlockSpec(memory_space=pl.ANY)] * len(hbm_outs),
        scratch_shapes=[
            pltpu.VMEM((s.count, s.hists, s.lanes), jnp.float32),
            pltpu.VMEM((s.count, s.rows, 2 * s.cols), jnp.bfloat16),
            pltpu.SemaphoreType.DMA((s.count,)),
            pltpu.SemaphoreType.DMA((8,)),
            *[pltpu.VMEM(state.shape, state.dtype) for state in scratch],
        ],
        cost_estimate=pl.CostEstimate(
            flops=products * 2 * s.count * s.rows * 2 * s.cols * 256,
            bytes_accessed=s.count * s.rows * 2 * s.cols * 4,
            transcendentals=0,
        ),
        compiler_params=pltpu.CompilerParams(vmem_limit_bytes=VMEM),
    )(table, *arrays)


def swap_cores(x):
    return lax.ppermute(x, "tgt", [(0, 1), (1, 0)])


def local(
    source_mass,
    target_mass,
    kernel_tiles,
    tile_cols,
    tile_count,
    source_cotangent,
    target_cotangent,
):
    count = lax.axis_size("src")
    rows, cols_here = source_mass.shape
    share = target_mass.shape[1]
    s = Shape(count, rows, CB_DEV * kernel_tiles.shape[2], cols_here // count, share)
    ring = np.array(ring_order(count), np.int32)
    place = np.argsort(ring).astype(np.int32)
    me = lax.axis_index("src")
    core = lax.axis_index("tgt")
    at = jnp.asarray(place)[me]
    last = count // 2
    away = 2 * core - 1
    steps = [0] + [sign * k for k in range(1, last) for sign in (1, -1)] + [last]
    slots = (at + away * jnp.asarray(steps, jnp.int32)) % count
    table = jnp.concatenate([jnp.asarray(ring)[slots], core[None]]).astype(jnp.int32)

    def onward(x):
        pairs = []
        for p in range(count):
            pairs.append((int(ring[p]) * 2, int(ring[(p + 1) % count]) * 2))
            pairs.append((int(ring[p]) * 2 + 1, int(ring[(p - 1) % count]) * 2 + 1))
        return lax.ppermute(x, ("src", "tgt"), pairs)

    def exchange(x):
        return lax.all_to_all(x, "src", 0, 0, tiled=True)

    def in_order(mine, other, axis):
        return jnp.concatenate(
            [jnp.where(core == 0, mine, other), jnp.where(core == 0, other, mine)], axis=axis
        )

    def by_histogram(source, target):
        target = target.astype(HALF).reshape(share, 2, cols_here)
        mine = lax.dynamic_index_in_dim(target, core, 1, keepdims=False)
        other = lax.dynamic_index_in_dim(target, 1 - core, 1, keepdims=False)
        both = in_order(mine, swap_cores(other), 0).T
        return jnp.concatenate(
            [
                source.astype(HALF).T.reshape(count, s.hists, rows),
                both.reshape(count, s.hists, 2 * share),
            ],
            axis=2,
        )

    mine = dense_blocks(kernel_tiles, tile_cols, tile_count)
    theirs = swap_cores(mine)
    half = rows // s.halves
    heads = []
    for k in range(s.halves):
        start = half * jnp.where(core == 0, k, s.halves - 1 - k)
        both = [lax.dynamic_slice_in_dim(x, start, half, 0) for x in (mine, theirs)]
        heads.append(in_order(*both, 1))
    heads, mass_here, points_here, cot_here, cot_points = lax.optimization_barrier(
        (heads, source_mass, target_mass[0], source_cotangent, target_cotangent[0])
    )
    units = list(heads)
    mass_message = by_histogram(mass_here, points_here)
    cot_message = by_histogram(cot_here * COT_SCALE, cot_points * COT_SCALE)
    came, swapped = {}, {}
    for step in range(1, last):
        for k in range(s.halves):
            if step > 2:
                heads[k], swapped[step - 2, k] = lax.optimization_barrier(
                    (heads[k], swapped[step - 2, k])
                )
            if step == 2 and k == 0:
                heads[k], table = lax.optimization_barrier((heads[k], table))
            came[step, k] = heads[k] = onward(heads[k])
            leaving = heads[k]
            if step == last - 1 and k == 0:
                mass_here = exchange(mass_message)
                mass = mass_here.astype(jnp.float32)
                leaving, mass = lax.optimization_barrier((leaving, mass))
            swapped[step, k] = swap_cores(leaving)
            if step == 1 and k == 0:
                swapped[step, k], mass_message = lax.optimization_barrier(
                    (swapped[step, k], mass_message)
                )
    if s.halves == 1:
        piece = lax.dynamic_slice_in_dim(heads[0], core * (rows // 2), rows // 2, 0)
    else:
        piece = heads[0]
    due = [swapped[last - 2, k] for k in range(s.halves)]
    piece, due, cot_message, mass_here = lax.optimization_barrier(
        (piece, due, cot_message, mass_here)
    )
    swapped.update({(last - 2, k): due[k] for k in range(s.halves)})
    piece = onward(piece)
    for step in range(1, last):
        for part in (came, swapped):
            units += [part[step, k] for k in range(s.halves)]
    units += [piece, swap_cores(piece)]
    cot = exchange(cot_message).astype(jnp.float32)

    wide = jax.ShapeDtypeStruct((count, s.hists, s.lanes), jnp.float32)
    panel = jax.ShapeDtypeStruct((count, s.hists, rows), jnp.float32)
    sums = jax.ShapeDtypeStruct((count, 8, rows), jnp.float32)
    column = jax.ShapeDtypeStruct((s.hists, 2 * s.cols), jnp.float32)
    states = [panel, sums, column, column, column]
    thirds, *state = call(
        forward_kernel, s, 7, [wide], states, table, [mass, *units], states
    )
    (grads,) = call(
        backward_kernel,
        s,
        5,
        [wide],
        [],
        table,
        [mass, cot, thirds, *state, *units],
        [*states, wide, wide],
    )

    def by_point(pieces):
        turned = pieces.reshape(cols_here, s.lanes).astype(jnp.float32).T
        target = turned[rows:].reshape(2, share, cols_here)
        own = lax.dynamic_index_in_dim(target, core, 0, keepdims=False)
        other = lax.dynamic_index_in_dim(target, 1 - core, 0, keepdims=False)
        other = swap_cores(other.astype(HALF)).astype(jnp.float32)
        return turned[:rows], in_order(own, other, 1)

    row_three, col_three = by_point(exchange(thirds.astype(HALF)))
    source_potential = jnp.log(source_mass / row_three)
    target_potential = jnp.log(target_mass[0] / col_three)
    source_known = source_cotangent / source_mass
    target_known = target_cotangent[0] / target_mass[0]
    back, source_potential, target_potential, source_known, target_known = lax.optimization_barrier(
        (
            exchange(grads.astype(HALF)),
            source_potential,
            target_potential,
            source_known,
            target_known,
        )
    )
    source_term, target_term = by_point(back)
    return (
        source_potential,
        target_potential[None],
        source_known + source_term * (1 / COT_SCALE),
        (target_known + target_term * (1 / COT_SCALE))[None],
    )


def solution(mesh):
    return jax.shard_map(
        local,
        mesh=mesh,
        in_specs=(
            P(("grp", "src"), "tgt"),
            P("tgt", ("grp", "src"), None),
            P(("grp", "src"), "tgt", None, None),
            P(("grp", "src"), "tgt"),
            P(("grp", "src"), "tgt"),
            P(("grp", "src"), "tgt"),
            P("tgt", ("grp", "src"), None),
        ),
        out_specs=(
            P(("grp", "src"), "tgt"),
            P("tgt", ("grp", "src"), None),
            P(("grp", "src"), "tgt"),
            P("tgt", ("grp", "src"), None),
        ),
        check_vma=False,
    )
```

```python
import functools

import jax
import jax.numpy as jnp
import numpy as np
from jax import lax
from jax.experimental import pallas as pl
from jax.experimental.pallas import tpu as pltpu
from jax.sharding import PartitionSpec as P

CB_DEV = 2
HALF = jnp.float16
COT_SCALE = 256.0
VMEM = 56 * 1024 * 1024
AHEAD = 3


def ring_order(count):
    if count == 8:
        return [0, 2, 4, 6, 7, 5, 3, 1]
    return list(range(count))


def dense_blocks(kernel_tiles, tile_cols, tile_count):
    keep = kernel_tiles.shape[1]
    live = jnp.arange(keep, dtype=jnp.int32)[None, :] < tile_count
    hits = (tile_cols[:, :, None] == jnp.arange(CB_DEV, dtype=jnp.int32)) & live[:, :, None]
    blocks = jnp.einsum(
        "rkc,rkab->racb",
        hits.astype(jnp.bfloat16),
        kernel_tiles,
        preferred_element_type=jnp.float32,
    )
    rows, cols = blocks.shape[0] * blocks.shape[1], blocks.shape[2] * blocks.shape[3]
    return blocks.astype(jnp.bfloat16).reshape(rows, cols)


def nt(x, y):
    return lax.dot_general(x, y, (((1,), (1,)), ((), ())), preferred_element_type=jnp.float32)


def nn(x, y):
    return jnp.dot(x, y, preferred_element_type=jnp.float32)


class Shape:
    def __init__(self, count, rows, cols, hists, share):
        self.count = count
        self.rows = rows
        self.cols = cols
        self.hists = hists
        self.share = share
        self.lanes = rows + 2 * share
        self.halves = 2 if count <= 8 else 1


class Arrivals:
    def __init__(self, s, table, units, matrix, sems, paired):
        self.count = s.count
        self.copies = {d: [] for d in range(s.count)}
        core = table[s.count]
        units = iter(units)
        for d in range(s.count):
            parts = 2 if d == s.count - 1 else s.halves
            size = s.rows // parts
            for part in range(parts):
                first = 1 - core if d and d % 2 == 0 else core
                side = first if part == 0 else 1 - first
                start = pl.multiple_of(side * size, size) if parts > 1 else 0
                target = matrix.at[d, pl.ds(start, size)]
                self.copies[d].append(pltpu.make_async_copy(next(units), target, sems.at[d]))
        for d in range(s.count):
            k = table[d]
            for source, target in paired:
                self.copies[d].append(
                    pltpu.make_async_copy(source.at[k], target.at[k], sems.at[d])
                )
        self.ahead = AHEAD if s.count <= 8 else s.count
        for d in range(min(self.ahead, s.count)):
            self.start(d)
        if s.count > 8:
            for d in range(s.count):
                self.wait(d)

    def start(self, d):
        for piece in self.copies[d]:
            piece.start()

    def wait(self, d):
        for piece in self.copies[d]:
            piece.wait()

    def __call__(self, d):
        if self.count <= 8:
            self.wait(d)
            if d + self.ahead < self.count:
                self.start(d + self.ahead)


def load(sources, targets, sems):
    copies = [
        pltpu.make_async_copy(source, target, sems.at[k])
        for k, (source, target) in enumerate(zip(sources, targets))
    ]
    for copy in copies:
        copy.start()
    return copies


def gather_targets(s, pieces):
    return jnp.concatenate(
        [
            pieces[i, :, s.rows + t * s.share : s.rows + (t + 1) * s.share]
            for t in range(2)
            for i in range(s.count)
        ],
        axis=1,
    )


def scatter_targets(s, out, values):
    for i in range(s.count):
        out[i, :, s.rows : s.lanes] = jnp.concatenate(
            [
                values[:, t * s.cols + i * s.share : t * s.cols + (i + 1) * s.share]
                for t in range(2)
            ],
            axis=1,
        )


def chain(count, product, use, total):
    if count > 8:
        return lax.fori_loop(0, count, lambda d, t: use(d, product(d), t), total)
    ready = product(0)
    for d in range(count):
        later = product(d + 1) if d + 1 < count else None
        total = use(d, ready, total)
        ready = later
    return total


def forward_kernel(s, table, mass_in, *refs):
    given = 2 + (s.count - 1) * s.halves
    units, refs = refs[:given], refs[given:]
    thirds, leaving, (mass, matrix, sems, more_sems), state = refs[0], refs[1:6], refs[6:10], refs[10:]
    row_two, row_one, col_one, col_two, col_three = state
    arrived = Arrivals(s, table, units, matrix, sems, [(mass_in, mass)])
    ones = jnp.ones((8, 2 * s.cols), jnp.bfloat16)
    zero = jnp.zeros((s.hists, 2 * s.cols), jnp.float32)

    def sums(d):
        arrived(d)
        return nt(ones, matrix[d])

    def times(panel):
        return lambda d: nt(panel, matrix[d])

    def first(d, row, total):
        row_one[d] = row
        left = mass[table[d], :, : s.rows] * (1 / row[0:1])
        return total + nn(left.astype(jnp.bfloat16), matrix[d])

    total = chain(s.count, sums, first, zero)
    col_one[...] = total
    target = gather_targets(s, mass)
    panel = (target / total).astype(jnp.bfloat16)

    def second(d, row, total):
        row_two[d] = row
        left = mass[table[d], :, : s.rows] / row
        return total + nn(left.astype(jnp.bfloat16), matrix[d])

    total = chain(s.count, times(panel), second, zero)
    col_two[...] = total
    started = load(state[:4], leaving[:4], more_sems)
    last_panel = (target / total).astype(jnp.bfloat16)

    def third(d, row, total):
        thirds[table[d], :, : s.rows] = row
        left = mass[table[d], :, : s.rows] / row
        return total + nn(left.astype(jnp.bfloat16), matrix[d])

    total = chain(s.count, times(last_panel), third, zero)
    col_three[...] = total
    last = pltpu.make_async_copy(col_three, leaving[4], more_sems.at[4])
    last.start()
    scatter_targets(s, thirds, total)
    for copy in [*started, last]:
        copy.wait()


def backward_kernel(s, table, mass_in, cot_in, thirds_in, *refs):
    given = 2 + (s.count - 1) * s.halves
    state_in, units, refs = refs[:5], refs[5 : 5 + given], refs[5 + given :]
    out, (mass, matrix, sems, more_sems), state, (cot, thirds) = (
        refs[0],
        refs[1:5],
        refs[5:10],
        refs[10:],
    )
    row_two, row_one, col_one, col_two, col_three = state
    early = load([state_in[4], cot_in], [col_three, cot], more_sems)
    paired = [(mass_in, mass), (thirds_in, thirds)]
    arrived = Arrivals(s, table, units, matrix, sems, paired)
    late = [
        pltpu.make_async_copy(state_in[k], state[k], more_sems.at[2 + k]) for k in range(4)
    ]
    for copy in early:
        copy.wait()
    target_cot = gather_targets(s, cot)
    panel = (-target_cot / col_three[...]).astype(jnp.bfloat16)
    zero = jnp.zeros((s.hists, 2 * s.cols), jnp.float32)

    def first_product(d):
        arrived(d)
        if s.count <= 8 and d == s.count - AHEAD:
            for copy in late:
                copy.start()
        return nt(panel, matrix[d])

    def third(d, grad, total):
        k = table[d]
        over = 1 / thirds[k, :, : s.rows]
        term = grad * over
        out[k, :, : s.rows] = term
        rowgrad = -over * (cot[k, :, : s.rows] + term * mass[k, :, : s.rows])
        return total + nn(rowgrad.astype(jnp.bfloat16), matrix[d])

    total = chain(s.count, first_product, third, zero)
    for copy in late:
        if s.count > 8:
            copy.start()
        copy.wait()
    target = gather_targets(s, mass)
    term_two = total / col_two[...]
    panel_two = (-term_two * (target / col_two[...])).astype(jnp.bfloat16)

    def second(d, grad, total):
        k = table[d]
        over = 1 / row_two[d]
        term = grad * over
        out[k, :, : s.rows] += term
        rowgrad = -term * (mass[k, :, : s.rows] * over)
        return total + nn(rowgrad.astype(jnp.bfloat16), matrix[d])

    total = chain(s.count, lambda d: nt(panel_two, matrix[d]), second, zero)
    term_one = total / col_one[...]
    panel_one = (-term_one * (target / col_one[...])).astype(jnp.bfloat16)

    def first(d, grad, carry):
        out[table[d], :, : s.rows] += grad * (1 / row_one[d, 0:1])
        return carry

    chain(s.count, lambda d: nt(panel_one, matrix[d]), first, 0)
    scatter_targets(s, out, term_two + term_one)


def call(kernel, s, products, vmem_outs, hbm_outs, table, arrays, scratch):
    return pl.pallas_call(
        functools.partial(kernel, s),
        out_shape=[*vmem_outs, *hbm_outs],
        in_specs=[pl.BlockSpec(memory_space=pltpu.SMEM)]
        + [pl.BlockSpec(memory_space=pl.ANY)] * len(arrays),
        out_specs=[pl.BlockSpec(memory_space=pltpu.VMEM)] * len(vmem_outs)
        + [pl.BlockSpec(memory_space=pl.ANY)] * len(hbm_outs),
        scratch_shapes=[
            pltpu.VMEM((s.count, s.hists, s.lanes), jnp.float32),
            pltpu.VMEM((s.count, s.rows, 2 * s.cols), jnp.bfloat16),
            pltpu.SemaphoreType.DMA((s.count,)),
            pltpu.SemaphoreType.DMA((8,)),
            *[pltpu.VMEM(state.shape, state.dtype) for state in scratch],
        ],
        cost_estimate=pl.CostEstimate(
            flops=products * 2 * s.count * s.rows * 2 * s.cols * 256,
            bytes_accessed=s.count * s.rows * 2 * s.cols * 4,
            transcendentals=0,
        ),
        compiler_params=pltpu.CompilerParams(vmem_limit_bytes=VMEM),
    )(table, *arrays)


def swap_cores(x):
    return lax.ppermute(x, "tgt", [(0, 1), (1, 0)])


def local(
    source_mass,
    target_mass,
    kernel_tiles,
    tile_cols,
    tile_count,
    source_cotangent,
    target_cotangent,
):
    count = lax.axis_size("src")
    rows, cols_here = source_mass.shape
    share = target_mass.shape[1]
    s = Shape(count, rows, CB_DEV * kernel_tiles.shape[2], cols_here // count, share)
    ring = np.array(ring_order(count), np.int32)
    place = np.argsort(ring).astype(np.int32)
    me = lax.axis_index("src")
    core = lax.axis_index("tgt")
    at = jnp.asarray(place)[me]
    last = count // 2
    away = 2 * core - 1
    steps = [0] + [sign * k for k in range(1, last) for sign in (1, -1)] + [last]
    slots = (at + away * jnp.asarray(steps, jnp.int32)) % count
    table = jnp.concatenate([jnp.asarray(ring)[slots], core[None]]).astype(jnp.int32)

    def onward(x):
        pairs = []
        for p in range(count):
            pairs.append((int(ring[p]) * 2, int(ring[(p + 1) % count]) * 2))
            pairs.append((int(ring[p]) * 2 + 1, int(ring[(p - 1) % count]) * 2 + 1))
        return lax.ppermute(x, ("src", "tgt"), pairs)

    def exchange(x):
        return lax.all_to_all(x, "src", 0, 0, tiled=True)

    def in_order(mine, other, axis):
        return jnp.concatenate(
            [jnp.where(core == 0, mine, other), jnp.where(core == 0, other, mine)], axis=axis
        )

    def by_histogram(source, target):
        target = target.astype(HALF).reshape(share, 2, cols_here)
        mine = lax.dynamic_index_in_dim(target, core, 1, keepdims=False)
        other = lax.dynamic_index_in_dim(target, 1 - core, 1, keepdims=False)
        both = in_order(mine, swap_cores(other), 0).T
        return jnp.concatenate(
            [
                source.astype(HALF).T.reshape(count, s.hists, rows),
                both.reshape(count, s.hists, 2 * share),
            ],
            axis=2,
        )

    mine = dense_blocks(kernel_tiles, tile_cols, tile_count)
    theirs = swap_cores(mine)
    half = rows // s.halves
    cut = lambda x: [x[k * half : (k + 1) * half] for k in range(s.halves)]
    heads = [
        jnp.concatenate([jnp.where(core == 0, a, d), jnp.where(core == 0, b, c)], axis=1)
        for a, b, c, d in zip(cut(mine), cut(theirs), reversed(cut(mine)), reversed(cut(theirs)))
    ]
    heads, mass_here, points_here, cot_here, cot_points = lax.optimization_barrier(
        (heads, source_mass, target_mass[0], source_cotangent, target_cotangent[0])
    )
    units = list(heads)
    mass_message = by_histogram(mass_here, points_here)
    cot_message = by_histogram(cot_here * COT_SCALE, cot_points * COT_SCALE)
    came, swapped = {}, {}
    for step in range(1, last):
        for k in range(s.halves):
            if step > 2:
                heads[k], swapped[step - 2, k] = lax.optimization_barrier(
                    (heads[k], swapped[step - 2, k])
                )
            if step == 2 and k == 0:
                heads[k], table = lax.optimization_barrier((heads[k], table))
            came[step, k] = heads[k] = onward(heads[k])
            leaving = heads[k]
            if step == last - 1 and k == 0:
                mass_here = exchange(mass_message)
                mass = mass_here.astype(jnp.float32)
                leaving, mass = lax.optimization_barrier((leaving, mass))
            swapped[step, k] = swap_cores(leaving)
            if step == 1 and k == s.halves - 1:
                swapped[step, k], mass_message = lax.optimization_barrier(
                    (swapped[step, k], mass_message)
                )
    if s.halves == 1:
        piece = lax.dynamic_slice_in_dim(heads[0], core * (rows // 2), rows // 2, 0)
    else:
        piece = heads[0]
    due = [swapped[last - 2, k] for k in range(s.halves)]
    piece, due, cot_message, mass_here = lax.optimization_barrier(
        (piece, due, cot_message, mass_here)
    )
    swapped.update({(last - 2, k): due[k] for k in range(s.halves)})
    piece = onward(piece)
    for step in range(1, last):
        for part in (came, swapped):
            units += [part[step, k] for k in range(s.halves)]
    units += [piece, swap_cores(piece)]
    cot = exchange(cot_message).astype(jnp.float32)

    wide = jax.ShapeDtypeStruct((count, s.hists, s.lanes), jnp.float32)
    panel = jax.ShapeDtypeStruct((count, s.hists, rows), jnp.float32)
    sums = jax.ShapeDtypeStruct((count, 8, rows), jnp.float32)
    column = jax.ShapeDtypeStruct((s.hists, 2 * s.cols), jnp.float32)
    states = [panel, sums, column, column, column]
    thirds, *state = call(
        forward_kernel, s, 7, [wide], states, table, [mass, *units], states
    )
    (grads,) = call(
        backward_kernel,
        s,
        5,
        [wide],
        [],
        table,
        [mass, cot, thirds, *state, *units],
        [*states, wide, wide],
    )

    def by_point(pieces):
        turned = pieces.reshape(cols_here, s.lanes).astype(jnp.float32).T
        target = turned[rows:].reshape(2, share, cols_here)
        own = lax.dynamic_index_in_dim(target, core, 0, keepdims=False)
        other = lax.dynamic_index_in_dim(target, 1 - core, 0, keepdims=False)
        other = swap_cores(other.astype(HALF)).astype(jnp.float32)
        return turned[:rows], in_order(own, other, 1)

    row_three, col_three = by_point(exchange(thirds.astype(HALF)))
    source_potential = jnp.log(source_mass / row_three)
    target_potential = jnp.log(target_mass[0] / col_three)
    source_known = source_cotangent / source_mass
    target_known = target_cotangent[0] / target_mass[0]
    back, source_potential, target_potential, source_known, target_known = lax.optimization_barrier(
        (
            exchange(grads.astype(HALF)),
            source_potential,
            target_potential,
            source_known,
            target_known,
        )
    )
    source_term, target_term = by_point(back)
    return (
        source_potential,
        target_potential[None],
        source_known + source_term * (1 / COT_SCALE),
        (target_known + target_term * (1 / COT_SCALE))[None],
    )


def solution(mesh):
    return jax.shard_map(
        local,
        mesh=mesh,
        in_specs=(
            P(("grp", "src"), "tgt"),
            P("tgt", ("grp", "src"), None),
            P(("grp", "src"), "tgt", None, None),
            P(("grp", "src"), "tgt"),
            P(("grp", "src"), "tgt"),
            P(("grp", "src"), "tgt"),
            P("tgt", ("grp", "src"), None),
        ),
        out_specs=(
            P(("grp", "src"), "tgt"),
            P("tgt", ("grp", "src"), None),
            P(("grp", "src"), "tgt"),
            P("tgt", ("grp", "src"), None),
        ),
        check_vma=False,
    )
```

```python
import functools

import jax
import jax.numpy as jnp
import numpy as np
from jax import lax
from jax.experimental import pallas as pl
from jax.experimental.pallas import tpu as pltpu
from jax.sharding import PartitionSpec as P

CB_DEV = 2
HALF = jnp.float16
COT_SCALE = 256.0
VMEM = 56 * 1024 * 1024
AHEAD = 3


def ring_order(count):
    if count == 8:
        return [0, 2, 4, 6, 7, 5, 3, 1]
    return list(range(count))


def dense_blocks(kernel_tiles, tile_cols, tile_count):
    keep = kernel_tiles.shape[1]
    live = jnp.arange(keep, dtype=jnp.int32)[None, :] < tile_count
    hits = (tile_cols[:, :, None] == jnp.arange(CB_DEV, dtype=jnp.int32)) & live[:, :, None]
    blocks = jnp.einsum(
        "rkc,rkab->racb",
        hits.astype(jnp.bfloat16),
        kernel_tiles,
        preferred_element_type=jnp.float32,
    )
    rows, cols = blocks.shape[0] * blocks.shape[1], blocks.shape[2] * blocks.shape[3]
    return blocks.astype(jnp.bfloat16).reshape(rows, cols)


def nt(x, y):
    return lax.dot_general(x, y, (((1,), (1,)), ((), ())), preferred_element_type=jnp.float32)


def nn(x, y):
    return jnp.dot(x, y, preferred_element_type=jnp.float32)


class Shape:
    def __init__(self, count, rows, cols, hists, share):
        self.count = count
        self.rows = rows
        self.cols = cols
        self.hists = hists
        self.share = share
        self.lanes = rows + 2 * share
        self.halves = 2 if count <= 8 else 1


class Arrivals:
    def __init__(self, s, table, units, matrix, sems, paired):
        self.count = s.count
        self.copies = {d: [] for d in range(s.count)}
        core = table[s.count]
        units = iter(units)
        for d in range(s.count):
            parts = 2 if d == s.count - 1 else s.halves
            size = s.rows // parts
            for part in range(parts):
                first = 1 - core if d and d % 2 == 0 else core
                side = first if part == 0 else 1 - first
                start = pl.multiple_of(side * size, size) if parts > 1 else 0
                target = matrix.at[d, pl.ds(start, size)]
                self.copies[d].append(pltpu.make_async_copy(next(units), target, sems.at[d]))
        for d in range(s.count):
            k = table[d]
            for source, target in paired:
                self.copies[d].append(
                    pltpu.make_async_copy(source.at[k], target.at[k], sems.at[d])
                )
        self.ahead = AHEAD if s.count <= 8 else s.count
        for d in range(min(self.ahead, s.count)):
            self.start(d)
        if s.count > 8:
            for d in range(s.count):
                self.wait(d)

    def start(self, d):
        for piece in self.copies[d]:
            piece.start()

    def wait(self, d):
        for piece in self.copies[d]:
            piece.wait()

    def __call__(self, d):
        if self.count <= 8:
            self.wait(d)
            if d + self.ahead < self.count:
                self.start(d + self.ahead)


def load(sources, targets, sems):
    copies = [
        pltpu.make_async_copy(source, target, sems.at[k])
        for k, (source, target) in enumerate(zip(sources, targets))
    ]
    for copy in copies:
        copy.start()
    return copies


def gather_targets(s, pieces):
    return jnp.concatenate(
        [
            pieces[i, :, s.rows + t * s.share : s.rows + (t + 1) * s.share]
            for t in range(2)
            for i in range(s.count)
        ],
        axis=1,
    )


def scatter_targets(s, out, values):
    for i in range(s.count):
        out[i, :, s.rows : s.lanes] = jnp.concatenate(
            [
                values[:, t * s.cols + i * s.share : t * s.cols + (i + 1) * s.share]
                for t in range(2)
            ],
            axis=1,
        )


def chain(count, product, use, total):
    if count > 8:
        return lax.fori_loop(0, count, lambda d, t: use(d, product(d), t), total)
    ready = product(0)
    for d in range(count):
        later = product(d + 1) if d + 1 < count else None
        total = use(d, ready, total)
        ready = later
    return total


def forward_kernel(s, table, mass_in, *refs):
    given = 2 + (s.count - 1) * s.halves
    units, refs = refs[:given], refs[given:]
    thirds, leaving, (mass, matrix, sems, more_sems), state = refs[0], refs[1:6], refs[6:10], refs[10:]
    row_two, row_one, col_one, col_two, col_three = state
    arrived = Arrivals(s, table, units, matrix, sems, [(mass_in, mass)])
    ones = jnp.ones((8, 2 * s.cols), jnp.bfloat16)
    zero = jnp.zeros((s.hists, 2 * s.cols), jnp.float32)

    def sums(d):
        arrived(d)
        return nt(ones, matrix[d])

    def times(panel):
        return lambda d: nt(panel, matrix[d])

    def first(d, row, total):
        row_one[d] = row
        left = mass[table[d], :, : s.rows] * (1 / row[0:1])
        return total + nn(left.astype(jnp.bfloat16), matrix[d])

    total = chain(s.count, sums, first, zero)
    col_one[...] = total
    target = gather_targets(s, mass)
    panel = (target / total).astype(jnp.bfloat16)

    def second(d, row, total):
        row_two[d] = row
        left = mass[table[d], :, : s.rows] / row
        return total + nn(left.astype(jnp.bfloat16), matrix[d])

    total = chain(s.count, times(panel), second, zero)
    col_two[...] = total
    started = load(state[:4], leaving[:4], more_sems)
    last_panel = (target / total).astype(jnp.bfloat16)

    def third(d, row, total):
        thirds[table[d], :, : s.rows] = row
        left = mass[table[d], :, : s.rows] / row
        return total + nn(left.astype(jnp.bfloat16), matrix[d])

    total = chain(s.count, times(last_panel), third, zero)
    col_three[...] = total
    last = pltpu.make_async_copy(col_three, leaving[4], more_sems.at[4])
    last.start()
    scatter_targets(s, thirds, total)
    for copy in [*started, last]:
        copy.wait()


def backward_kernel(s, table, mass_in, cot_in, thirds_in, *refs):
    given = 2 + (s.count - 1) * s.halves
    state_in, units, refs = refs[:5], refs[5 : 5 + given], refs[5 + given :]
    out, (mass, matrix, sems, more_sems), state, (cot, thirds) = (
        refs[0],
        refs[1:5],
        refs[5:10],
        refs[10:],
    )
    row_two, row_one, col_one, col_two, col_three = state
    early = load([state_in[4], cot_in], [col_three, cot], more_sems)
    paired = [(mass_in, mass), (thirds_in, thirds)]
    arrived = Arrivals(s, table, units, matrix, sems, paired)
    late = [
        pltpu.make_async_copy(state_in[k], state[k], more_sems.at[2 + k]) for k in range(4)
    ]
    for copy in early:
        copy.wait()
    target_cot = gather_targets(s, cot)
    panel = (-target_cot / col_three[...]).astype(jnp.bfloat16)
    zero = jnp.zeros((s.hists, 2 * s.cols), jnp.float32)

    def first_product(d):
        arrived(d)
        if s.count <= 8 and d == s.count - AHEAD:
            for copy in late:
                copy.start()
        return nt(panel, matrix[d])

    def third(d, grad, total):
        k = table[d]
        over = 1 / thirds[k, :, : s.rows]
        term = grad * over
        out[k, :, : s.rows] = term
        rowgrad = -over * (cot[k, :, : s.rows] + term * mass[k, :, : s.rows])
        return total + nn(rowgrad.astype(jnp.bfloat16), matrix[d])

    total = chain(s.count, first_product, third, zero)
    for copy in late:
        if s.count > 8:
            copy.start()
        copy.wait()
    target = gather_targets(s, mass)
    term_two = total / col_two[...]
    panel_two = (-term_two * (target / col_two[...])).astype(jnp.bfloat16)

    def second(d, grad, total):
        k = table[d]
        over = 1 / row_two[d]
        term = grad * over
        out[k, :, : s.rows] += term
        rowgrad = -term * (mass[k, :, : s.rows] * over)
        return total + nn(rowgrad.astype(jnp.bfloat16), matrix[d])

    total = chain(s.count, lambda d: nt(panel_two, matrix[d]), second, zero)
    term_one = total / col_one[...]
    panel_one = (-term_one * (target / col_one[...])).astype(jnp.bfloat16)

    def first(d, grad, carry):
        out[table[d], :, : s.rows] += grad * (1 / row_one[d, 0:1])
        return carry

    chain(s.count, lambda d: nt(panel_one, matrix[d]), first, 0)
    scatter_targets(s, out, term_two + term_one)


def call(kernel, s, products, vmem_outs, hbm_outs, table, arrays, scratch):
    return pl.pallas_call(
        functools.partial(kernel, s),
        out_shape=[*vmem_outs, *hbm_outs],
        in_specs=[pl.BlockSpec(memory_space=pltpu.SMEM)]
        + [pl.BlockSpec(memory_space=pl.ANY)] * len(arrays),
        out_specs=[pl.BlockSpec(memory_space=pltpu.VMEM)] * len(vmem_outs)
        + [pl.BlockSpec(memory_space=pl.ANY)] * len(hbm_outs),
        scratch_shapes=[
            pltpu.VMEM((s.count, s.hists, s.lanes), jnp.float32),
            pltpu.VMEM((s.count, s.rows, 2 * s.cols), jnp.bfloat16),
            pltpu.SemaphoreType.DMA((s.count,)),
            pltpu.SemaphoreType.DMA((8,)),
            *[pltpu.VMEM(state.shape, state.dtype) for state in scratch],
        ],
        cost_estimate=pl.CostEstimate(
            flops=products * 2 * s.count * s.rows * 2 * s.cols * 256,
            bytes_accessed=s.count * s.rows * 2 * s.cols * 4,
            transcendentals=0,
        ),
        compiler_params=pltpu.CompilerParams(vmem_limit_bytes=VMEM),
    )(table, *arrays)


def swap_cores(x):
    return lax.ppermute(x, "tgt", [(0, 1), (1, 0)])


def local(
    source_mass,
    target_mass,
    kernel_tiles,
    tile_cols,
    tile_count,
    source_cotangent,
    target_cotangent,
):
    count = lax.axis_size("src")
    rows, cols_here = source_mass.shape
    share = target_mass.shape[1]
    s = Shape(count, rows, CB_DEV * kernel_tiles.shape[2], cols_here // count, share)
    ring = np.array(ring_order(count), np.int32)
    place = np.argsort(ring).astype(np.int32)
    me = lax.axis_index("src")
    core = lax.axis_index("tgt")
    at = jnp.asarray(place)[me]
    last = count // 2
    away = 2 * core - 1
    steps = [0] + [sign * k for k in range(1, last) for sign in (1, -1)] + [last]
    slots = (at + away * jnp.asarray(steps, jnp.int32)) % count
    table = jnp.concatenate([jnp.asarray(ring)[slots], core[None]]).astype(jnp.int32)

    def onward(x):
        pairs = []
        for p in range(count):
            pairs.append((int(ring[p]) * 2, int(ring[(p + 1) % count]) * 2))
            pairs.append((int(ring[p]) * 2 + 1, int(ring[(p - 1) % count]) * 2 + 1))
        return lax.ppermute(x, ("src", "tgt"), pairs)

    def exchange(x):
        return lax.all_to_all(x, "src", 0, 0, tiled=True)

    def in_order(mine, other, axis):
        return jnp.concatenate(
            [jnp.where(core == 0, mine, other), jnp.where(core == 0, other, mine)], axis=axis
        )

    def by_histogram(source, target):
        target = target.astype(HALF).reshape(share, 2, cols_here)
        mine = lax.dynamic_index_in_dim(target, core, 1, keepdims=False)
        other = lax.dynamic_index_in_dim(target, 1 - core, 1, keepdims=False)
        both = in_order(mine, swap_cores(other), 0).T
        return jnp.concatenate(
            [
                source.astype(HALF).T.reshape(count, s.hists, rows),
                both.reshape(count, s.hists, 2 * share),
            ],
            axis=2,
        )

    mine = dense_blocks(kernel_tiles, tile_cols, tile_count)
    theirs = swap_cores(mine)
    half = rows // s.halves
    cut = lambda x: [x[k * half : (k + 1) * half] for k in range(s.halves)]
    heads = [
        jnp.concatenate([jnp.where(core == 0, a, d), jnp.where(core == 0, b, c)], axis=1)
        for a, b, c, d in zip(cut(mine), cut(theirs), reversed(cut(mine)), reversed(cut(theirs)))
    ]
    heads, mass_here, points_here, cot_here, cot_points = lax.optimization_barrier(
        (heads, source_mass, target_mass[0], source_cotangent, target_cotangent[0])
    )
    units = list(heads)
    mass_message = by_histogram(mass_here, points_here)
    cot_message = by_histogram(cot_here * COT_SCALE, cot_points * COT_SCALE)
    came, swapped = {}, {}
    for step in range(1, last):
        for k in range(s.halves):
            if step > 2:
                heads[k], swapped[step - 2, k] = lax.optimization_barrier(
                    (heads[k], swapped[step - 2, k])
                )
            came[step, k] = heads[k] = onward(heads[k])
            if step == min(2, last - 1) and k == 0:
                heads[k], mass_message, table = lax.optimization_barrier(
                    (heads[k], mass_message, table)
                )
                came[step, k] = heads[k]
            leaving = heads[k]
            if step == last - 1 and k == 0:
                mass = exchange(mass_message).astype(jnp.float32)
                leaving, mass = lax.optimization_barrier((leaving, mass))
            swapped[step, k] = swap_cores(leaving)
    if s.halves == 1:
        piece = lax.dynamic_slice_in_dim(heads[0], core * (rows // 2), rows // 2, 0)
    else:
        piece = heads[0]
    due = [swapped[last - 2, k] for k in range(s.halves)]
    piece, due, cot_message = lax.optimization_barrier((piece, due, cot_message))
    swapped.update({(last - 2, k): due[k] for k in range(s.halves)})
    piece = onward(piece)
    for step in range(1, last):
        for part in (came, swapped):
            units += [part[step, k] for k in range(s.halves)]
    units += [piece, swap_cores(piece)]
    cot = exchange(cot_message).astype(jnp.float32)

    wide = jax.ShapeDtypeStruct((count, s.hists, s.lanes), jnp.float32)
    panel = jax.ShapeDtypeStruct((count, s.hists, rows), jnp.float32)
    sums = jax.ShapeDtypeStruct((count, 8, rows), jnp.float32)
    column = jax.ShapeDtypeStruct((s.hists, 2 * s.cols), jnp.float32)
    states = [panel, sums, column, column, column]
    thirds, *state = call(
        forward_kernel, s, 7, [wide], states, table, [mass, *units], states
    )
    (grads,) = call(
        backward_kernel,
        s,
        5,
        [wide],
        [],
        table,
        [mass, cot, thirds, *state, *units],
        [*states, wide, wide],
    )

    def by_point(pieces):
        turned = pieces.reshape(cols_here, s.lanes).astype(jnp.float32).T
        target = turned[rows:].reshape(2, share, cols_here)
        own = lax.dynamic_index_in_dim(target, core, 0, keepdims=False)
        other = lax.dynamic_index_in_dim(target, 1 - core, 0, keepdims=False)
        other = swap_cores(other.astype(HALF)).astype(jnp.float32)
        return turned[:rows], in_order(own, other, 1)

    row_three, col_three = by_point(exchange(thirds.astype(HALF)))
    source_potential = jnp.log(source_mass / row_three)
    target_potential = jnp.log(target_mass[0] / col_three)
    source_known = source_cotangent / source_mass
    target_known = target_cotangent[0] / target_mass[0]
    back, source_potential, target_potential, source_known, target_known = lax.optimization_barrier(
        (
            exchange(grads.astype(HALF)),
            source_potential,
            target_potential,
            source_known,
            target_known,
        )
    )
    source_term, target_term = by_point(back)
    return (
        source_potential,
        target_potential[None],
        source_known + source_term * (1 / COT_SCALE),
        (target_known + target_term * (1 / COT_SCALE))[None],
    )


def solution(mesh):
    return jax.shard_map(
        local,
        mesh=mesh,
        in_specs=(
            P(("grp", "src"), "tgt"),
            P("tgt", ("grp", "src"), None),
            P(("grp", "src"), "tgt", None, None),
            P(("grp", "src"), "tgt"),
            P(("grp", "src"), "tgt"),
            P(("grp", "src"), "tgt"),
            P("tgt", ("grp", "src"), None),
        ),
        out_specs=(
            P(("grp", "src"), "tgt"),
            P("tgt", ("grp", "src"), None),
            P(("grp", "src"), "tgt"),
            P("tgt", ("grp", "src"), None),
        ),
        check_vma=False,
    )
```

```python
import functools

import jax
import jax.numpy as jnp
import numpy as np
from jax import lax
from jax.experimental import pallas as pl
from jax.experimental.pallas import tpu as pltpu
from jax.sharding import PartitionSpec as P

CB_DEV = 2
HALF = jnp.float16
COT_SCALE = 256.0
VMEM = 56 * 1024 * 1024
AHEAD = 3


def ring_order(count):
    if count == 8:
        return [0, 2, 4, 6, 7, 5, 3, 1]
    return list(range(count))


def dense_blocks(kernel_tiles, tile_cols, tile_count):
    keep = kernel_tiles.shape[1]
    live = jnp.arange(keep, dtype=jnp.int32)[None, :] < tile_count
    hits = (tile_cols[:, :, None] == jnp.arange(CB_DEV, dtype=jnp.int32)) & live[:, :, None]
    blocks = jnp.einsum(
        "rkc,rkab->racb",
        hits.astype(jnp.bfloat16),
        kernel_tiles,
        preferred_element_type=jnp.float32,
    )
    rows, cols = blocks.shape[0] * blocks.shape[1], blocks.shape[2] * blocks.shape[3]
    return blocks.astype(jnp.bfloat16).reshape(rows, cols)


def nt(x, y):
    return lax.dot_general(x, y, (((1,), (1,)), ((), ())), preferred_element_type=jnp.float32)


def nn(x, y):
    return jnp.dot(x, y, preferred_element_type=jnp.float32)


class Shape:
    def __init__(self, count, rows, cols, hists, share):
        self.count = count
        self.rows = rows
        self.cols = cols
        self.hists = hists
        self.share = share
        self.lanes = rows + 2 * share
        self.halves = 2 if count <= 8 else 1


class Arrivals:
    def __init__(self, s, table, units, matrix, sems, paired):
        self.count = s.count
        self.copies = {d: [] for d in range(s.count)}
        core = table[s.count]
        units = iter(units)
        for d in range(s.count):
            parts = 2 if d == s.count - 1 else s.halves
            size = s.rows // parts
            for part in range(parts):
                first = 1 - core if d and d % 2 == 0 else core
                side = first if part == 0 else 1 - first
                start = pl.multiple_of(side * size, size) if parts > 1 else 0
                unit = next(units)
                for t in range(2):
                    target = matrix.at[d, pl.ds(start, size), pl.ds(t * s.cols, s.cols)]
                    self.copies[d].append(pltpu.make_async_copy(unit.at[t], target, sems.at[d]))
        for d in range(s.count):
            k = table[d]
            for source, target in paired:
                place = (k, slice(None), pl.ds(0, target.shape[2]))
                self.copies[d].append(
                    pltpu.make_async_copy(source.at[place], target.at[place], sems.at[d])
                )
        self.ahead = AHEAD if s.count <= 8 else s.count
        for d in range(min(self.ahead, s.count)):
            self.start(d)
        if s.count > 8:
            for d in range(s.count):
                self.wait(d)

    def start(self, d):
        for piece in self.copies[d]:
            piece.start()

    def wait(self, d):
        for piece in self.copies[d]:
            piece.wait()

    def __call__(self, d):
        if self.count <= 8:
            self.wait(d)
            if d + self.ahead < self.count:
                self.start(d + self.ahead)


def load(sources, targets, sems):
    copies = [
        pltpu.make_async_copy(source, target, sems.at[k])
        for k, (source, target) in enumerate(zip(sources, targets))
    ]
    for copy in copies:
        copy.start()
    return copies


def gather_targets(s, pieces, first):
    return jnp.concatenate(
        [
            pieces[i, :, first + t * s.share : first + (t + 1) * s.share]
            for t in range(2)
            for i in range(s.count)
        ],
        axis=1,
    )


def scatter_targets(s, out, values):
    for i in range(s.count):
        out[i, :, s.rows : s.lanes] = jnp.concatenate(
            [
                values[:, t * s.cols + i * s.share : t * s.cols + (i + 1) * s.share]
                for t in range(2)
            ],
            axis=1,
        )


def chain(count, product, use, total):
    if count > 8:
        return lax.fori_loop(0, count, lambda d, t: use(d, product(d), t), total)
    ready = product(0)
    for d in range(count):
        later = product(d + 1) if d + 1 < count else None
        total = use(d, ready, total)
        ready = later
    return total


def forward_kernel(s, table, mass_in, *refs):
    given = 2 + (s.count - 1) * s.halves
    units, refs = refs[:given], refs[given:]
    thirds, leaving, (mass, matrix, sems, more_sems), state = refs[0], refs[1:6], refs[6:10], refs[10:]
    row_two, row_one, col_one, col_two, col_three = state
    arrived = Arrivals(s, table, units, matrix, sems, [(mass_in, mass)])
    ones = jnp.ones((8, 2 * s.cols), jnp.bfloat16)
    zero = jnp.zeros((s.hists, 2 * s.cols), jnp.float32)

    def sums(d):
        arrived(d)
        return nt(ones, matrix[d])

    def times(panel):
        return lambda d: nt(panel, matrix[d])

    def first(d, row, total):
        row_one[d] = row
        left = mass[table[d], :, : s.rows] * (1 / row[0:1])
        return total + nn(left.astype(jnp.bfloat16), matrix[d])

    total = chain(s.count, sums, first, zero)
    col_one[...] = total
    target = gather_targets(s, mass, s.rows)
    panel = (target / total).astype(jnp.bfloat16)

    def second(d, row, total):
        row_two[d] = row
        left = mass[table[d], :, : s.rows] / row
        return total + nn(left.astype(jnp.bfloat16), matrix[d])

    total = chain(s.count, times(panel), second, zero)
    col_two[...] = total
    started = load(state[:4], leaving[:4], more_sems)
    last_panel = (target / total).astype(jnp.bfloat16)

    def third(d, row, total):
        thirds[table[d], :, : s.rows] = row
        left = mass[table[d], :, : s.rows] / row
        return total + nn(left.astype(jnp.bfloat16), matrix[d])

    total = chain(s.count, times(last_panel), third, zero)
    col_three[...] = total
    last = pltpu.make_async_copy(col_three, leaving[4], more_sems.at[4])
    last.start()
    scatter_targets(s, thirds, total)
    for copy in [*started, last]:
        copy.wait()


def backward_kernel(s, table, mass_in, cot_in, thirds_in, *refs):
    given = 2 + (s.count - 1) * s.halves
    state_in, units, refs = refs[:5], refs[5 : 5 + given], refs[5 + given :]
    out, (mass, matrix, sems, more_sems), state, (cot, thirds, cot_points) = (
        refs[0],
        refs[1:5],
        refs[5:10],
        refs[10:],
    )
    row_two, row_one, col_one, col_two, col_three = state
    points = cot_in.at[:, :, pl.ds(s.rows, 2 * s.share)]
    early = load([state_in[4], points], [col_three, cot_points], more_sems)
    paired = [(mass_in, mass), (thirds_in, thirds), (cot_in, cot)]
    arrived = Arrivals(s, table, units, matrix, sems, paired)
    late = [
        pltpu.make_async_copy(state_in[k], state[k], more_sems.at[2 + k]) for k in range(4)
    ]
    for copy in early:
        copy.wait()
    target_cot = gather_targets(s, cot_points, 0)
    panel = (-target_cot / col_three[...]).astype(jnp.bfloat16)
    zero = jnp.zeros((s.hists, 2 * s.cols), jnp.float32)

    def first_product(d):
        arrived(d)
        if s.count <= 8 and d == s.count - AHEAD:
            for copy in late:
                copy.start()
        return nt(panel, matrix[d])

    def third(d, grad, total):
        k = table[d]
        over = 1 / thirds[k, :, : s.rows]
        term = grad * over
        out[k, :, : s.rows] = term
        rowgrad = -over * (cot[k, :, : s.rows] + term * mass[k, :, : s.rows])
        return total + nn(rowgrad.astype(jnp.bfloat16), matrix[d])

    total = chain(s.count, first_product, third, zero)
    for copy in late:
        if s.count > 8:
            copy.start()
        copy.wait()
    target = gather_targets(s, mass, s.rows)
    term_two = total / col_two[...]
    panel_two = (-term_two * (target / col_two[...])).astype(jnp.bfloat16)

    def second(d, grad, total):
        k = table[d]
        over = 1 / row_two[d]
        term = grad * over
        out[k, :, : s.rows] += term
        rowgrad = -term * (mass[k, :, : s.rows] * over)
        return total + nn(rowgrad.astype(jnp.bfloat16), matrix[d])

    total = chain(s.count, lambda d: nt(panel_two, matrix[d]), second, zero)
    term_one = total / col_one[...]
    panel_one = (-term_one * (target / col_one[...])).astype(jnp.bfloat16)

    def first(d, grad, carry):
        out[table[d], :, : s.rows] += grad * (1 / row_one[d, 0:1])
        return carry

    chain(s.count, lambda d: nt(panel_one, matrix[d]), first, 0)
    scatter_targets(s, out, term_two + term_one)


def call(kernel, s, products, vmem_outs, hbm_outs, table, arrays, scratch):
    return pl.pallas_call(
        functools.partial(kernel, s),
        out_shape=[*vmem_outs, *hbm_outs],
        in_specs=[pl.BlockSpec(memory_space=pltpu.SMEM)]
        + [pl.BlockSpec(memory_space=pl.ANY)] * len(arrays),
        out_specs=[pl.BlockSpec(memory_space=pltpu.VMEM)] * len(vmem_outs)
        + [pl.BlockSpec(memory_space=pl.ANY)] * len(hbm_outs),
        scratch_shapes=[
            pltpu.VMEM((s.count, s.hists, s.lanes), jnp.float32),
            pltpu.VMEM((s.count, s.rows, 2 * s.cols), jnp.bfloat16),
            pltpu.SemaphoreType.DMA((s.count,)),
            pltpu.SemaphoreType.DMA((8,)),
            *[pltpu.VMEM(state.shape, state.dtype) for state in scratch],
        ],
        cost_estimate=pl.CostEstimate(
            flops=products * 2 * s.count * s.rows * 2 * s.cols * 256,
            bytes_accessed=s.count * s.rows * 2 * s.cols * 4,
            transcendentals=0,
        ),
        compiler_params=pltpu.CompilerParams(vmem_limit_bytes=VMEM),
    )(table, *arrays)


def swap_cores(x):
    return lax.ppermute(x, "tgt", [(0, 1), (1, 0)])


def local(
    source_mass,
    target_mass,
    kernel_tiles,
    tile_cols,
    tile_count,
    source_cotangent,
    target_cotangent,
):
    count = lax.axis_size("src")
    rows, cols_here = source_mass.shape
    share = target_mass.shape[1]
    s = Shape(count, rows, CB_DEV * kernel_tiles.shape[2], cols_here // count, share)
    ring = np.array(ring_order(count), np.int32)
    place = np.argsort(ring).astype(np.int32)
    me = lax.axis_index("src")
    core = lax.axis_index("tgt")
    at = jnp.asarray(place)[me]
    last = count // 2
    away = 2 * core - 1
    steps = [0] + [sign * k for k in range(1, last) for sign in (1, -1)] + [last]
    slots = (at + away * jnp.asarray(steps, jnp.int32)) % count
    table = jnp.concatenate([jnp.asarray(ring)[slots], core[None]]).astype(jnp.int32)

    def onward(x):
        pairs = []
        for p in range(count):
            pairs.append((int(ring[p]) * 2, int(ring[(p + 1) % count]) * 2))
            pairs.append((int(ring[p]) * 2 + 1, int(ring[(p - 1) % count]) * 2 + 1))
        return lax.ppermute(x, ("src", "tgt"), pairs)

    def exchange(x):
        return lax.all_to_all(x, "src", 0, 0, tiled=True)

    def in_order(mine, other, axis):
        return jnp.concatenate(
            [jnp.where(core == 0, mine, other), jnp.where(core == 0, other, mine)], axis=axis
        )

    def by_histogram(source, target):
        target = target.astype(HALF).reshape(share, 2, cols_here)
        mine = lax.dynamic_index_in_dim(target, core, 1, keepdims=False)
        other = lax.dynamic_index_in_dim(target, 1 - core, 1, keepdims=False)
        both = in_order(mine, swap_cores(other), 0).T
        return jnp.concatenate(
            [
                source.astype(HALF).T.reshape(count, s.hists, rows),
                both.reshape(count, s.hists, 2 * share),
            ],
            axis=2,
        )

    mine = dense_blocks(kernel_tiles, tile_cols, tile_count)
    theirs = swap_cores(mine)
    half = rows // s.halves
    cut = lambda x: [x[k * half : (k + 1) * half] for k in range(s.halves)]
    heads = [
        jnp.stack([jnp.where(core == 0, a, d), jnp.where(core == 0, b, c)])
        for a, b, c, d in zip(cut(mine), cut(theirs), reversed(cut(mine)), reversed(cut(theirs)))
    ]
    heads, mass_here, points_here, cot_here, cot_points = lax.optimization_barrier(
        (heads, source_mass, target_mass[0], source_cotangent, target_cotangent[0])
    )
    units = list(heads)
    mass_message = by_histogram(mass_here, points_here)
    cot_message = by_histogram(cot_here * COT_SCALE, cot_points * COT_SCALE)
    came, swapped = {}, {}
    for step in range(1, last):
        for k in range(s.halves):
            if step > 2:
                heads[k], swapped[step - 2, k] = lax.optimization_barrier(
                    (heads[k], swapped[step - 2, k])
                )
            came[step, k] = heads[k] = onward(heads[k])
            if step == min(2, last - 1) and k == 0:
                heads[k], mass_message, table = lax.optimization_barrier(
                    (heads[k], mass_message, table)
                )
                came[step, k] = heads[k]
            swapped[step, k] = swap_cores(heads[k])
    if s.halves == 1:
        piece = lax.dynamic_slice_in_dim(heads[0], core * (rows // 2), rows // 2, 1)
    else:
        piece = heads[0]
    due = [swapped[last - 2, k] for k in range(s.halves)]
    piece, due, cot_message = lax.optimization_barrier((piece, due, cot_message))
    swapped.update({(last - 2, k): due[k] for k in range(s.halves)})
    piece = onward(piece)
    for step in range(1, last):
        for part in (came, swapped):
            units += [part[step, k] for k in range(s.halves)]
    mass = exchange(mass_message).astype(jnp.float32)
    piece, mass = lax.optimization_barrier((piece, mass))
    units += [piece, swap_cores(piece)]
    cot = exchange(cot_message).astype(jnp.float32)

    wide = jax.ShapeDtypeStruct((count, s.hists, s.lanes), jnp.float32)
    panel = jax.ShapeDtypeStruct((count, s.hists, rows), jnp.float32)
    sums = jax.ShapeDtypeStruct((count, 8, rows), jnp.float32)
    column = jax.ShapeDtypeStruct((s.hists, 2 * s.cols), jnp.float32)
    points = jax.ShapeDtypeStruct((count, s.hists, 2 * share), jnp.float32)
    states = [panel, sums, column, column, column]
    thirds, *state = call(
        forward_kernel, s, 7, [wide], states, table, [mass, *units], states
    )
    (grads,) = call(
        backward_kernel,
        s,
        5,
        [wide],
        [],
        table,
        [mass, cot, thirds, *state, *units],
        [*states, panel, wide, points],
    )

    def by_point(pieces):
        turned = pieces.reshape(cols_here, s.lanes).astype(jnp.float32).T
        target = turned[rows:].reshape(2, share, cols_here)
        own = lax.dynamic_index_in_dim(target, core, 0, keepdims=False)
        other = lax.dynamic_index_in_dim(target, 1 - core, 0, keepdims=False)
        other = swap_cores(other.astype(HALF)).astype(jnp.float32)
        return turned[:rows], in_order(own, other, 1)

    row_three, col_three = by_point(exchange(thirds.astype(HALF)))
    source_potential = jnp.log(source_mass / row_three)
    target_potential = jnp.log(target_mass[0] / col_three)
    source_known = source_cotangent / source_mass
    target_known = target_cotangent[0] / target_mass[0]
    back, source_potential, target_potential, source_known, target_known = lax.optimization_barrier(
        (
            exchange(grads.astype(HALF)),
            source_potential,
            target_potential,
            source_known,
            target_known,
        )
    )
    source_term, target_term = by_point(back)
    return (
        source_potential,
        target_potential[None],
        source_known + source_term * (1 / COT_SCALE),
        (target_known + target_term * (1 / COT_SCALE))[None],
    )


def solution(mesh):
    return jax.shard_map(
        local,
        mesh=mesh,
        in_specs=(
            P(("grp", "src"), "tgt"),
            P("tgt", ("grp", "src"), None),
            P(("grp", "src"), "tgt", None, None),
            P(("grp", "src"), "tgt"),
            P(("grp", "src"), "tgt"),
            P(("grp", "src"), "tgt"),
            P("tgt", ("grp", "src"), None),
        ),
        out_specs=(
            P(("grp", "src"), "tgt"),
            P("tgt", ("grp", "src"), None),
            P(("grp", "src"), "tgt"),
            P("tgt", ("grp", "src"), None),
        ),
        check_vma=False,
    )
```

```python
import functools

import jax
import jax.numpy as jnp
import numpy as np
from jax import lax
from jax.experimental import pallas as pl
from jax.experimental.pallas import tpu as pltpu
from jax.sharding import PartitionSpec as P

CB_DEV = 2
HALF = jnp.float16
COT_SCALE = 256.0
VMEM = 56 * 1024 * 1024
AHEAD = 3


def ring_order(count):
    if count == 8:
        return [0, 2, 4, 6, 7, 5, 3, 1]
    return list(range(count))


def dense_blocks(kernel_tiles, tile_cols, tile_count):
    keep = kernel_tiles.shape[1]
    live = jnp.arange(keep, dtype=jnp.int32)[None, :] < tile_count
    hits = (tile_cols[:, :, None] == jnp.arange(CB_DEV, dtype=jnp.int32)) & live[:, :, None]
    blocks = jnp.einsum(
        "rkc,rkab->racb",
        hits.astype(jnp.bfloat16),
        kernel_tiles,
        preferred_element_type=jnp.float32,
    )
    rows, cols = blocks.shape[0] * blocks.shape[1], blocks.shape[2] * blocks.shape[3]
    return blocks.astype(jnp.bfloat16).reshape(rows, cols)


def nt(x, y):
    return lax.dot_general(x, y, (((1,), (1,)), ((), ())), preferred_element_type=jnp.float32)


def nn(x, y):
    return jnp.dot(x, y, preferred_element_type=jnp.float32)


class Shape:
    def __init__(self, count, rows, cols, hists, share):
        self.count = count
        self.rows = rows
        self.cols = cols
        self.hists = hists
        self.share = share
        self.lanes = rows + 2 * share
        self.halves = 2 if count <= 8 else 1


class Arrivals:
    def __init__(self, s, table, units, matrix, sems, paired):
        self.count = s.count
        self.copies = {d: [] for d in range(s.count)}
        core = table[s.count]
        units = iter(units)
        for d in range(s.count):
            parts = 2 if d == s.count - 1 else s.halves
            size = s.rows // parts
            for part in range(parts):
                first = 1 - core if d and d % 2 == 0 else core
                side = first if part == 0 else 1 - first
                start = pl.multiple_of(side * size, size) if parts > 1 else 0
                unit = next(units)
                for t in range(2):
                    target = matrix.at[d, pl.ds(start, size), pl.ds(t * s.cols, s.cols)]
                    self.copies[d].append(pltpu.make_async_copy(unit.at[t], target, sems.at[d]))
        for d in range(s.count):
            k = table[d]
            for source, target in paired:
                place = (k, slice(None), pl.ds(0, target.shape[2]))
                self.copies[d].append(
                    pltpu.make_async_copy(source.at[place], target.at[place], sems.at[d])
                )
        self.ahead = AHEAD if s.count <= 8 else s.count
        for d in range(min(self.ahead, s.count)):
            self.start(d)
        if s.count > 8:
            for d in range(s.count):
                self.wait(d)

    def start(self, d):
        for piece in self.copies[d]:
            piece.start()

    def wait(self, d):
        for piece in self.copies[d]:
            piece.wait()

    def __call__(self, d):
        if self.count <= 8:
            self.wait(d)
            if d + self.ahead < self.count:
                self.start(d + self.ahead)


def load(sources, targets, sems):
    copies = [
        pltpu.make_async_copy(source, target, sems.at[k])
        for k, (source, target) in enumerate(zip(sources, targets))
    ]
    for copy in copies:
        copy.start()
    return copies


def gather_targets(s, pieces, first):
    return jnp.concatenate(
        [
            pieces[i, :, first + t * s.share : first + (t + 1) * s.share]
            for t in range(2)
            for i in range(s.count)
        ],
        axis=1,
    )


def scatter_targets(s, out, values):
    for i in range(s.count):
        out[i, :, s.rows : s.lanes] = jnp.concatenate(
            [
                values[:, t * s.cols + i * s.share : t * s.cols + (i + 1) * s.share]
                for t in range(2)
            ],
            axis=1,
        )


def chain(count, product, use, total):
    if count > 8:
        return lax.fori_loop(0, count, lambda d, t: use(d, product(d), t), total)
    ready = product(0)
    for d in range(count):
        later = product(d + 1) if d + 1 < count else None
        total = use(d, ready, total)
        ready = later
    return total


def forward_kernel(s, table, mass_in, *refs):
    given = 2 + (s.count - 1) * s.halves
    units, refs = refs[:given], refs[given:]
    thirds, leaving, (mass, matrix, sems, more_sems), state = refs[0], refs[1:6], refs[6:10], refs[10:]
    row_two, row_one, col_one, col_two, col_three = state
    arrived = Arrivals(s, table, units, matrix, sems, [(mass_in, mass)])
    ones = jnp.ones((8, 2 * s.cols), jnp.bfloat16)
    zero = jnp.zeros((s.hists, 2 * s.cols), jnp.float32)

    def sums(d):
        arrived(d)
        return nt(ones, matrix[d])

    def times(panel):
        return lambda d: nt(panel, matrix[d])

    def first(d, row, total):
        row_one[d] = row
        left = mass[table[d], :, : s.rows] * (1 / row[0:1])
        return total + nn(left.astype(jnp.bfloat16), matrix[d])

    total = chain(s.count, sums, first, zero)
    col_one[...] = total
    target = gather_targets(s, mass, s.rows)
    panel = (target / total).astype(jnp.bfloat16)

    def second(d, row, total):
        row_two[d] = row
        left = mass[table[d], :, : s.rows] / row
        return total + nn(left.astype(jnp.bfloat16), matrix[d])

    total = chain(s.count, times(panel), second, zero)
    col_two[...] = total
    started = load(state[:4], leaving[:4], more_sems)
    last_panel = (target / total).astype(jnp.bfloat16)

    def third(d, row, total):
        thirds[table[d], :, : s.rows] = row
        left = mass[table[d], :, : s.rows] / row
        return total + nn(left.astype(jnp.bfloat16), matrix[d])

    total = chain(s.count, times(last_panel), third, zero)
    col_three[...] = total
    last = pltpu.make_async_copy(col_three, leaving[4], more_sems.at[4])
    last.start()
    scatter_targets(s, thirds, total)
    for copy in [*started, last]:
        copy.wait()


def backward_kernel(s, table, mass_in, cot_in, thirds_in, *refs):
    given = 2 + (s.count - 1) * s.halves
    state_in, units, refs = refs[:5], refs[5 : 5 + given], refs[5 + given :]
    out, (mass, matrix, sems, more_sems), state, (cot, thirds, cot_points) = (
        refs[0],
        refs[1:5],
        refs[5:10],
        refs[10:],
    )
    row_two, row_one, col_one, col_two, col_three = state
    points = cot_in.at[:, :, pl.ds(s.rows, 2 * s.share)]
    early = load([state_in[4], points], [col_three, cot_points], more_sems)
    paired = [(mass_in, mass), (thirds_in, thirds), (cot_in, cot)]
    arrived = Arrivals(s, table, units, matrix, sems, paired)
    late = [
        pltpu.make_async_copy(state_in[k], state[k], more_sems.at[2 + k]) for k in range(4)
    ]
    for copy in early:
        copy.wait()
    target_cot = gather_targets(s, cot_points, 0)
    panel = (-target_cot / col_three[...]).astype(jnp.bfloat16)
    zero = jnp.zeros((s.hists, 2 * s.cols), jnp.float32)

    def first_product(d):
        arrived(d)
        if s.count <= 8 and d == s.count - AHEAD:
            for copy in late:
                copy.start()
        return nt(panel, matrix[d])

    def third(d, grad, total):
        k = table[d]
        over = 1 / thirds[k, :, : s.rows]
        term = grad * over
        out[k, :, : s.rows] = term
        rowgrad = -over * (cot[k, :, : s.rows] + term * mass[k, :, : s.rows])
        return total + nn(rowgrad.astype(jnp.bfloat16), matrix[d])

    total = chain(s.count, first_product, third, zero)
    for copy in late:
        if s.count > 8:
            copy.start()
        copy.wait()
    target = gather_targets(s, mass, s.rows)
    term_two = total / col_two[...]
    panel_two = (-term_two * (target / col_two[...])).astype(jnp.bfloat16)

    def second(d, grad, total):
        k = table[d]
        over = 1 / row_two[d]
        term = grad * over
        out[k, :, : s.rows] += term
        rowgrad = -term * (mass[k, :, : s.rows] * over)
        return total + nn(rowgrad.astype(jnp.bfloat16), matrix[d])

    total = chain(s.count, lambda d: nt(panel_two, matrix[d]), second, zero)
    term_one = total / col_one[...]
    panel_one = (-term_one * (target / col_one[...])).astype(jnp.bfloat16)

    def first(d, grad, carry):
        out[table[d], :, : s.rows] += grad * (1 / row_one[d, 0:1])
        return carry

    chain(s.count, lambda d: nt(panel_one, matrix[d]), first, 0)
    scatter_targets(s, out, term_two + term_one)


def call(kernel, s, products, vmem_outs, hbm_outs, table, arrays, scratch):
    return pl.pallas_call(
        functools.partial(kernel, s),
        out_shape=[*vmem_outs, *hbm_outs],
        in_specs=[pl.BlockSpec(memory_space=pltpu.SMEM)]
        + [pl.BlockSpec(memory_space=pl.ANY)] * len(arrays),
        out_specs=[pl.BlockSpec(memory_space=pltpu.VMEM)] * len(vmem_outs)
        + [pl.BlockSpec(memory_space=pl.ANY)] * len(hbm_outs),
        scratch_shapes=[
            pltpu.VMEM((s.count, s.hists, s.lanes), jnp.float32),
            pltpu.VMEM((s.count, s.rows, 2 * s.cols), jnp.bfloat16),
            pltpu.SemaphoreType.DMA((s.count,)),
            pltpu.SemaphoreType.DMA((8,)),
            *[pltpu.VMEM(state.shape, state.dtype) for state in scratch],
        ],
        cost_estimate=pl.CostEstimate(
            flops=products * 2 * s.count * s.rows * 2 * s.cols * 256,
            bytes_accessed=s.count * s.rows * 2 * s.cols * 4,
            transcendentals=0,
        ),
        compiler_params=pltpu.CompilerParams(vmem_limit_bytes=VMEM),
    )(table, *arrays)


def swap_cores(x):
    return lax.ppermute(x, "tgt", [(0, 1), (1, 0)])


def local(
    source_mass,
    target_mass,
    kernel_tiles,
    tile_cols,
    tile_count,
    source_cotangent,
    target_cotangent,
):
    count = lax.axis_size("src")
    rows, cols_here = source_mass.shape
    share = target_mass.shape[1]
    s = Shape(count, rows, CB_DEV * kernel_tiles.shape[2], cols_here // count, share)
    ring = np.array(ring_order(count), np.int32)
    place = np.argsort(ring).astype(np.int32)
    me = lax.axis_index("src")
    core = lax.axis_index("tgt")
    at = jnp.asarray(place)[me]
    last = count // 2
    away = 2 * core - 1
    steps = [0] + [sign * k for k in range(1, last) for sign in (1, -1)] + [last]
    slots = (at + away * jnp.asarray(steps, jnp.int32)) % count
    table = jnp.concatenate([jnp.asarray(ring)[slots], core[None]]).astype(jnp.int32)

    def onward(x):
        pairs = []
        for p in range(count):
            pairs.append((int(ring[p]) * 2, int(ring[(p + 1) % count]) * 2))
            pairs.append((int(ring[p]) * 2 + 1, int(ring[(p - 1) % count]) * 2 + 1))
        return lax.ppermute(x, ("src", "tgt"), pairs)

    def exchange(x):
        return lax.all_to_all(x, "src", 0, 0, tiled=True)

    def in_order(mine, other, axis):
        return jnp.concatenate(
            [jnp.where(core == 0, mine, other), jnp.where(core == 0, other, mine)], axis=axis
        )

    def by_histogram(source, target):
        target = target.astype(HALF).reshape(share, 2, cols_here)
        mine = lax.dynamic_index_in_dim(target, core, 1, keepdims=False)
        other = lax.dynamic_index_in_dim(target, 1 - core, 1, keepdims=False)
        both = in_order(mine, swap_cores(other), 0).T
        return jnp.concatenate(
            [
                source.astype(HALF).T.reshape(count, s.hists, rows),
                both.reshape(count, s.hists, 2 * share),
            ],
            axis=2,
        )

    mine = dense_blocks(kernel_tiles, tile_cols, tile_count)
    theirs = swap_cores(mine)
    half = rows // s.halves
    cut = lambda x: [x[k * half : (k + 1) * half] for k in range(s.halves)]
    own_set = (jnp.arange(2, dtype=jnp.int32) == core)[:, None, None]
    pick = lambda x: [jnp.where(core == 0, *pair) for pair in zip(cut(x), reversed(cut(x)))]
    heads = [jnp.where(own_set, a[None], b[None]) for a, b in zip(pick(mine), pick(theirs))]
    heads, mass_here, points_here, cot_here, cot_points = lax.optimization_barrier(
        (heads, source_mass, target_mass[0], source_cotangent, target_cotangent[0])
    )
    units = list(heads)
    mass_message = by_histogram(mass_here, points_here)
    cot_message = by_histogram(cot_here * COT_SCALE, cot_points * COT_SCALE)
    came, swapped = {}, {}
    for step in range(1, last):
        for k in range(s.halves):
            if step > 2:
                heads[k], swapped[step - 2, k] = lax.optimization_barrier(
                    (heads[k], swapped[step - 2, k])
                )
            came[step, k] = heads[k] = onward(heads[k])
            swapped[step, k] = swap_cores(heads[k])
            if step == min(2, last - 1) and k == 0:
                swapped[step, k], mass_message, table = lax.optimization_barrier(
                    (swapped[step, k], mass_message, table)
                )
    if s.halves == 1:
        piece = lax.dynamic_slice_in_dim(heads[0], core * (rows // 2), rows // 2, 1)
    else:
        piece = heads[0]
    due = [swapped[last - 2, k] for k in range(s.halves)]
    piece, due, cot_message = lax.optimization_barrier((piece, due, cot_message))
    swapped.update({(last - 2, k): due[k] for k in range(s.halves)})
    piece = onward(piece)
    for step in range(1, last):
        for part in (came, swapped):
            units += [part[step, k] for k in range(s.halves)]
    mass = exchange(mass_message).astype(jnp.float32)
    piece, mass = lax.optimization_barrier((piece, mass))
    units += [piece, swap_cores(piece)]
    cot = exchange(cot_message).astype(jnp.float32)

    wide = jax.ShapeDtypeStruct((count, s.hists, s.lanes), jnp.float32)
    panel = jax.ShapeDtypeStruct((count, s.hists, rows), jnp.float32)
    sums = jax.ShapeDtypeStruct((count, 8, rows), jnp.float32)
    column = jax.ShapeDtypeStruct((s.hists, 2 * s.cols), jnp.float32)
    points = jax.ShapeDtypeStruct((count, s.hists, 2 * share), jnp.float32)
    states = [panel, sums, column, column, column]
    thirds, *state = call(
        forward_kernel, s, 7, [wide], states, table, [mass, *units], states
    )
    (grads,) = call(
        backward_kernel,
        s,
        5,
        [wide],
        [],
        table,
        [mass, cot, thirds, *state, *units],
        [*states, panel, wide, points],
    )

    def by_point(pieces):
        turned = pieces.reshape(cols_here, s.lanes).astype(jnp.float32).T
        target = turned[rows:].reshape(2, share, cols_here)
        own = lax.dynamic_index_in_dim(target, core, 0, keepdims=False)
        other = lax.dynamic_index_in_dim(target, 1 - core, 0, keepdims=False)
        other = swap_cores(other.astype(HALF)).astype(jnp.float32)
        return turned[:rows], in_order(own, other, 1)

    row_three, col_three = by_point(exchange(thirds.astype(HALF)))
    source_potential = jnp.log(source_mass / row_three)
    target_potential = jnp.log(target_mass[0] / col_three)
    source_known = source_cotangent / source_mass
    target_known = target_cotangent[0] / target_mass[0]
    back, source_potential, target_potential, source_known, target_known = lax.optimization_barrier(
        (
            exchange(grads.astype(HALF)),
            source_potential,
            target_potential,
            source_known,
            target_known,
        )
    )
    source_term, target_term = by_point(back)
    return (
        source_potential,
        target_potential[None],
        source_known + source_term * (1 / COT_SCALE),
        (target_known + target_term * (1 / COT_SCALE))[None],
    )


def solution(mesh):
    return jax.shard_map(
        local,
        mesh=mesh,
        in_specs=(
            P(("grp", "src"), "tgt"),
            P("tgt", ("grp", "src"), None),
            P(("grp", "src"), "tgt", None, None),
            P(("grp", "src"), "tgt"),
            P(("grp", "src"), "tgt"),
            P(("grp", "src"), "tgt"),
            P("tgt", ("grp", "src"), None),
        ),
        out_specs=(
            P(("grp", "src"), "tgt"),
            P("tgt", ("grp", "src"), None),
            P(("grp", "src"), "tgt"),
            P("tgt", ("grp", "src"), None),
        ),
        check_vma=False,
    )
```

```python
import functools

import jax
import jax.numpy as jnp
import numpy as np
from jax import lax
from jax.experimental import pallas as pl
from jax.experimental.pallas import tpu as pltpu
from jax.sharding import PartitionSpec as P

CB_DEV = 2
HALF = jnp.float16
COT_SCALE = 256.0
VMEM = 56 * 1024 * 1024
AHEAD = 3


def ring_order(count):
    if count == 8:
        return [0, 2, 4, 6, 7, 5, 3, 1]
    return list(range(count))


def dense_blocks(kernel_tiles, tile_cols, tile_count):
    keep = kernel_tiles.shape[1]
    live = jnp.arange(keep, dtype=jnp.int32)[None, :] < tile_count
    hits = (tile_cols[:, :, None] == jnp.arange(CB_DEV, dtype=jnp.int32)) & live[:, :, None]
    blocks = jnp.einsum(
        "rkc,rkab->racb",
        hits.astype(jnp.bfloat16),
        kernel_tiles,
        preferred_element_type=jnp.float32,
    )
    rows, cols = blocks.shape[0] * blocks.shape[1], blocks.shape[2] * blocks.shape[3]
    return blocks.astype(jnp.bfloat16).reshape(rows, cols)


def nt(x, y):
    return lax.dot_general(x, y, (((1,), (1,)), ((), ())), preferred_element_type=jnp.float32)


def nn(x, y):
    return jnp.dot(x, y, preferred_element_type=jnp.float32)


class Shape:
    def __init__(self, count, rows, cols, hists, share):
        self.count = count
        self.rows = rows
        self.cols = cols
        self.hists = hists
        self.share = share
        self.lanes = rows + 2 * share
        self.halves = 2 if count <= 8 else 1


class Arrivals:
    def __init__(self, s, table, units, matrix, sems, paired):
        self.count = s.count
        self.copies = {d: [] for d in range(s.count)}
        core = table[s.count]
        units = iter(units)
        for d in range(s.count):
            parts = 2 if d == s.count - 1 else s.halves
            size = s.rows // parts
            for part in range(parts):
                first = 1 - core if d and d % 2 == 0 else core
                side = first if part == 0 else 1 - first
                start = pl.multiple_of(side * size, size) if parts > 1 else 0
                unit = next(units)
                for t in range(2):
                    target = matrix.at[d, pl.ds(start, size), pl.ds(t * s.cols, s.cols)]
                    self.copies[d].append(pltpu.make_async_copy(unit.at[t], target, sems.at[d]))
        for d in range(s.count):
            k = table[d]
            for source, target in paired:
                place = (k, slice(None), pl.ds(0, target.shape[2]))
                self.copies[d].append(
                    pltpu.make_async_copy(source.at[place], target.at[place], sems.at[d])
                )
        self.ahead = AHEAD if s.count <= 8 else s.count
        for d in range(min(self.ahead, s.count)):
            self.start(d)
        if s.count > 8:
            for d in range(s.count):
                self.wait(d)

    def start(self, d):
        for piece in self.copies[d]:
            piece.start()

    def wait(self, d):
        for piece in self.copies[d]:
            piece.wait()

    def __call__(self, d):
        if self.count <= 8:
            self.wait(d)
            if d + self.ahead < self.count:
                self.start(d + self.ahead)


def load(sources, targets, sems):
    copies = [
        pltpu.make_async_copy(source, target, sems.at[k])
        for k, (source, target) in enumerate(zip(sources, targets))
    ]
    for copy in copies:
        copy.start()
    return copies


def gather_targets(s, pieces, first):
    return jnp.concatenate(
        [
            pieces[i, :, first + t * s.share : first + (t + 1) * s.share]
            for t in range(2)
            for i in range(s.count)
        ],
        axis=1,
    )


def scatter_targets(s, out, values):
    for i in range(s.count):
        out[i, :, s.rows : s.lanes] = jnp.concatenate(
            [
                values[:, t * s.cols + i * s.share : t * s.cols + (i + 1) * s.share]
                for t in range(2)
            ],
            axis=1,
        )


def chain(count, product, use, total):
    if count > 8:
        return lax.fori_loop(0, count, lambda d, t: use(d, product(d), t), total)
    ready = product(0)
    for d in range(count):
        later = product(d + 1) if d + 1 < count else None
        total = use(d, ready, total)
        ready = later
    return total


def forward_kernel(s, table, mass_in, *refs):
    given = 2 + (s.count - 1) * s.halves
    units, refs = refs[:given], refs[given:]
    thirds, leaving, (mass, matrix, sems, more_sems), state = refs[0], refs[1:6], refs[6:10], refs[10:]
    row_two, row_one, col_one, col_two, col_three = state
    arrived = Arrivals(s, table, units, matrix, sems, [(mass_in, mass)])
    ones = jnp.ones((8, 2 * s.cols), jnp.bfloat16)
    zero = jnp.zeros((s.hists, 2 * s.cols), jnp.float32)

    def sums(d):
        arrived(d)
        return nt(ones, matrix[d])

    def times(panel):
        return lambda d: nt(panel, matrix[d])

    def first(d, row, total):
        row_one[d] = row
        left = mass[table[d], :, : s.rows] * (1 / row[0:1])
        return total + nn(left.astype(jnp.bfloat16), matrix[d])

    total = chain(s.count, sums, first, zero)
    col_one[...] = total
    target = gather_targets(s, mass, s.rows)
    panel = (target / total).astype(jnp.bfloat16)

    def second(d, row, total):
        row_two[d] = row
        left = mass[table[d], :, : s.rows] / row
        return total + nn(left.astype(jnp.bfloat16), matrix[d])

    total = chain(s.count, times(panel), second, zero)
    col_two[...] = total
    started = load(state[:4], leaving[:4], more_sems)
    last_panel = (target / total).astype(jnp.bfloat16)

    def third(d, row, total):
        thirds[table[d], :, : s.rows] = row
        left = mass[table[d], :, : s.rows] / row
        return total + nn(left.astype(jnp.bfloat16), matrix[d])

    total = chain(s.count, times(last_panel), third, zero)
    col_three[...] = total
    last = pltpu.make_async_copy(col_three, leaving[4], more_sems.at[4])
    last.start()
    scatter_targets(s, thirds, total)
    for copy in [*started, last]:
        copy.wait()


def backward_kernel(s, table, mass_in, cot_in, thirds_in, *refs):
    given = 2 + (s.count - 1) * s.halves
    state_in, units, refs = refs[:5], refs[5 : 5 + given], refs[5 + given :]
    out, (mass, matrix, sems, more_sems), state, (cot, thirds, cot_points) = (
        refs[0],
        refs[1:5],
        refs[5:10],
        refs[10:],
    )
    row_two, row_one, col_one, col_two, col_three = state
    points = cot_in.at[:, :, pl.ds(s.rows, 2 * s.share)]
    early = load([state_in[4], points], [col_three, cot_points], more_sems)
    paired = [(mass_in, mass), (thirds_in, thirds), (cot_in, cot)]
    arrived = Arrivals(s, table, units, matrix, sems, paired)
    late = [
        pltpu.make_async_copy(state_in[k], state[k], more_sems.at[2 + k]) for k in range(4)
    ]
    for copy in early:
        copy.wait()
    target_cot = gather_targets(s, cot_points, 0)
    panel = (-target_cot / col_three[...]).astype(jnp.bfloat16)
    zero = jnp.zeros((s.hists, 2 * s.cols), jnp.float32)

    def first_product(d):
        arrived(d)
        if s.count <= 8 and d == s.count - AHEAD:
            for copy in late:
                copy.start()
        return nt(panel, matrix[d])

    def third(d, grad, total):
        k = table[d]
        over = 1 / thirds[k, :, : s.rows]
        term = grad * over
        out[k, :, : s.rows] = term
        rowgrad = -over * (cot[k, :, : s.rows] + term * mass[k, :, : s.rows])
        return total + nn(rowgrad.astype(jnp.bfloat16), matrix[d])

    total = chain(s.count, first_product, third, zero)
    for copy in late:
        if s.count > 8:
            copy.start()
        copy.wait()
    target = gather_targets(s, mass, s.rows)
    term_two = total / col_two[...]
    panel_two = (-term_two * (target / col_two[...])).astype(jnp.bfloat16)

    def second(d, grad, total):
        k = table[d]
        over = 1 / row_two[d]
        term = grad * over
        out[k, :, : s.rows] += term
        rowgrad = -term * (mass[k, :, : s.rows] * over)
        return total + nn(rowgrad.astype(jnp.bfloat16), matrix[d])

    total = chain(s.count, lambda d: nt(panel_two, matrix[d]), second, zero)
    term_one = total / col_one[...]
    panel_one = (-term_one * (target / col_one[...])).astype(jnp.bfloat16)

    def first(d, grad, carry):
        out[table[d], :, : s.rows] += grad * (1 / row_one[d, 0:1])
        return carry

    chain(s.count, lambda d: nt(panel_one, matrix[d]), first, 0)
    scatter_targets(s, out, term_two + term_one)


def call(kernel, s, products, vmem_outs, hbm_outs, table, arrays, scratch):
    return pl.pallas_call(
        functools.partial(kernel, s),
        out_shape=[*vmem_outs, *hbm_outs],
        in_specs=[pl.BlockSpec(memory_space=pltpu.SMEM)]
        + [pl.BlockSpec(memory_space=pl.ANY)] * len(arrays),
        out_specs=[pl.BlockSpec(memory_space=pltpu.VMEM)] * len(vmem_outs)
        + [pl.BlockSpec(memory_space=pl.ANY)] * len(hbm_outs),
        scratch_shapes=[
            pltpu.VMEM((s.count, s.hists, s.lanes), jnp.float32),
            pltpu.VMEM((s.count, s.rows, 2 * s.cols), jnp.bfloat16),
            pltpu.SemaphoreType.DMA((s.count,)),
            pltpu.SemaphoreType.DMA((8,)),
            *[pltpu.VMEM(state.shape, state.dtype) for state in scratch],
        ],
        cost_estimate=pl.CostEstimate(
            flops=products * 2 * s.count * s.rows * 2 * s.cols * 256,
            bytes_accessed=s.count * s.rows * 2 * s.cols * 4,
            transcendentals=0,
        ),
        compiler_params=pltpu.CompilerParams(vmem_limit_bytes=VMEM),
    )(table, *arrays)


def swap_cores(x):
    return lax.ppermute(x, "tgt", [(0, 1), (1, 0)])


def local(
    source_mass,
    target_mass,
    kernel_tiles,
    tile_cols,
    tile_count,
    source_cotangent,
    target_cotangent,
):
    count = lax.axis_size("src")
    rows, cols_here = source_mass.shape
    share = target_mass.shape[1]
    s = Shape(count, rows, CB_DEV * kernel_tiles.shape[2], cols_here // count, share)
    ring = np.array(ring_order(count), np.int32)
    place = np.argsort(ring).astype(np.int32)
    me = lax.axis_index("src")
    core = lax.axis_index("tgt")
    at = jnp.asarray(place)[me]
    last = count // 2
    away = 2 * core - 1
    steps = [0] + [sign * k for k in range(1, last) for sign in (1, -1)] + [last]
    slots = (at + away * jnp.asarray(steps, jnp.int32)) % count
    table = jnp.concatenate([jnp.asarray(ring)[slots], core[None]]).astype(jnp.int32)

    def onward(x):
        pairs = []
        for p in range(count):
            pairs.append((int(ring[p]) * 2, int(ring[(p + 1) % count]) * 2))
            pairs.append((int(ring[p]) * 2 + 1, int(ring[(p - 1) % count]) * 2 + 1))
        return lax.ppermute(x, ("src", "tgt"), pairs)

    def exchange(x):
        return lax.all_to_all(x, "src", 0, 0, tiled=True)

    def in_order(mine, other, axis):
        return jnp.concatenate(
            [jnp.where(core == 0, mine, other), jnp.where(core == 0, other, mine)], axis=axis
        )

    def by_histogram(source, target):
        target = target.astype(HALF).reshape(share, 2, cols_here)
        mine = lax.dynamic_index_in_dim(target, core, 1, keepdims=False)
        other = lax.dynamic_index_in_dim(target, 1 - core, 1, keepdims=False)
        both = in_order(mine, swap_cores(other), 0).T
        return jnp.concatenate(
            [
                source.astype(HALF).T.reshape(count, s.hists, rows),
                both.reshape(count, s.hists, 2 * share),
            ],
            axis=2,
        )

    mine = dense_blocks(kernel_tiles, tile_cols, tile_count)
    theirs = swap_cores(mine)
    half = rows // s.halves
    cut = lambda x: [x[k * half : (k + 1) * half] for k in range(s.halves)]
    own_set = (jnp.arange(2, dtype=jnp.int32) == core)[:, None, None]
    pick = lambda x: [jnp.where(core == 0, *pair) for pair in zip(cut(x), reversed(cut(x)))]
    heads = [jnp.where(own_set, a[None], b[None]) for a, b in zip(pick(mine), pick(theirs))]
    heads, mass_here, points_here, cot_here, cot_points = lax.optimization_barrier(
        (heads, source_mass, target_mass[0], source_cotangent, target_cotangent[0])
    )
    units = list(heads)
    mass_message = by_histogram(mass_here, points_here)
    cot_message = by_histogram(cot_here * COT_SCALE, cot_points * COT_SCALE)
    came, swapped = {}, {}
    for step in range(1, last):
        for k in range(s.halves):
            if step > 2:
                heads[k], swapped[step - 2, k] = lax.optimization_barrier(
                    (heads[k], swapped[step - 2, k])
                )
            came[step, k] = heads[k] = onward(heads[k])
            if step == min(2, last - 1) and k == 0:
                heads[k], mass_message, table = lax.optimization_barrier(
                    (heads[k], mass_message, table)
                )
                came[step, k] = heads[k]
            swapped[step, k] = swap_cores(heads[k])
    if s.halves == 1:
        piece = lax.dynamic_slice_in_dim(heads[0], core * (rows // 2), rows // 2, 1)
    else:
        piece = heads[0]
    due = [swapped[last - 2, k] for k in range(s.halves)]
    piece, due, cot_message = lax.optimization_barrier((piece, due, cot_message))
    swapped.update({(last - 2, k): due[k] for k in range(s.halves)})
    piece = onward(piece)
    for step in range(1, last):
        for part in (came, swapped):
            units += [part[step, k] for k in range(s.halves)]
    mass = exchange(mass_message).astype(jnp.float32)
    piece, mass = lax.optimization_barrier((piece, mass))
    units += [piece, swap_cores(piece)]
    cot = exchange(cot_message).astype(jnp.float32)

    wide = jax.ShapeDtypeStruct((count, s.hists, s.lanes), jnp.float32)
    panel = jax.ShapeDtypeStruct((count, s.hists, rows), jnp.float32)
    sums = jax.ShapeDtypeStruct((count, 8, rows), jnp.float32)
    column = jax.ShapeDtypeStruct((s.hists, 2 * s.cols), jnp.float32)
    points = jax.ShapeDtypeStruct((count, s.hists, 2 * share), jnp.float32)
    states = [panel, sums, column, column, column]
    thirds, *state = call(
        forward_kernel, s, 7, [wide], states, table, [mass, *units], states
    )
    (grads,) = call(
        backward_kernel,
        s,
        5,
        [wide],
        [],
        table,
        [mass, cot, thirds, *state, *units],
        [*states, panel, wide, points],
    )

    def by_point(pieces):
        turned = pieces.reshape(cols_here, s.lanes).astype(jnp.float32).T
        target = turned[rows:].reshape(2, share, cols_here)
        own = lax.dynamic_index_in_dim(target, core, 0, keepdims=False)
        other = lax.dynamic_index_in_dim(target, 1 - core, 0, keepdims=False)
        other = swap_cores(other.astype(HALF)).astype(jnp.float32)
        return turned[:rows], in_order(own, other, 1)

    row_three, col_three = by_point(exchange(thirds.astype(HALF)))
    source_potential = jnp.log(source_mass / row_three)
    target_potential = jnp.log(target_mass[0] / col_three)
    source_known = source_cotangent / source_mass
    target_known = target_cotangent[0] / target_mass[0]
    back, source_potential, target_potential, source_known, target_known = lax.optimization_barrier(
        (
            exchange(grads.astype(HALF)),
            source_potential,
            target_potential,
            source_known,
            target_known,
        )
    )
    source_term, target_term = by_point(back)
    return (
        source_potential,
        target_potential[None],
        source_known + source_term * (1 / COT_SCALE),
        (target_known + target_term * (1 / COT_SCALE))[None],
    )


def solution(mesh):
    return jax.shard_map(
        local,
        mesh=mesh,
        in_specs=(
            P(("grp", "src"), "tgt"),
            P("tgt", ("grp", "src"), None),
            P(("grp", "src"), "tgt", None, None),
            P(("grp", "src"), "tgt"),
            P(("grp", "src"), "tgt"),
            P(("grp", "src"), "tgt"),
            P("tgt", ("grp", "src"), None),
        ),
        out_specs=(
            P(("grp", "src"), "tgt"),
            P("tgt", ("grp", "src"), None),
            P(("grp", "src"), "tgt"),
            P("tgt", ("grp", "src"), None),
        ),
        check_vma=False,
    )
```

```python
import functools

import jax
import jax.numpy as jnp
import numpy as np
from jax import lax
from jax.experimental import pallas as pl
from jax.experimental.pallas import tpu as pltpu
from jax.sharding import PartitionSpec as P

CB_DEV = 2
HALF = jnp.float16
COT_SCALE = 256.0
VMEM = 56 * 1024 * 1024
AHEAD = 8


def ring_order(count):
    if count == 8:
        return [0, 2, 4, 6, 7, 5, 3, 1]
    return list(range(count))


def dense_blocks(kernel_tiles, tile_cols, tile_count):
    keep = kernel_tiles.shape[1]
    live = jnp.arange(keep, dtype=jnp.int32)[None, :] < tile_count
    hits = (tile_cols[:, :, None] == jnp.arange(CB_DEV, dtype=jnp.int32)) & live[:, :, None]
    blocks = jnp.einsum(
        "rkc,rkab->racb",
        hits.astype(jnp.bfloat16),
        kernel_tiles,
        preferred_element_type=jnp.float32,
    )
    rows, cols = blocks.shape[0] * blocks.shape[1], blocks.shape[2] * blocks.shape[3]
    return blocks.astype(jnp.bfloat16).reshape(rows, cols)


def nt(x, y):
    return lax.dot_general(x, y, (((1,), (1,)), ((), ())), preferred_element_type=jnp.float32)


def nn(x, y):
    return jnp.dot(x, y, preferred_element_type=jnp.float32)


class Shape:
    def __init__(self, count, rows, cols, hists, share):
        self.count = count
        self.rows = rows
        self.cols = cols
        self.hists = hists
        self.share = share
        self.lanes = rows + 2 * share
        self.halves = 2 if count <= 8 else 1


class Arrivals:
    def __init__(self, s, table, units, matrix, sems, paired):
        self.count = s.count
        self.copies = {d: [] for d in range(s.count)}
        core = table[s.count]
        units = iter(units)
        for d in range(s.count):
            parts = 2 if d == s.count - 1 else s.halves
            size = s.rows // parts
            for part in range(parts):
                first = 1 - core if d and d % 2 == 0 else core
                side = first if part == 0 else 1 - first
                start = pl.multiple_of(side * size, size) if parts > 1 else 0
                unit = next(units)
                for t in range(2):
                    target = matrix.at[d, pl.ds(start, size), pl.ds(t * s.cols, s.cols)]
                    self.copies[d].append(pltpu.make_async_copy(unit.at[t], target, sems.at[d]))
        for d in range(s.count):
            k = table[d]
            for source, target in paired:
                place = (k, slice(None), pl.ds(0, target.shape[2]))
                self.copies[d].append(
                    pltpu.make_async_copy(source.at[place], target.at[place], sems.at[d])
                )
        self.ahead = AHEAD if s.count <= 8 else s.count
        for d in range(min(self.ahead, s.count)):
            self.start(d)
        if s.count > 8:
            for d in range(s.count):
                self.wait(d)

    def start(self, d):
        for piece in self.copies[d]:
            piece.start()

    def wait(self, d):
        for piece in self.copies[d]:
            piece.wait()

    def __call__(self, d):
        if self.count <= 8:
            self.wait(d)
            if d + self.ahead < self.count:
                self.start(d + self.ahead)


def load(sources, targets, sems):
    copies = [
        pltpu.make_async_copy(source, target, sems.at[k])
        for k, (source, target) in enumerate(zip(sources, targets))
    ]
    for copy in copies:
        copy.start()
    return copies


def gather_targets(s, pieces, first):
    return jnp.concatenate(
        [
            pieces[i, :, first + t * s.share : first + (t + 1) * s.share]
            for t in range(2)
            for i in range(s.count)
        ],
        axis=1,
    )


def scatter_targets(s, out, values):
    for i in range(s.count):
        out[i, :, s.rows : s.lanes] = jnp.concatenate(
            [
                values[:, t * s.cols + i * s.share : t * s.cols + (i + 1) * s.share]
                for t in range(2)
            ],
            axis=1,
        )


def chain(count, product, use, total):
    if count > 8:
        return lax.fori_loop(0, count, lambda d, t: use(d, product(d), t), total)
    ready = product(0)
    for d in range(count):
        later = product(d + 1) if d + 1 < count else None
        total = use(d, ready, total)
        ready = later
    return total


def forward_kernel(s, table, mass_in, *refs):
    given = 2 + (s.count - 1) * s.halves
    units, refs = refs[:given], refs[given:]
    thirds, leaving, (mass, matrix, sems, more_sems), state = refs[0], refs[1:6], refs[6:10], refs[10:]
    row_two, row_one, col_one, col_two, col_three = state
    arrived = Arrivals(s, table, units, matrix, sems, [(mass_in, mass)])
    ones = jnp.ones((8, 2 * s.cols), jnp.bfloat16)
    zero = jnp.zeros((s.hists, 2 * s.cols), jnp.float32)

    def sums(d):
        arrived(d)
        return nt(ones, matrix[d])

    def times(panel):
        return lambda d: nt(panel, matrix[d])

    def first(d, row, total):
        row_one[d] = row
        left = mass[table[d], :, : s.rows] * (1 / row[0:1])
        return total + nn(left.astype(jnp.bfloat16), matrix[d])

    total = chain(s.count, sums, first, zero)
    col_one[...] = total
    target = gather_targets(s, mass, s.rows)
    panel = (target / total).astype(jnp.bfloat16)

    def second(d, row, total):
        row_two[d] = row
        left = mass[table[d], :, : s.rows] / row
        return total + nn(left.astype(jnp.bfloat16), matrix[d])

    total = chain(s.count, times(panel), second, zero)
    col_two[...] = total
    started = load(state[:4], leaving[:4], more_sems)
    last_panel = (target / total).astype(jnp.bfloat16)

    def third(d, row, total):
        thirds[table[d], :, : s.rows] = row
        left = mass[table[d], :, : s.rows] / row
        return total + nn(left.astype(jnp.bfloat16), matrix[d])

    total = chain(s.count, times(last_panel), third, zero)
    col_three[...] = total
    last = pltpu.make_async_copy(col_three, leaving[4], more_sems.at[4])
    last.start()
    scatter_targets(s, thirds, total)
    for copy in [*started, last]:
        copy.wait()


def backward_kernel(s, table, mass_in, cot_in, thirds_in, *refs):
    given = 2 + (s.count - 1) * s.halves
    state_in, units, refs = refs[:5], refs[5 : 5 + given], refs[5 + given :]
    out, (mass, matrix, sems, more_sems), state, (cot, thirds, cot_points) = (
        refs[0],
        refs[1:5],
        refs[5:10],
        refs[10:],
    )
    row_two, row_one, col_one, col_two, col_three = state
    points = cot_in.at[:, :, pl.ds(s.rows, 2 * s.share)]
    early = load([state_in[4], points], [col_three, cot_points], more_sems)
    paired = [(mass_in, mass), (thirds_in, thirds), (cot_in, cot)]
    arrived = Arrivals(s, table, units, matrix, sems, paired)
    late = [
        pltpu.make_async_copy(state_in[k], state[k], more_sems.at[2 + k]) for k in range(4)
    ]
    for copy in early:
        copy.wait()
    target_cot = gather_targets(s, cot_points, 0)
    panel = (-target_cot / col_three[...]).astype(jnp.bfloat16)
    zero = jnp.zeros((s.hists, 2 * s.cols), jnp.float32)

    def first_product(d):
        arrived(d)
        if s.count <= 8 and d == max(s.count - AHEAD, 0):
            for copy in late:
                copy.start()
        return nt(panel, matrix[d])

    def third(d, grad, total):
        k = table[d]
        over = 1 / thirds[k, :, : s.rows]
        term = grad * over
        out[k, :, : s.rows] = term
        rowgrad = -over * (cot[k, :, : s.rows] + term * mass[k, :, : s.rows])
        return total + nn(rowgrad.astype(jnp.bfloat16), matrix[d])

    total = chain(s.count, first_product, third, zero)
    for copy in late:
        if s.count > 8:
            copy.start()
        copy.wait()
    target = gather_targets(s, mass, s.rows)
    term_two = total / col_two[...]
    panel_two = (-term_two * (target / col_two[...])).astype(jnp.bfloat16)

    def second(d, grad, total):
        k = table[d]
        over = 1 / row_two[d]
        term = grad * over
        out[k, :, : s.rows] += term
        rowgrad = -term * (mass[k, :, : s.rows] * over)
        return total + nn(rowgrad.astype(jnp.bfloat16), matrix[d])

    total = chain(s.count, lambda d: nt(panel_two, matrix[d]), second, zero)
    term_one = total / col_one[...]
    panel_one = (-term_one * (target / col_one[...])).astype(jnp.bfloat16)

    def first(d, grad, carry):
        out[table[d], :, : s.rows] += grad * (1 / row_one[d, 0:1])
        return carry

    chain(s.count, lambda d: nt(panel_one, matrix[d]), first, 0)
    scatter_targets(s, out, term_two + term_one)


def call(kernel, s, products, vmem_outs, hbm_outs, table, arrays, scratch):
    return pl.pallas_call(
        functools.partial(kernel, s),
        out_shape=[*vmem_outs, *hbm_outs],
        in_specs=[pl.BlockSpec(memory_space=pltpu.SMEM)]
        + [pl.BlockSpec(memory_space=pl.ANY)] * len(arrays),
        out_specs=[pl.BlockSpec(memory_space=pltpu.VMEM)] * len(vmem_outs)
        + [pl.BlockSpec(memory_space=pl.ANY)] * len(hbm_outs),
        scratch_shapes=[
            pltpu.VMEM((s.count, s.hists, s.lanes), jnp.float32),
            pltpu.VMEM((s.count, s.rows, 2 * s.cols), jnp.bfloat16),
            pltpu.SemaphoreType.DMA((s.count,)),
            pltpu.SemaphoreType.DMA((8,)),
            *[pltpu.VMEM(state.shape, state.dtype) for state in scratch],
        ],
        cost_estimate=pl.CostEstimate(
            flops=products * 2 * s.count * s.rows * 2 * s.cols * 256,
            bytes_accessed=s.count * s.rows * 2 * s.cols * 4,
            transcendentals=0,
        ),
        compiler_params=pltpu.CompilerParams(vmem_limit_bytes=VMEM),
    )(table, *arrays)


def swap_cores(x):
    return lax.ppermute(x, "tgt", [(0, 1), (1, 0)])


def local(
    source_mass,
    target_mass,
    kernel_tiles,
    tile_cols,
    tile_count,
    source_cotangent,
    target_cotangent,
):
    count = lax.axis_size("src")
    rows, cols_here = source_mass.shape
    share = target_mass.shape[1]
    s = Shape(count, rows, CB_DEV * kernel_tiles.shape[2], cols_here // count, share)
    ring = np.array(ring_order(count), np.int32)
    place = np.argsort(ring).astype(np.int32)
    me = lax.axis_index("src")
    core = lax.axis_index("tgt")
    at = jnp.asarray(place)[me]
    last = count // 2
    away = 2 * core - 1
    steps = [0] + [sign * k for k in range(1, last) for sign in (1, -1)] + [last]
    slots = (at + away * jnp.asarray(steps, jnp.int32)) % count
    table = jnp.concatenate([jnp.asarray(ring)[slots], core[None]]).astype(jnp.int32)

    def onward(x):
        pairs = []
        for p in range(count):
            pairs.append((int(ring[p]) * 2, int(ring[(p + 1) % count]) * 2))
            pairs.append((int(ring[p]) * 2 + 1, int(ring[(p - 1) % count]) * 2 + 1))
        return lax.ppermute(x, ("src", "tgt"), pairs)

    def exchange(x):
        return lax.all_to_all(x, "src", 0, 0, tiled=True)

    def in_order(mine, other, axis):
        return jnp.concatenate(
            [jnp.where(core == 0, mine, other), jnp.where(core == 0, other, mine)], axis=axis
        )

    def by_histogram(source, target):
        target = target.astype(HALF).reshape(share, 2, cols_here)
        mine = lax.dynamic_index_in_dim(target, core, 1, keepdims=False)
        other = lax.dynamic_index_in_dim(target, 1 - core, 1, keepdims=False)
        both = in_order(mine, swap_cores(other), 0).T
        return jnp.concatenate(
            [
                source.astype(HALF).T.reshape(count, s.hists, rows),
                both.reshape(count, s.hists, 2 * share),
            ],
            axis=2,
        )

    mine = dense_blocks(kernel_tiles, tile_cols, tile_count)
    theirs = swap_cores(mine)
    half = rows // s.halves
    cut = lambda x: [x[k * half : (k + 1) * half] for k in range(s.halves)]
    own_set = (jnp.arange(2, dtype=jnp.int32) == core)[:, None, None]
    pick = lambda x: [jnp.where(core == 0, *pair) for pair in zip(cut(x), reversed(cut(x)))]
    heads = [jnp.where(own_set, a[None], b[None]) for a, b in zip(pick(mine), pick(theirs))]
    heads, mass_here, points_here, cot_here, cot_points = lax.optimization_barrier(
        (heads, source_mass, target_mass[0], source_cotangent, target_cotangent[0])
    )
    units = list(heads)
    mass_message = by_histogram(mass_here, points_here)
    cot_message = by_histogram(cot_here * COT_SCALE, cot_points * COT_SCALE)
    came, swapped = {}, {}
    for step in range(1, last):
        for k in range(s.halves):
            if step > 2:
                heads[k], swapped[step - 2, k] = lax.optimization_barrier(
                    (heads[k], swapped[step - 2, k])
                )
            came[step, k] = heads[k] = onward(heads[k])
            if step == min(2, last - 1) and k == 0:
                heads[k], mass_message, table = lax.optimization_barrier(
                    (heads[k], mass_message, table)
                )
                came[step, k] = heads[k]
            swapped[step, k] = swap_cores(heads[k])
    if s.halves == 1:
        piece = lax.dynamic_slice_in_dim(heads[0], core * (rows // 2), rows // 2, 1)
    else:
        piece = heads[0]
    due = [swapped[last - 2, k] for k in range(s.halves)]
    piece, due, cot_message = lax.optimization_barrier((piece, due, cot_message))
    swapped.update({(last - 2, k): due[k] for k in range(s.halves)})
    piece = onward(piece)
    for step in range(1, last):
        for part in (came, swapped):
            units += [part[step, k] for k in range(s.halves)]
    mass = exchange(mass_message).astype(jnp.float32)
    piece, mass = lax.optimization_barrier((piece, mass))
    units += [piece, swap_cores(piece)]
    cot = exchange(cot_message).astype(jnp.float32)

    wide = jax.ShapeDtypeStruct((count, s.hists, s.lanes), jnp.float32)
    panel = jax.ShapeDtypeStruct((count, s.hists, rows), jnp.float32)
    sums = jax.ShapeDtypeStruct((count, 8, rows), jnp.float32)
    column = jax.ShapeDtypeStruct((s.hists, 2 * s.cols), jnp.float32)
    points = jax.ShapeDtypeStruct((count, s.hists, 2 * share), jnp.float32)
    states = [panel, sums, column, column, column]
    thirds, *state = call(
        forward_kernel, s, 7, [wide], states, table, [mass, *units], states
    )
    (grads,) = call(
        backward_kernel,
        s,
        5,
        [wide],
        [],
        table,
        [mass, cot, thirds, *state, *units],
        [*states, panel, wide, points],
    )

    def by_point(pieces):
        turned = pieces.reshape(cols_here, s.lanes).astype(jnp.float32).T
        target = turned[rows:].reshape(2, share, cols_here)
        own = lax.dynamic_index_in_dim(target, core, 0, keepdims=False)
        other = lax.dynamic_index_in_dim(target, 1 - core, 0, keepdims=False)
        other = swap_cores(other.astype(HALF)).astype(jnp.float32)
        return turned[:rows], in_order(own, other, 1)

    row_three, col_three = by_point(exchange(thirds.astype(HALF)))
    source_potential = jnp.log(source_mass / row_three)
    target_potential = jnp.log(target_mass[0] / col_three)
    source_known = source_cotangent / source_mass
    target_known = target_cotangent[0] / target_mass[0]
    back, source_potential, target_potential, source_known, target_known = lax.optimization_barrier(
        (
            exchange(grads.astype(HALF)),
            source_potential,
            target_potential,
            source_known,
            target_known,
        )
    )
    source_term, target_term = by_point(back)
    return (
        source_potential,
        target_potential[None],
        source_known + source_term * (1 / COT_SCALE),
        (target_known + target_term * (1 / COT_SCALE))[None],
    )


def solution(mesh):
    return jax.shard_map(
        local,
        mesh=mesh,
        in_specs=(
            P(("grp", "src"), "tgt"),
            P("tgt", ("grp", "src"), None),
            P(("grp", "src"), "tgt", None, None),
            P(("grp", "src"), "tgt"),
            P(("grp", "src"), "tgt"),
            P(("grp", "src"), "tgt"),
            P("tgt", ("grp", "src"), None),
        ),
        out_specs=(
            P(("grp", "src"), "tgt"),
            P("tgt", ("grp", "src"), None),
            P(("grp", "src"), "tgt"),
            P("tgt", ("grp", "src"), None),
        ),
        check_vma=False,
    )
```

```python
import functools

import jax
import jax.numpy as jnp
import numpy as np
from jax import lax
from jax.experimental import pallas as pl
from jax.experimental.pallas import tpu as pltpu
from jax.sharding import PartitionSpec as P

CB_DEV = 2
HALF = jnp.float16
COT_SCALE = 256.0
VMEM = 56 * 1024 * 1024
AHEAD = 3


def ring_order(count):
    if count == 8:
        return [0, 2, 4, 6, 7, 5, 3, 1]
    return list(range(count))


def dense_blocks(kernel_tiles, tile_cols, tile_count):
    keep = kernel_tiles.shape[1]
    live = jnp.arange(keep, dtype=jnp.int32)[None, :] < tile_count
    hits = (tile_cols[:, :, None] == jnp.arange(CB_DEV, dtype=jnp.int32)) & live[:, :, None]
    blocks = jnp.einsum(
        "rkc,rkab->racb",
        hits.astype(jnp.bfloat16),
        kernel_tiles,
        preferred_element_type=jnp.float32,
    )
    rows, cols = blocks.shape[0] * blocks.shape[1], blocks.shape[2] * blocks.shape[3]
    return blocks.astype(jnp.bfloat16).reshape(rows, cols)


def nt(x, y):
    return lax.dot_general(x, y, (((1,), (1,)), ((), ())), preferred_element_type=jnp.float32)


def nn(x, y):
    return jnp.dot(x, y, preferred_element_type=jnp.float32)


class Shape:
    def __init__(self, count, rows, cols, hists, share):
        self.count = count
        self.rows = rows
        self.cols = cols
        self.hists = hists
        self.share = share
        self.lanes = rows + 2 * share
        self.halves = 2 if count <= 8 else 1


class Arrivals:
    def __init__(self, s, table, units, matrix, sems, paired):
        self.count = s.count
        self.copies = {d: [] for d in range(s.count)}
        core = table[s.count]
        units = iter(units)
        for d in range(s.count):
            parts = 2 if d == s.count - 1 else s.halves
            size = s.rows // parts
            for part in range(parts):
                first = 1 - core if d and d % 2 == 0 else core
                side = first if part == 0 else 1 - first
                start = pl.multiple_of(side * size, size) if parts > 1 else 0
                unit = next(units)
                for t in range(2):
                    target = matrix.at[d, pl.ds(start, size), pl.ds(t * s.cols, s.cols)]
                    self.copies[d].append(pltpu.make_async_copy(unit.at[t], target, sems.at[d]))
        for d in range(s.count):
            k = table[d]
            for source, target in paired:
                place = (k, slice(None), pl.ds(0, target.shape[2]))
                self.copies[d].append(
                    pltpu.make_async_copy(source.at[place], target.at[place], sems.at[d])
                )
        self.ahead = AHEAD if s.count <= 8 else s.count
        for d in range(min(self.ahead, s.count)):
            self.start(d)
        if s.count > 8:
            for d in range(s.count):
                self.wait(d)

    def start(self, d):
        for piece in self.copies[d]:
            piece.start()

    def wait(self, d):
        for piece in self.copies[d]:
            piece.wait()

    def __call__(self, d):
        if self.count <= 8:
            self.wait(d)
            if d + self.ahead < self.count:
                self.start(d + self.ahead)


def load(sources, targets, sems):
    copies = [
        pltpu.make_async_copy(source, target, sems.at[k])
        for k, (source, target) in enumerate(zip(sources, targets))
    ]
    for copy in copies:
        copy.start()
    return copies


def gather_targets(s, pieces, first):
    return jnp.concatenate(
        [
            pieces[i, :, first + t * s.share : first + (t + 1) * s.share]
            for t in range(2)
            for i in range(s.count)
        ],
        axis=1,
    )


def scatter_targets(s, out, values):
    for i in range(s.count):
        out[i, :, s.rows : s.lanes] = jnp.concatenate(
            [
                values[:, t * s.cols + i * s.share : t * s.cols + (i + 1) * s.share]
                for t in range(2)
            ],
            axis=1,
        )


def chain(count, product, use, total):
    if count > 8:
        return lax.fori_loop(0, count, lambda d, t: use(d, product(d), t), total)
    ready = product(0)
    for d in range(count):
        later = product(d + 1) if d + 1 < count else None
        total = use(d, ready, total)
        ready = later
    return total


def forward_kernel(s, table, mass_in, *refs):
    given = 2 + (s.count - 1) * s.halves
    units, refs = refs[:given], refs[given:]
    thirds, leaving, (mass, matrix, sems, more_sems), state = refs[0], refs[1:6], refs[6:10], refs[10:]
    row_two, row_one, col_one, col_two, col_three = state
    arrived = Arrivals(s, table, units, matrix, sems, [(mass_in, mass)])
    ones = jnp.ones((8, 2 * s.cols), jnp.bfloat16)
    zero = jnp.zeros((s.hists, 2 * s.cols), jnp.float32)

    def sums(d):
        arrived(d)
        return nt(ones, matrix[d])

    def times(panel):
        return lambda d: nt(panel, matrix[d])

    def first(d, row, total):
        row_one[d] = row
        left = mass[table[d], :, : s.rows] * (1 / row[0:1])
        return total + nn(left.astype(jnp.bfloat16), matrix[d])

    total = chain(s.count, sums, first, zero)
    col_one[...] = total
    target = gather_targets(s, mass, s.rows)
    panel = (target / total).astype(jnp.bfloat16)

    def second(d, row, total):
        row_two[d] = row
        left = mass[table[d], :, : s.rows] / row
        return total + nn(left.astype(jnp.bfloat16), matrix[d])

    total = chain(s.count, times(panel), second, zero)
    col_two[...] = total
    started = load(state[:4], leaving[:4], more_sems)
    last_panel = (target / total).astype(jnp.bfloat16)

    def third(d, row, total):
        thirds[table[d], :, : s.rows] = row
        left = mass[table[d], :, : s.rows] / row
        return total + nn(left.astype(jnp.bfloat16), matrix[d])

    total = chain(s.count, times(last_panel), third, zero)
    col_three[...] = total
    last = pltpu.make_async_copy(col_three, leaving[4], more_sems.at[4])
    last.start()
    scatter_targets(s, thirds, total)
    for copy in [*started, last]:
        copy.wait()


def backward_kernel(s, table, mass_in, cot_in, thirds_in, *refs):
    given = 2 + (s.count - 1) * s.halves
    state_in, units, refs = refs[:5], refs[5 : 5 + given], refs[5 + given :]
    out, (mass, matrix, sems, more_sems), state, (cot, thirds, cot_points) = (
        refs[0],
        refs[1:5],
        refs[5:10],
        refs[10:],
    )
    row_two, row_one, col_one, col_two, col_three = state
    points = cot_in.at[:, :, pl.ds(s.rows, 2 * s.share)]
    early = load([state_in[4], points, state_in[3]], [col_three, cot_points, col_two], more_sems)
    paired = [(mass_in, mass), (thirds_in, thirds), (cot_in, cot)]
    arrived = Arrivals(s, table, units, matrix, sems, paired)
    late = [
        pltpu.make_async_copy(state_in[k], state[k], more_sems.at[3 + k]) for k in range(3)
    ]
    for copy in early:
        copy.wait()
    target_cot = gather_targets(s, cot_points, 0)
    panel = (-target_cot / col_three[...]).astype(jnp.bfloat16)
    zero = jnp.zeros((s.hists, 2 * s.cols), jnp.float32)

    def first_product(d):
        arrived(d)
        return nt(panel, matrix[d])

    def third(d, grad, total):
        k = table[d]
        over = 1 / thirds[k, :, : s.rows]
        term = grad * over
        out[k, :, : s.rows] = term
        rowgrad = -over * (cot[k, :, : s.rows] + term * mass[k, :, : s.rows])
        return total + nn(rowgrad.astype(jnp.bfloat16), matrix[d])

    total = chain(s.count, first_product, third, zero)
    for copy in late:
        copy.start()
    target = gather_targets(s, mass, s.rows)
    term_two = total / col_two[...]
    panel_two = (-term_two * (target / col_two[...])).astype(jnp.bfloat16)
    for copy in late:
        copy.wait()

    def second(d, grad, total):
        k = table[d]
        over = 1 / row_two[d]
        term = grad * over
        out[k, :, : s.rows] += term
        rowgrad = -term * (mass[k, :, : s.rows] * over)
        return total + nn(rowgrad.astype(jnp.bfloat16), matrix[d])

    total = chain(s.count, lambda d: nt(panel_two, matrix[d]), second, zero)
    term_one = total / col_one[...]
    panel_one = (-term_one * (target / col_one[...])).astype(jnp.bfloat16)

    def first(d, grad, carry):
        out[table[d], :, : s.rows] += grad * (1 / row_one[d, 0:1])
        return carry

    chain(s.count, lambda d: nt(panel_one, matrix[d]), first, 0)
    scatter_targets(s, out, term_two + term_one)


def call(kernel, s, products, vmem_outs, hbm_outs, table, arrays, scratch):
    return pl.pallas_call(
        functools.partial(kernel, s),
        out_shape=[*vmem_outs, *hbm_outs],
        in_specs=[pl.BlockSpec(memory_space=pltpu.SMEM)]
        + [pl.BlockSpec(memory_space=pl.ANY)] * len(arrays),
        out_specs=[pl.BlockSpec(memory_space=pltpu.VMEM)] * len(vmem_outs)
        + [pl.BlockSpec(memory_space=pl.ANY)] * len(hbm_outs),
        scratch_shapes=[
            pltpu.VMEM((s.count, s.hists, s.lanes), jnp.float32),
            pltpu.VMEM((s.count, s.rows, 2 * s.cols), jnp.bfloat16),
            pltpu.SemaphoreType.DMA((s.count,)),
            pltpu.SemaphoreType.DMA((8,)),
            *[pltpu.VMEM(state.shape, state.dtype) for state in scratch],
        ],
        cost_estimate=pl.CostEstimate(
            flops=products * 2 * s.count * s.rows * 2 * s.cols * 256,
            bytes_accessed=s.count * s.rows * 2 * s.cols * 4,
            transcendentals=0,
        ),
        compiler_params=pltpu.CompilerParams(vmem_limit_bytes=VMEM),
    )(table, *arrays)


def swap_cores(x):
    return lax.ppermute(x, "tgt", [(0, 1), (1, 0)])


def local(
    source_mass,
    target_mass,
    kernel_tiles,
    tile_cols,
    tile_count,
    source_cotangent,
    target_cotangent,
):
    count = lax.axis_size("src")
    rows, cols_here = source_mass.shape
    share = target_mass.shape[1]
    s = Shape(count, rows, CB_DEV * kernel_tiles.shape[2], cols_here // count, share)
    ring = np.array(ring_order(count), np.int32)
    place = np.argsort(ring).astype(np.int32)
    me = lax.axis_index("src")
    core = lax.axis_index("tgt")
    at = jnp.asarray(place)[me]
    last = count // 2
    away = 2 * core - 1
    steps = [0] + [sign * k for k in range(1, last) for sign in (1, -1)] + [last]
    slots = (at + away * jnp.asarray(steps, jnp.int32)) % count
    table = jnp.concatenate([jnp.asarray(ring)[slots], core[None]]).astype(jnp.int32)

    def onward(x):
        pairs = []
        for p in range(count):
            pairs.append((int(ring[p]) * 2, int(ring[(p + 1) % count]) * 2))
            pairs.append((int(ring[p]) * 2 + 1, int(ring[(p - 1) % count]) * 2 + 1))
        return lax.ppermute(x, ("src", "tgt"), pairs)

    def exchange(x):
        return lax.all_to_all(x, "src", 0, 0, tiled=True)

    def in_order(mine, other, axis):
        return jnp.concatenate(
            [jnp.where(core == 0, mine, other), jnp.where(core == 0, other, mine)], axis=axis
        )

    def by_histogram(source, target):
        target = target.astype(HALF).reshape(share, 2, cols_here)
        mine = lax.dynamic_index_in_dim(target, core, 1, keepdims=False)
        other = lax.dynamic_index_in_dim(target, 1 - core, 1, keepdims=False)
        both = in_order(mine, swap_cores(other), 0).T
        return jnp.concatenate(
            [
                source.astype(HALF).T.reshape(count, s.hists, rows),
                both.reshape(count, s.hists, 2 * share),
            ],
            axis=2,
        )

    mine = dense_blocks(kernel_tiles, tile_cols, tile_count)
    theirs = swap_cores(mine)
    half = rows // s.halves
    cut = lambda x: [x[k * half : (k + 1) * half] for k in range(s.halves)]
    own_set = (jnp.arange(2, dtype=jnp.int32) == core)[:, None, None]
    pick = lambda x: [jnp.where(core == 0, *pair) for pair in zip(cut(x), reversed(cut(x)))]
    heads = [jnp.where(own_set, a[None], b[None]) for a, b in zip(pick(mine), pick(theirs))]
    heads, mass_here, points_here, cot_here, cot_points = lax.optimization_barrier(
        (heads, source_mass, target_mass[0], source_cotangent, target_cotangent[0])
    )
    units = list(heads)
    mass_message = by_histogram(mass_here, points_here)
    cot_message = by_histogram(cot_here * COT_SCALE, cot_points * COT_SCALE)
    came, swapped = {}, {}
    for step in range(1, last):
        for k in range(s.halves):
            if step > 2:
                heads[k], swapped[step - 2, k] = lax.optimization_barrier(
                    (heads[k], swapped[step - 2, k])
                )
            came[step, k] = heads[k] = onward(heads[k])
            if step == min(2, last - 1) and k == 0:
                heads[k], mass_message, table = lax.optimization_barrier(
                    (heads[k], mass_message, table)
                )
                came[step, k] = heads[k]
            swapped[step, k] = swap_cores(heads[k])
    if s.halves == 1:
        piece = lax.dynamic_slice_in_dim(heads[0], core * (rows // 2), rows // 2, 1)
    else:
        piece = heads[0]
    due = [swapped[last - 2, k] for k in range(s.halves)]
    piece, due, cot_message = lax.optimization_barrier((piece, due, cot_message))
    swapped.update({(last - 2, k): due[k] for k in range(s.halves)})
    piece = onward(piece)
    for step in range(1, last):
        for part in (came, swapped):
            units += [part[step, k] for k in range(s.halves)]
    mass = exchange(mass_message).astype(jnp.float32)
    piece, mass = lax.optimization_barrier((piece, mass))
    units += [piece, swap_cores(piece)]
    cot = exchange(cot_message).astype(jnp.float32)

    wide = jax.ShapeDtypeStruct((count, s.hists, s.lanes), jnp.float32)
    panel = jax.ShapeDtypeStruct((count, s.hists, rows), jnp.float32)
    sums = jax.ShapeDtypeStruct((count, 8, rows), jnp.float32)
    column = jax.ShapeDtypeStruct((s.hists, 2 * s.cols), jnp.float32)
    points = jax.ShapeDtypeStruct((count, s.hists, 2 * share), jnp.float32)
    states = [panel, sums, column, column, column]
    thirds, *state = call(
        forward_kernel, s, 7, [wide], states, table, [mass, *units], states
    )
    (grads,) = call(
        backward_kernel,
        s,
        5,
        [wide],
        [],
        table,
        [mass, cot, thirds, *state, *units],
        [*states, panel, wide, points],
    )

    def by_point(pieces):
        turned = pieces.reshape(cols_here, s.lanes).astype(jnp.float32).T
        target = turned[rows:].reshape(2, share, cols_here)
        own = lax.dynamic_index_in_dim(target, core, 0, keepdims=False)
        other = lax.dynamic_index_in_dim(target, 1 - core, 0, keepdims=False)
        other = swap_cores(other.astype(HALF)).astype(jnp.float32)
        return turned[:rows], in_order(own, other, 1)

    row_three, col_three = by_point(exchange(thirds.astype(HALF)))
    source_potential = jnp.log(source_mass / row_three)
    target_potential = jnp.log(target_mass[0] / col_three)
    source_known = source_cotangent / source_mass
    target_known = target_cotangent[0] / target_mass[0]
    back, source_potential, target_potential, source_known, target_known = lax.optimization_barrier(
        (
            exchange(grads.astype(HALF)),
            source_potential,
            target_potential,
            source_known,
            target_known,
        )
    )
    source_term, target_term = by_point(back)
    return (
        source_potential,
        target_potential[None],
        source_known + source_term * (1 / COT_SCALE),
        (target_known + target_term * (1 / COT_SCALE))[None],
    )


def solution(mesh):
    return jax.shard_map(
        local,
        mesh=mesh,
        in_specs=(
            P(("grp", "src"), "tgt"),
            P("tgt", ("grp", "src"), None),
            P(("grp", "src"), "tgt", None, None),
            P(("grp", "src"), "tgt"),
            P(("grp", "src"), "tgt"),
            P(("grp", "src"), "tgt"),
            P("tgt", ("grp", "src"), None),
        ),
        out_specs=(
            P(("grp", "src"), "tgt"),
            P("tgt", ("grp", "src"), None),
            P(("grp", "src"), "tgt"),
            P("tgt", ("grp", "src"), None),
        ),
        check_vma=False,
    )
```

```python
import functools

import jax
import jax.numpy as jnp
import numpy as np
from jax import lax
from jax.experimental import pallas as pl
from jax.experimental.pallas import tpu as pltpu
from jax.sharding import PartitionSpec as P

CB_DEV = 2
HALF = jnp.float16
COT_SCALE = 256.0
VMEM = 56 * 1024 * 1024
AHEAD = 3


def ring_order(count):
    if count == 8:
        return [0, 2, 4, 6, 7, 5, 3, 1]
    return list(range(count))


def dense_blocks(kernel_tiles, tile_cols, tile_count):
    keep = kernel_tiles.shape[1]
    live = jnp.arange(keep, dtype=jnp.int32)[None, :] < tile_count
    hits = (tile_cols[:, :, None] == jnp.arange(CB_DEV, dtype=jnp.int32)) & live[:, :, None]
    blocks = jnp.einsum(
        "rkc,rkab->racb",
        hits.astype(jnp.bfloat16),
        kernel_tiles,
        preferred_element_type=jnp.float32,
    )
    rows, cols = blocks.shape[0] * blocks.shape[1], blocks.shape[2] * blocks.shape[3]
    return blocks.astype(jnp.bfloat16).reshape(rows, cols)


def nt(x, y):
    return lax.dot_general(x, y, (((1,), (1,)), ((), ())), preferred_element_type=jnp.float32)


def nn(x, y):
    return jnp.dot(x, y, preferred_element_type=jnp.float32)


class Shape:
    def __init__(self, count, rows, cols, hists, share):
        self.count = count
        self.rows = rows
        self.cols = cols
        self.hists = hists
        self.share = share
        self.lanes = rows + 2 * share
        self.halves = 2 if count <= 8 else 1


class Arrivals:
    def __init__(self, s, table, units, matrix, sems, paired):
        self.count = s.count
        self.copies = {d: [] for d in range(s.count)}
        core = table[s.count]
        units = iter(units)
        for d in range(s.count):
            parts = 2 if d == s.count - 1 else s.halves
            size = s.rows // parts
            for part in range(parts):
                first = 1 - core if d and d % 2 == 0 else core
                side = first if part == 0 else 1 - first
                start = pl.multiple_of(side * size, size) if parts > 1 else 0
                unit = next(units)
                for t in range(2):
                    target = matrix.at[d, pl.ds(start, size), pl.ds(t * s.cols, s.cols)]
                    self.copies[d].append(pltpu.make_async_copy(unit.at[t], target, sems.at[d]))
        for d in range(s.count):
            k = table[d]
            for source, target in paired:
                place = (k, slice(None), pl.ds(0, target.shape[2]))
                self.copies[d].append(
                    pltpu.make_async_copy(source.at[place], target.at[place], sems.at[d])
                )
        self.ahead = AHEAD if s.count <= 8 else s.count
        for d in range(min(self.ahead, s.count)):
            self.start(d)
        if s.count > 8:
            for d in range(s.count):
                self.wait(d)

    def start(self, d):
        for piece in self.copies[d]:
            piece.start()

    def wait(self, d):
        for piece in self.copies[d]:
            piece.wait()

    def __call__(self, d):
        if self.count <= 8:
            self.wait(d)
            if d + self.ahead < self.count:
                self.start(d + self.ahead)


def load(sources, targets, sems):
    copies = [
        pltpu.make_async_copy(source, target, sems.at[k])
        for k, (source, target) in enumerate(zip(sources, targets))
    ]
    for copy in copies:
        copy.start()
    return copies


def gather_targets(s, pieces, first):
    return jnp.concatenate(
        [
            pieces[i, :, first + t * s.share : first + (t + 1) * s.share]
            for t in range(2)
            for i in range(s.count)
        ],
        axis=1,
    )


def scatter_targets(s, out, values):
    for i in range(s.count):
        out[i, :, s.rows : s.lanes] = jnp.concatenate(
            [
                values[:, t * s.cols + i * s.share : t * s.cols + (i + 1) * s.share]
                for t in range(2)
            ],
            axis=1,
        )


def chain(count, product, use, total):
    if count > 8:
        return lax.fori_loop(0, count, lambda d, t: use(d, product(d), t), total)
    ready = product(0)
    for d in range(count):
        later = product(d + 1) if d + 1 < count else None
        total = use(d, ready, total)
        ready = later
    return total


def forward_kernel(s, table, mass_in, *refs):
    given = 2 + (s.count - 1) * s.halves
    units, refs = refs[:given], refs[given:]
    thirds, leaving, (mass, matrix, sems, more_sems), state = refs[0], refs[1:6], refs[6:10], refs[10:]
    row_two, row_one, col_one, col_two, col_three = state
    arrived = Arrivals(s, table, units, matrix, sems, [(mass_in, mass)])
    ones = jnp.ones((8, 2 * s.cols), jnp.bfloat16)
    zero = jnp.zeros((s.hists, 2 * s.cols), jnp.float32)

    def sums(d):
        arrived(d)
        return nt(ones, matrix[d])

    def times(panel):
        return lambda d: nt(panel, matrix[d])

    def first(d, row, total):
        row_one[d] = row
        left = mass[table[d], :, : s.rows] * (1 / row[0:1])
        return total + nn(left.astype(jnp.bfloat16), matrix[d])

    total = chain(s.count, sums, first, zero)
    col_one[...] = total
    target = gather_targets(s, mass, s.rows)
    panel = (target / total).astype(jnp.bfloat16)

    def second(d, row, total):
        row_two[d] = row
        left = mass[table[d], :, : s.rows] / row
        return total + nn(left.astype(jnp.bfloat16), matrix[d])

    total = chain(s.count, times(panel), second, zero)
    col_two[...] = total
    started = load(state[:4], leaving[:4], more_sems)
    last_panel = (target / total).astype(jnp.bfloat16)

    def third(d, row, total):
        thirds[table[d], :, : s.rows] = row
        left = mass[table[d], :, : s.rows] / row
        return total + nn(left.astype(jnp.bfloat16), matrix[d])

    total = chain(s.count, times(last_panel), third, zero)
    col_three[...] = total
    last = pltpu.make_async_copy(col_three, leaving[4], more_sems.at[4])
    last.start()
    scatter_targets(s, thirds, total)
    for copy in [*started, last]:
        copy.wait()


def backward_kernel(s, table, mass_in, cot_in, thirds_in, *refs):
    given = 2 + (s.count - 1) * s.halves
    state_in, units, refs = refs[:5], refs[5 : 5 + given], refs[5 + given :]
    out, (mass, matrix, sems, more_sems), state, (cot, thirds, cot_points) = (
        refs[0],
        refs[1:5],
        refs[5:10],
        refs[10:],
    )
    row_two, row_one, col_one, col_two, col_three = state
    points = cot_in.at[:, :, pl.ds(s.rows, 2 * s.share)]
    early = load([state_in[4], points], [col_three, cot_points], more_sems)
    paired = [(mass_in, mass), (thirds_in, thirds), (cot_in, cot)]
    arrived = Arrivals(s, table, units, matrix, sems, paired)
    late = [
        pltpu.make_async_copy(state_in[k], state[k], more_sems.at[2 + k]) for k in range(4)
    ]
    for copy in early:
        copy.wait()
    target_cot = gather_targets(s, cot_points, 0)
    panel = (-target_cot / col_three[...]).astype(jnp.bfloat16)
    zero = jnp.zeros((s.hists, 2 * s.cols), jnp.float32)

    def first_product(d):
        arrived(d)
        if s.count <= 8 and d == s.count - AHEAD:
            for copy in late:
                copy.start()
        return nt(panel, matrix[d])

    def third(d, grad, total):
        k = table[d]
        over = 1 / thirds[k, :, : s.rows]
        term = grad * over
        out[k, :, : s.rows] = term
        rowgrad = -over * (cot[k, :, : s.rows] + term * mass[k, :, : s.rows])
        return total + nn(rowgrad.astype(jnp.bfloat16), matrix[d])

    total = chain(s.count, first_product, third, zero)
    for copy in late:
        if s.count > 8:
            copy.start()
        copy.wait()
    target = gather_targets(s, mass, s.rows)
    term_two = total / col_two[...]
    panel_two = (-term_two * (target / col_two[...])).astype(jnp.bfloat16)

    def second(d, grad, total):
        k = table[d]
        over = 1 / row_two[d]
        term = grad * over
        out[k, :, : s.rows] += term
        rowgrad = -term * (mass[k, :, : s.rows] * over)
        return total + nn(rowgrad.astype(jnp.bfloat16), matrix[d])

    total = chain(s.count, lambda d: nt(panel_two, matrix[d]), second, zero)
    term_one = total / col_one[...]
    panel_one = (-term_one * (target / col_one[...])).astype(jnp.bfloat16)

    def first(d, grad, carry):
        out[table[d], :, : s.rows] += grad * (1 / row_one[d, 0:1])
        return carry

    chain(s.count, lambda d: nt(panel_one, matrix[d]), first, 0)
    scatter_targets(s, out, term_two + term_one)


def call(kernel, s, products, vmem_outs, hbm_outs, table, arrays, scratch):
    return pl.pallas_call(
        functools.partial(kernel, s),
        out_shape=[*vmem_outs, *hbm_outs],
        in_specs=[pl.BlockSpec(memory_space=pltpu.SMEM)]
        + [pl.BlockSpec(memory_space=pl.ANY)] * len(arrays),
        out_specs=[pl.BlockSpec(memory_space=pltpu.VMEM)] * len(vmem_outs)
        + [pl.BlockSpec(memory_space=pl.ANY)] * len(hbm_outs),
        scratch_shapes=[
            pltpu.VMEM((s.count, s.hists, s.lanes), jnp.float32),
            pltpu.VMEM((s.count, s.rows, 2 * s.cols), jnp.bfloat16),
            pltpu.SemaphoreType.DMA((s.count,)),
            pltpu.SemaphoreType.DMA((8,)),
            *[pltpu.VMEM(state.shape, state.dtype) for state in scratch],
        ],
        cost_estimate=pl.CostEstimate(
            flops=products * 2 * s.count * s.rows * 2 * s.cols * 256,
            bytes_accessed=s.count * s.rows * 2 * s.cols * 4,
            transcendentals=0,
        ),
        compiler_params=pltpu.CompilerParams(vmem_limit_bytes=VMEM),
    )(table, *arrays)


def swap_cores(x):
    return lax.ppermute(x, "tgt", [(0, 1), (1, 0)])


def local(
    source_mass,
    target_mass,
    kernel_tiles,
    tile_cols,
    tile_count,
    source_cotangent,
    target_cotangent,
):
    count = lax.axis_size("src")
    rows, cols_here = source_mass.shape
    share = target_mass.shape[1]
    s = Shape(count, rows, CB_DEV * kernel_tiles.shape[2], cols_here // count, share)
    ring = np.array(ring_order(count), np.int32)
    place = np.argsort(ring).astype(np.int32)
    me = lax.axis_index("src")
    core = lax.axis_index("tgt")
    at = jnp.asarray(place)[me]
    last = count // 2
    away = 2 * core - 1
    steps = [0] + [sign * k for k in range(1, last) for sign in (1, -1)] + [last]
    slots = (at + away * jnp.asarray(steps, jnp.int32)) % count
    table = jnp.concatenate([jnp.asarray(ring)[slots], core[None]]).astype(jnp.int32)

    def onward(x):
        pairs = []
        for p in range(count):
            pairs.append((int(ring[p]) * 2, int(ring[(p + 1) % count]) * 2))
            pairs.append((int(ring[p]) * 2 + 1, int(ring[(p - 1) % count]) * 2 + 1))
        return lax.ppermute(x, ("src", "tgt"), pairs)

    def exchange(x):
        return lax.all_to_all(x, "src", 0, 0, tiled=True)

    def in_order(mine, other, axis):
        return jnp.concatenate(
            [jnp.where(core == 0, mine, other), jnp.where(core == 0, other, mine)], axis=axis
        )

    def by_histogram(source, target):
        target = target.astype(HALF).reshape(share, 2, cols_here)
        mine = lax.dynamic_index_in_dim(target, core, 1, keepdims=False)
        other = lax.dynamic_index_in_dim(target, 1 - core, 1, keepdims=False)
        both = in_order(mine, swap_cores(other), 0).T
        return jnp.concatenate(
            [
                source.astype(HALF).T.reshape(count, s.hists, rows),
                both.reshape(count, s.hists, 2 * share),
            ],
            axis=2,
        )

    mine = dense_blocks(kernel_tiles, tile_cols, tile_count)
    theirs = swap_cores(mine)
    half = rows // s.halves
    cut = lambda x: [x[k * half : (k + 1) * half] for k in range(s.halves)]
    own_set = (jnp.arange(2, dtype=jnp.int32) == core)[:, None, None]
    pick = lambda x: [jnp.where(core == 0, *pair) for pair in zip(cut(x), reversed(cut(x)))]
    heads = [jnp.where(own_set, a[None], b[None]) for a, b in zip(pick(mine), pick(theirs))]
    heads, mass_here, points_here, cot_here, cot_points = lax.optimization_barrier(
        (heads, source_mass, target_mass[0], source_cotangent, target_cotangent[0])
    )
    units = list(heads)
    mass_message = by_histogram(mass_here, points_here)
    cot_message = by_histogram(cot_here * COT_SCALE, cot_points * COT_SCALE)
    came, swapped = {}, {}
    for step in range(1, last):
        for k in range(s.halves):
            if step > 2:
                heads[k], swapped[step - 2, k] = lax.optimization_barrier(
                    (heads[k], swapped[step - 2, k])
                )
            came[step, k] = heads[k] = onward(heads[k])
            if step == min(2, last - 1) and k == s.halves - 1:
                heads[k], mass_message, table = lax.optimization_barrier(
                    (heads[k], mass_message, table)
                )
                came[step, k] = heads[k]
            swapped[step, k] = swap_cores(heads[k])
    if s.halves == 1:
        piece = lax.dynamic_slice_in_dim(heads[0], core * (rows // 2), rows // 2, 1)
    else:
        piece = heads[0]
    due = [swapped[last - 2, k] for k in range(s.halves)]
    piece, due, cot_message = lax.optimization_barrier((piece, due, cot_message))
    swapped.update({(last - 2, k): due[k] for k in range(s.halves)})
    piece = onward(piece)
    for step in range(1, last):
        for part in (came, swapped):
            units += [part[step, k] for k in range(s.halves)]
    mass = exchange(mass_message).astype(jnp.float32)
    piece, mass = lax.optimization_barrier((piece, mass))
    units += [piece, swap_cores(piece)]
    cot = exchange(cot_message).astype(jnp.float32)

    wide = jax.ShapeDtypeStruct((count, s.hists, s.lanes), jnp.float32)
    panel = jax.ShapeDtypeStruct((count, s.hists, rows), jnp.float32)
    sums = jax.ShapeDtypeStruct((count, 8, rows), jnp.float32)
    column = jax.ShapeDtypeStruct((s.hists, 2 * s.cols), jnp.float32)
    points = jax.ShapeDtypeStruct((count, s.hists, 2 * share), jnp.float32)
    states = [panel, sums, column, column, column]
    thirds, *state = call(
        forward_kernel, s, 7, [wide], states, table, [mass, *units], states
    )
    (grads,) = call(
        backward_kernel,
        s,
        5,
        [wide],
        [],
        table,
        [mass, cot, thirds, *state, *units],
        [*states, panel, wide, points],
    )

    def by_point(pieces):
        turned = pieces.reshape(cols_here, s.lanes).astype(jnp.float32).T
        target = turned[rows:].reshape(2, share, cols_here)
        own = lax.dynamic_index_in_dim(target, core, 0, keepdims=False)
        other = lax.dynamic_index_in_dim(target, 1 - core, 0, keepdims=False)
        other = swap_cores(other.astype(HALF)).astype(jnp.float32)
        return turned[:rows], in_order(own, other, 1)

    row_three, col_three = by_point(exchange(thirds.astype(HALF)))
    source_potential = jnp.log(source_mass / row_three)
    target_potential = jnp.log(target_mass[0] / col_three)
    source_known = source_cotangent / source_mass
    target_known = target_cotangent[0] / target_mass[0]
    back, source_potential, target_potential, source_known, target_known = lax.optimization_barrier(
        (
            exchange(grads.astype(HALF)),
            source_potential,
            target_potential,
            source_known,
            target_known,
        )
    )
    source_term, target_term = by_point(back)
    return (
        source_potential,
        target_potential[None],
        source_known + source_term * (1 / COT_SCALE),
        (target_known + target_term * (1 / COT_SCALE))[None],
    )


def solution(mesh):
    return jax.shard_map(
        local,
        mesh=mesh,
        in_specs=(
            P(("grp", "src"), "tgt"),
            P("tgt", ("grp", "src"), None),
            P(("grp", "src"), "tgt", None, None),
            P(("grp", "src"), "tgt"),
            P(("grp", "src"), "tgt"),
            P(("grp", "src"), "tgt"),
            P("tgt", ("grp", "src"), None),
        ),
        out_specs=(
            P(("grp", "src"), "tgt"),
            P("tgt", ("grp", "src"), None),
            P(("grp", "src"), "tgt"),
            P("tgt", ("grp", "src"), None),
        ),
        check_vma=False,
    )
```
